128 devices in a mesh: tg: 8 (over x, y_hi), pool: 16 (over y_lo, z, core).
Axes of the slice: x: 4, y: 4 (y_hi: 2, y_lo: 2; y = y_hi * 2 + y_lo), z: 4, core: 2. Of those that a mesh axis runs over, the one named last changes fastest.
Arguments:
- wave_coef: float32 [2, 64, 512, 128], P(None, 'pool', 'tg'), may hold values from -6 to 6
- potential: float32 [128, 128, 128], P('tg'), may hold values from -1 to 3
- stick_pos: int32 [512], replicated, may hold values from 0 to 16383, as said below
- stick_count: int32 [8], replicated, may hold values from 32 to 64, as said below
- ritz_block: float32 [2, 64, 4096], P(None, 'pool'), may hold values from -0.75 to 0.75
- slab_base: bfloat16 [2, 65536, 4096], P(None, ('tg', 'pool')), may hold values from -6 to 6
Outputs:
- applied: float32 [2, 64, 512, 128], P(None, 'pool', 'tg')
- rotated: bfloat16 [2, 65536, 4096], P(None, ('tg', 'pool'))
The draws below stay inside these ranges and needn't reach their ends.
Inputs may be any that keep to these rules, and one draw needn't show every extreme that they name: `stick_pos`: distinct columns; both the first and the last column of the grid appear. `stick_count`: slots at or beyond this count on an index of tg are not in use; some index uses all 64 and some index half of them.
All inputs are finite; a program needn't handle non-finite values.
Results may differ from the reference program's by a relative error of at most 0.001.
Values sent between devices are 32-bit elements; how exact they have to be, the bound alone decides.
A program may use at most 128 MiB of HBM per device.

```python
import jax
import jax.numpy as jnp
from jax import lax

NX = 128
NY = 128
NZ = 128
NB = 4096
SDEV = 64
WIN = 64
NSTICK = 512
NCOEF = 65536
N_TG = 8


def draw_stick_pos(key, part):
    key = jax.random.fold_in(key, 11)
    key_one, key_two = jax.random.split(key)
    columns = NX * NY
    middle = 1 + jax.random.permutation(key_one, columns - 2)[:NSTICK - 2]
    chosen = jnp.concatenate([jnp.array([0, columns - 1], jnp.int32), middle.astype(jnp.int32)])
    shuffle = jax.random.permutation(key_two, NSTICK)
    return chosen[shuffle].astype(jnp.int32)


def draw_stick_count(key, part):
    key = jax.random.fold_in(key, 23)
    key_one, key_two = jax.random.split(key)
    counts = jax.random.randint(key_one, (N_TG,), SDEV // 2, SDEV + 1)
    chosen_ids = jax.random.permutation(key_two, N_TG)
    counts = counts.at[chosen_ids[0]].set(SDEV).at[chosen_ids[1]].set(SDEV // 2)
    return counts.astype(jnp.int32)


def block_scale(rng, dims, shards, low, top_value):
    level = 1.0
    for dim, parts in shards:
        heights = jax.random.uniform(jax.random.fold_in(jax.random.fold_in(rng, 6), dim), (parts,), jnp.float32, low / len(shards), top_value / len(shards))
        level = level * jnp.repeat(jnp.exp(heights), dims[dim] // parts).reshape((-1,) + (1,) * (len(dims) - 1 - dim))
    return level


def bell_draw(own_key, dims, scale, most, pieces=(), kind=jnp.bfloat16):
    entries = scale * jax.random.normal(own_key, dims, jnp.float32)
    if pieces:
        entries = entries * block_scale(own_key, dims, pieces, -0.22, 0.18)
    return jnp.clip(entries, -most, most).astype(kind)


def setup_inputs(seed: int = 0) -> dict:
    splits = jax.random.split(jax.random.key(seed), 7)
    return {
        "wave_coef": bell_draw(splits[0], (2, WIN, NSTICK, NZ), 1.0, 6.0, ((1, 16), (2, 8)), jnp.float32),
        "potential": jnp.clip(-1.0 + 4.0 * jax.random.uniform(splits[1], (NZ, NX, NY), jnp.float32) ** block_scale(splits[1], (NZ, NX, NY), ((0, 8),), -0.2, 0.2), -1.0, 3.0),
        "stick_pos": draw_stick_pos(jax.random.fold_in(splits[6], 71), 0),
        "stick_count": draw_stick_count(jax.random.fold_in(splits[6], 71), 0),
        "ritz_block": bell_draw(splits[4], (2, WIN, NB), WIN ** -0.5, 0.75, ((1, 16),), jnp.float32),
        "slab_base": bell_draw(splits[5], (2, NCOEF, NB), 1.0, 6.0, ((1, 128),)),
    }


def reference(wave_coef, potential, stick_pos, stick_count, ritz_block, slab_base):
    slot_ids = jnp.arange(NSTICK, dtype=jnp.int32)
    usable = ((slot_ids % SDEV) < stick_count[slot_ids // SDEV]).astype(wave_coef.dtype)
    masked = wave_coef * usable[None, None, :, None]
    potential_xyz = jnp.transpose(potential, (1, 2, 0))

    def apply_one(pair):
        spectrum = pair[0] + 1j * pair[1]
        lattice = jnp.zeros((NX * NY, NZ), spectrum.dtype).at[stick_pos].set(spectrum)
        real_field = jnp.fft.ifftn(lattice.reshape(NX, NY, NZ))
        result = jnp.fft.fftn(real_field * potential_xyz)
        columns = result.reshape(NX * NY, NZ)[stick_pos]
        stacked = jnp.stack([jnp.real(columns), jnp.imag(columns)]).astype(wave_coef.dtype)
        return stacked * usable[None, :, None]

    applied = jnp.swapaxes(lax.map(apply_one, jnp.swapaxes(masked, 0, 1)), 0, 1)

    flat_coef = masked.reshape(2, WIN, NCOEF)
    flat_image = applied.reshape(2, WIN, NCOEF)

    def rotate_block(index):
        start = (index * NZ).astype(jnp.int32)
        part_coef = lax.dynamic_slice_in_dim(flat_coef, start, NZ, 2)
        part_image = lax.dynamic_slice_in_dim(flat_image, start, NZ, 2)
        base_part = lax.dynamic_slice_in_dim(slab_base, start, NZ, 1).astype(jnp.float32)
        first_term = jnp.einsum("cig,ij->cgj", part_coef, ritz_block[0], precision=lax.Precision.HIGHEST)
        second_term = jnp.einsum("cig,ij->cgj", part_image, ritz_block[1], precision=lax.Precision.HIGHEST)
        return (base_part + first_term + second_term).astype(jnp.bfloat16)

    blocks = lax.map(rotate_block, jnp.arange(NSTICK, dtype=jnp.int32))
    rotated = jnp.transpose(blocks, (1, 0, 2, 3)).reshape(2, NCOEF, NB)
    return applied, rotated
```

```python
import functools
import math

import jax
import jax.numpy as jnp
import ml_dtypes
import numpy as np
from jax import lax
from jax.experimental import pallas as pl
from jax.experimental.pallas import tpu as pltpu
from jax.sharding import PartitionSpec as P

NX = 128
NY = 128
BF16 = jnp.bfloat16
F32 = jnp.float32


def np_split(table):
    high = table.astype(np.float32).astype(ml_dtypes.bfloat16)
    low = (table - high.astype(np.float64)).astype(ml_dtypes.bfloat16)
    return high, low


def np_cs(length):
    idx = np.arange(length)
    ang = (idx[:, None] * idx[None, :] % length) * (2.0 * math.pi / length)
    return np.cos(ang), np.sin(ang)


def row_table(length, sign, scale=1.0):
    cos_t, sin_t = np_cs(length)
    return scale * np.block([[cos_t, sign * sin_t], [-sign * sin_t, cos_t]])


def split(values):
    high = values.astype(BF16)
    low = (values - high.astype(F32)).astype(BF16)
    return high, low


def as_rhs_rows(table):
    high, low = np_split(table)
    return np.concatenate([high, high, low], axis=0)


def as_lhs(table):
    high, low = np_split(table)
    return np.concatenate([high, high, low], axis=1)


def lanes3(values):
    high, low = split(values)
    return jnp.concatenate([high, low, high], axis=1)


def rows3(values):
    high, low = split(values)
    return jnp.concatenate([high, low, high], axis=0)


def dot(a, b):
    return lax.dot_general(a, b, (((1,), (0,)), ((), ())), preferred_element_type=F32)


def dot_nt(a, b):
    return lax.dot_general(a, b, (((1,), (1,)), ((), ())), preferred_element_type=F32)


def plane_kernel(pos_ref, sticks_ref, parity_ref, pot_ref, ty_ref, ax_ref, bx_ref, by_ref,
                 out_ref, grid_ref, re_ref, im_ref, gre_ref, gim_ref):
    slots = sticks_ref.shape[0]
    half = 64

    @pl.loop(0, 128)
    def _(x):
        grid_ref[pl.ds(pl.multiple_of(x * 128, 128), 128), :] = jnp.zeros((128, 128), F32)

    @pl.loop(0, slots // 8)
    def _(block):
        base = pl.multiple_of(block * 8, 8)
        rows = sticks_ref[pl.ds(base, 8), :]
        for k in range(8):
            grid_ref[pl.ds(pos_ref[base + k], 1), :] = rows[k:k + 1, :]

    @pl.loop(0, 64)
    def _(pair):
        parts = []
        for k in range(2):
            x = pair * 2 + k
            flipped = grid_ref[pl.ds(pl.multiple_of(x * 128, 128), 128), :].T
            parts.append(jnp.concatenate([flipped[:half], flipped[half:]], axis=1))
        res = dot(lanes3(jnp.concatenate(parts, axis=0)), ty_ref[...])
        at = pl.ds(pl.multiple_of(pair * 128, 128), 128)
        re_ref[at, :] = res[:, :128]
        im_ref[at, :] = res[:, 128:]

    @pl.loop(0, 16)
    def _(z):
        pot = pot_ref[z]
        for pair in range(2):
            at = [pl.ds((pair * 2 + k) * 16 + z, 128, half) for k in range(2)]
            data = jnp.concatenate(
                [jnp.concatenate([re_ref[a, :], im_ref[a, :]], axis=0) for a in at], axis=1)
            field = dot(ax_ref[...], rows3(data))
            wide = jnp.concatenate([pot, pot], axis=1)
            wide = jnp.concatenate([wide, wide], axis=0)
            back = dot(bx_ref[...], rows3(field * wide))
            for k in range(2):
                re_ref[at[k], :] = back[:128, k * 128:(k + 1) * 128]
                im_ref[at[k], :] = back[128:, k * 128:(k + 1) * 128]

    @pl.loop(0, 32)
    def _(group):
        at = pl.ds(pl.multiple_of(group * 256, 256), 256)
        data = jnp.concatenate([re_ref[at, :], im_ref[at, :]], axis=1)
        res = dot_nt(by_ref[...], lanes3(data))
        for k in range(2):
            to = pl.ds(pl.multiple_of((group * 2 + k) * 256, 256), 256)
            grid_ref[to, :] = res[:, k * 128:(k + 1) * 128]

    @pl.loop(0, slots // 8)
    def _(block):
        base = pl.multiple_of(block * 8, 8)
        for k in range(8):
            pos = pos_ref[base + k]
            row = (pos >> 8) * 256 + (pos & 127)
            gre_ref[pl.ds(base + k, 1), :] = grid_ref[pl.ds(row, 1), :]
            gim_ref[pl.ds(base + k, 1), :] = grid_ref[pl.ds(row + 128, 1), :]

    @pl.loop(0, slots // 64)
    def _(block):
        at = pl.ds(pl.multiple_of(block * 64, 64), 64)
        odd = jnp.broadcast_to(parity_ref[at, :], (64, half)) > 0
        gre = gre_ref[at, :]
        gim = gim_ref[at, :]
        out_ref[at, :] = jnp.concatenate(
            [jnp.where(odd, gre[:, half:], gre[:, :half]),
             jnp.where(odd, gim[:, half:], gim[:, :half])], axis=1)


def plane_step(sticks, stick_pos, pot):
    slots = sticks.shape[0]
    volume = 128.0 ** 3
    ty = as_rhs_rows(row_table(128, 1.0))
    ax = as_lhs(row_table(128, 1.0, 1.0 / volume).T)
    bx = as_lhs(row_table(128, -1.0).T)
    by = as_lhs(row_table(128, -1.0).T)
    parity = ((stick_pos >> 7) & 1).reshape(slots, 1)
    vmem = pl.BlockSpec(memory_space=pltpu.VMEM)
    return pl.pallas_call(
        plane_kernel,
        out_shape=jax.ShapeDtypeStruct((slots, 128), F32),
        in_specs=[pl.BlockSpec(memory_space=pltpu.SMEM)] + [vmem] * 7,
        out_specs=vmem,
        scratch_shapes=[
            pltpu.VMEM((16384, 128), F32),
            pltpu.VMEM((8192, 128), F32),
            pltpu.VMEM((8192, 128), F32),
            pltpu.VMEM((slots, 128), F32),
            pltpu.VMEM((slots, 128), F32),
        ],
        compiler_params=pltpu.CompilerParams(vmem_limit_bytes=44 * 2**20),
        name="planes",
    )(stick_pos, sticks, parity, pot, ty, ax, bx, by)


def rotate_kernel(coef_ref, image_ref, ritz_ref, base_ref, out_ref, split_ref):
    @pl.when((pl.program_id(0) == 0) & (pl.program_id(1) == 0))
    def _():
        for term in range(2):
            for j in range(0, 4096, 512):
                high, low = split(ritz_ref[term, :, j:j + 512])
                for k, piece in enumerate((high, high, low, low)):
                    split_ref[k * 128 + term * 64:k * 128 + term * 64 + 64, j:j + 512] = piece

    rows = jnp.concatenate([coef_ref[0], image_ref[0]], axis=0).T
    high, low = split(rows)
    left = jnp.concatenate([high, low, high, low], axis=1)

    @pl.loop(0, 4096 // 512)
    def _(j):
        at = pl.ds(pl.multiple_of(j * 512, 512), 512)
        out_ref[0, :, at] = (base_ref[0, :, at].astype(F32)
                             + dot(left, split_ref[:, at])).astype(BF16)


def rotate(coef, image, ritz, base):
    window, size = coef.shape[1], coef.shape[2]
    rows = 128
    data = pl.BlockSpec((1, window, rows), lambda c, g: (c, 0, g))
    slab = pl.BlockSpec((1, rows, 4096), lambda c, g: (c, g, 0))
    return pl.pallas_call(
        rotate_kernel,
        grid=(2, size // rows),
        out_shape=jax.ShapeDtypeStruct(base.shape, BF16),
        in_specs=[data, data, pl.BlockSpec((2, window, 4096), lambda c, g: (0, 0, 0)), slab],
        out_specs=slab,
        scratch_shapes=[pltpu.VMEM((512, 4096), BF16)],
        compiler_params=pltpu.CompilerParams(vmem_limit_bytes=40 * 2**20),
        name="rotate",
    )(coef, image, ritz, base)


def local(wave_coef, potential, stick_pos, stick_count, ritz_block, slab_base):
    _, bands, slots, height = wave_coef.shape
    own_count = stick_count[lax.axis_index("tg")]
    usable = (jnp.arange(slots, dtype=jnp.int32) < own_count).astype(F32)
    masked = wave_coef * usable[None, None, :, None]
    coef = lax.all_to_all(masked, "pool", split_axis=2, concat_axis=1, tiled=True)
    ritz_full = lax.all_gather(ritz_block, "pool", axis=1, tiled=True)

    cos_z, sin_z = (t.astype(np.float32) for t in np_cs(height))
    mul = functools.partial(jnp.einsum, precision=lax.Precision.HIGHEST)
    table_f = np.stack([np.stack([cos_z, sin_z]), np.stack([-sin_z, cos_z])])
    table_b = np.stack([np.stack([cos_z, -sin_z]), np.stack([sin_z, cos_z])])
    sticks = mul("pbsz,pqzn->sqbn", masked, table_f)
    planes = lax.all_to_all(sticks, "tg", split_axis=3, concat_axis=0, tiled=True)
    columns = plane_step(planes.reshape(planes.shape[0], -1), stick_pos, potential)
    returned = lax.all_to_all(columns.reshape(planes.shape), "tg", split_axis=0, concat_axis=3, tiled=True)
    applied = mul("spbz,pqzn->qbsn", returned, table_b) * usable[None, None, :, None]
    image = lax.all_to_all(applied, "pool", split_axis=2, concat_axis=1, tiled=True)
    window = coef.shape[1]
    rotated = rotate(coef.reshape(2, window, -1), image.reshape(2, window, -1), ritz_full, slab_base)
    return applied, rotated


def solution(mesh):
    in_specs = (
        P(None, "pool", "tg", None),
        P("tg", None, None),
        P(),
        P(),
        P(None, "pool", None),
        P(None, ("tg", "pool"), None),
    )
    out_specs = (P(None, "pool", "tg", None), P(None, ("tg", "pool"), None))
    return jax.shard_map(local, mesh=mesh, in_specs=in_specs, out_specs=out_specs, check_vma=False)
```

```python
import functools
import math

import jax
import jax.numpy as jnp
import ml_dtypes
import numpy as np
from jax import lax
from jax.experimental import pallas as pl
from jax.experimental.pallas import tpu as pltpu
from jax.sharding import PartitionSpec as P

NX = 128
NY = 128
BF16 = jnp.bfloat16
F32 = jnp.float32
MESH = pl.DeviceIdType.MESH


def np_split(table):
    high = table.astype(np.float32).astype(ml_dtypes.bfloat16)
    low = (table - high.astype(np.float64)).astype(ml_dtypes.bfloat16)
    return high, low


def np_cs(length):
    idx = np.arange(length)
    ang = (idx[:, None] * idx[None, :] % length) * (2.0 * math.pi / length)
    return np.cos(ang), np.sin(ang)


def row_table(length, sign, scale=1.0):
    cos_t, sin_t = np_cs(length)
    return scale * np.block([[cos_t, sign * sin_t], [-sign * sin_t, cos_t]])


def split(values):
    high = values.astype(BF16)
    low = (values - high.astype(F32)).astype(BF16)
    return high, low


def as_rhs_rows(table):
    high, low = np_split(table)
    return np.concatenate([high, high, low], axis=0)


def as_lhs(table):
    high, low = np_split(table)
    return np.concatenate([high, high, low], axis=1)


def lanes3(values):
    high, low = split(values)
    return jnp.concatenate([high, low, high], axis=1)


def rows3(values):
    high, low = split(values)
    return jnp.concatenate([high, low, high], axis=0)


def dot(a, b):
    return lax.dot_general(a, b, (((1,), (0,)), ((), ())), preferred_element_type=F32)


def dot_nt(a, b):
    return lax.dot_general(a, b, (((1,), (1,)), ((), ())), preferred_element_type=F32)


def plane_kernel(pos_ref, sticks_ref, parity_ref, pot_ref, ty_ref, ax_ref, bx_ref, by_ref,
                 out_ref, grid_ref, re_ref, im_ref, gre_ref, gim_ref):
    slots = sticks_ref.shape[0]
    half = 64

    @pl.loop(0, 128)
    def _(x):
        grid_ref[pl.ds(pl.multiple_of(x * 128, 128), 128), :] = jnp.zeros((128, 128), F32)

    @pl.loop(0, slots // 8)
    def _(block):
        base = pl.multiple_of(block * 8, 8)
        rows = sticks_ref[pl.ds(base, 8), :]
        for k in range(8):
            grid_ref[pl.ds(pos_ref[base + k], 1), :] = rows[k:k + 1, :]

    @pl.loop(0, 64)
    def _(pair):
        parts = []
        for k in range(2):
            x = pair * 2 + k
            flipped = grid_ref[pl.ds(pl.multiple_of(x * 128, 128), 128), :].T
            parts.append(jnp.concatenate([flipped[:half], flipped[half:]], axis=1))
        res = dot(lanes3(jnp.concatenate(parts, axis=0)), ty_ref[...])
        at = pl.ds(pl.multiple_of(pair * 128, 128), 128)
        re_ref[at, :] = res[:, :128]
        im_ref[at, :] = res[:, 128:]

    @pl.loop(0, 16)
    def _(z):
        pot = pot_ref[z]
        for pair in range(2):
            at = [pl.ds((pair * 2 + k) * 16 + z, 128, half) for k in range(2)]
            data = jnp.concatenate(
                [jnp.concatenate([re_ref[a, :], im_ref[a, :]], axis=0) for a in at], axis=1)
            field = dot(ax_ref[...], rows3(data))
            wide = jnp.concatenate([pot, pot], axis=1)
            wide = jnp.concatenate([wide, wide], axis=0)
            back = dot(bx_ref[...], rows3(field * wide))
            for k in range(2):
                re_ref[at[k], :] = back[:128, k * 128:(k + 1) * 128]
                im_ref[at[k], :] = back[128:, k * 128:(k + 1) * 128]

    @pl.loop(0, 32)
    def _(group):
        at = pl.ds(pl.multiple_of(group * 256, 256), 256)
        data = jnp.concatenate([re_ref[at, :], im_ref[at, :]], axis=1)
        res = dot_nt(by_ref[...], lanes3(data))
        for k in range(2):
            to = pl.ds(pl.multiple_of((group * 2 + k) * 256, 256), 256)
            grid_ref[to, :] = res[:, k * 128:(k + 1) * 128]

    @pl.loop(0, slots // 8)
    def _(block):
        base = pl.multiple_of(block * 8, 8)
        for k in range(8):
            pos = pos_ref[base + k]
            row = (pos >> 8) * 256 + (pos & 127)
            gre_ref[pl.ds(base + k, 1), :] = grid_ref[pl.ds(row, 1), :]
            gim_ref[pl.ds(base + k, 1), :] = grid_ref[pl.ds(row + 128, 1), :]

    @pl.loop(0, slots // 64)
    def _(block):
        at = pl.ds(pl.multiple_of(block * 64, 64), 64)
        odd = jnp.broadcast_to(parity_ref[at, :], (64, half)) > 0
        gre = gre_ref[at, :]
        gim = gim_ref[at, :]
        out_ref[at, :] = jnp.concatenate(
            [jnp.where(odd, gre[:, half:], gre[:, :half]),
             jnp.where(odd, gim[:, half:], gim[:, :half])], axis=1)


def plane_step(sticks, stick_pos, pot):
    slots = sticks.shape[0]
    volume = 128.0 ** 3
    ty = as_rhs_rows(row_table(128, 1.0))
    ax = as_lhs(row_table(128, 1.0, 1.0 / volume).T)
    bx = as_lhs(row_table(128, -1.0).T)
    by = as_lhs(row_table(128, -1.0).T)
    parity = ((stick_pos >> 7) & 1).reshape(slots, 1)
    vmem = pl.BlockSpec(memory_space=pltpu.VMEM)
    return pl.pallas_call(
        plane_kernel,
        out_shape=jax.ShapeDtypeStruct((slots, 128), F32),
        in_specs=[pl.BlockSpec(memory_space=pltpu.SMEM)] + [vmem] * 7,
        out_specs=vmem,
        scratch_shapes=[
            pltpu.VMEM((16384, 128), F32),
            pltpu.VMEM((8192, 128), F32),
            pltpu.VMEM((8192, 128), F32),
            pltpu.VMEM((slots, 128), F32),
            pltpu.VMEM((slots, 128), F32),
        ],
        compiler_params=pltpu.CompilerParams(vmem_limit_bytes=44 * 2**20),
        name="planes",
    )(stick_pos, sticks, parity, pot, ty, ax, bx, by)


def rotate_kernel(coef_ref, image_ref, ritz_ref, base_ref, applied_ref, out_ref, copy_ref, split_ref, rows_ref):
    part, block = pl.program_id(0), pl.program_id(1)

    @pl.when((part == 0) & (block == 0))
    def _():
        copy_ref[...] = applied_ref[...]
        for term in range(2):
            for j in range(0, 4096, 512):
                high, low = split(ritz_ref[term, :, j:j + 512])
                for k, piece in enumerate((high, high, low, low)):
                    split_ref[k * 128 + term * 64:k * 128 + term * 64 + 64, j:j + 512] = piece

    rows_ref[:128, :] = coef_ref[...].reshape(128, 128)
    rows_ref[128:, :] = image_ref[...].reshape(128, 128)
    rows = rows_ref[pl.ds(part, 128, 2), :].T
    high, low = split(rows)
    left = jnp.concatenate([high, low, high, low], axis=1)

    @pl.loop(0, 4096 // 512)
    def _(j):
        at = pl.ds(pl.multiple_of(j * 512, 512), 512)
        out_ref[0, :, at] = (base_ref[0, :, at].astype(F32)
                             + dot(left, split_ref[:, at])).astype(BF16)


def rotate(coef, image, ritz, base, applied):
    window, rows = ritz.shape[1], coef.shape[3]
    data = pl.BlockSpec((coef.shape[0], 1) + coef.shape[2:], lambda c, g: (0, g, 0, 0))
    slab = pl.BlockSpec((1, rows, 4096), lambda c, g: (c, g, 0))
    whole = pl.BlockSpec(applied.shape, lambda c, g: (0, 0))
    return pl.pallas_call(
        rotate_kernel,
        grid=(2, coef.shape[1]),
        out_shape=[jax.ShapeDtypeStruct(base.shape, BF16), jax.ShapeDtypeStruct(applied.shape, F32)],
        in_specs=[data, data, pl.BlockSpec((2, window, 4096), lambda c, g: (0, 0, 0)), slab, whole],
        out_specs=[slab, whole],
        scratch_shapes=[pltpu.VMEM((512, 4096), BF16), pltpu.VMEM((256, 128), F32)],
        compiler_params=pltpu.CompilerParams(vmem_limit_bytes=40 * 2**20),
        name="rotate",
    )(coef, image, ritz, base, applied)


def greet(n_tg, n_pool, tg, pool):
    barrier = pltpu.get_barrier_semaphore()
    for step in range(1, n_tg):
        pl.semaphore_signal(barrier, inc=1, device_id={"tg": lax.rem(tg + step, n_tg)}, device_id_type=MESH)
    for step in range(1, n_pool):
        pl.semaphore_signal(barrier, inc=1, device_id={"pool": lax.rem(pool + step, n_pool)}, device_id_type=MESH)
    pl.semaphore_wait(barrier, n_tg + n_pool - 2)


class Exchange:
    def __init__(self, axis, size, me, source, target, send_sem, recv_sem, own_sem):
        self.axis, self.size, self.me = axis, size, me
        self.source, self.target = source, target
        self.send_sem, self.recv_sem, self.own_sem = send_sem, recv_sem, own_sem

    def remote(self, step):
        peer = lax.rem(self.me + step, self.size)
        return pltpu.make_async_remote_copy(
            src_ref=self.source.at[peer], dst_ref=self.target.at[self.me],
            send_sem=self.send_sem.at[peer], recv_sem=self.recv_sem.at[self.me],
            device_id={self.axis: peer}, device_id_type=MESH)

    def own(self):
        return pltpu.make_async_copy(self.source.at[self.me], self.target.at[self.me], self.own_sem)

    def start(self):
        for step in range(1, self.size):
            self.remote(step).start()
        self.own().start()

    def wait_recv(self):
        self.own().wait()
        for step in range(1, self.size):
            peer = lax.rem(self.me + step, self.size)
            pltpu.make_async_remote_copy(
                src_ref=self.source.at[peer], dst_ref=self.target.at[peer],
                send_sem=self.send_sem.at[peer], recv_sem=self.recv_sem.at[peer],
                device_id={self.axis: peer}, device_id_type=MESH).wait_recv()

    def wait_send(self):
        for step in range(1, self.size):
            self.remote(step).wait_send()


def pack_rows(flat_ref, pack_ref, n_pool):
    for k in range(n_pool):
        for j in range(4):
            for part in range(2):
                rows = flat_ref[pl.ds(part * 256 + k * 4 + j, 4, 64), :]
                pack_ref[k, j, pl.ds(part, 4, 2), :] = rows


def spread_kernel(n_tg, n_pool, wave_ref, usable_ref, table_ref, planes_ref, coef_ref,
                  flat_ref, sticks_ref, pack_ref, send_t, recv_t, send_p, recv_p, own_sem):
    tg, pool = lax.axis_index("tg"), lax.axis_index("pool")
    greet(n_tg, n_pool, tg, pool)
    usable = jnp.broadcast_to(usable_ref[...], (64, 128))
    rows = []
    for band in range(4):
        pair = [wave_ref[part, band] * usable for part in range(2)]
        for part in range(2):
            flat_ref[(part * 4 + band) * 64:(part * 4 + band + 1) * 64, :] = pair[part]
        rows.append(jnp.concatenate(pair, axis=1))
    res = dot(lanes3(jnp.concatenate(rows, axis=0)), table_ref[...])
    for t in range(n_tg):
        sticks_ref[t] = jnp.concatenate(
            [res[band * 64:(band + 1) * 64, part * 128 + t * 16:part * 128 + t * 16 + 16]
             for part in range(2) for band in range(4)], axis=1)
    planes = Exchange("tg", n_tg, tg, sticks_ref, planes_ref, send_t, recv_t, own_sem.at[0])
    planes.start()
    pack_rows(flat_ref, pack_ref, n_pool)
    coef = Exchange("pool", n_pool, pool, pack_ref, coef_ref, send_p, recv_p, own_sem.at[1])
    coef.start()
    planes.wait_recv()
    coef.wait_recv()
    planes.wait_send()
    coef.wait_send()


def collect_kernel(n_tg, n_pool, cols_ref, usable_ref, table_ref, applied_ref, image_ref,
                   returned_ref, pack_ref, send_t, recv_t, send_p, recv_p, own_sem):
    tg, pool = lax.axis_index("tg"), lax.axis_index("pool")
    greet(n_tg, n_pool, tg, pool)
    back = Exchange("tg", n_tg, tg, cols_ref, returned_ref, send_t, recv_t, own_sem.at[0])
    back.start()
    usable = jnp.broadcast_to(usable_ref[...], (64, 256))
    back.wait_recv()
    rows = []
    for band in range(4):
        rows.append(jnp.concatenate(
            [returned_ref[t, :, part * 64 + band * 16:part * 64 + band * 16 + 16]
             for part in range(2) for t in range(n_tg)], axis=1))
    res = dot(lanes3(jnp.concatenate(rows, axis=0)), table_ref[...])
    for band in range(4):
        block = res[band * 64:(band + 1) * 64] * usable
        for part in range(2):
            at = (part * 4 + band) * 64
            applied_ref[at:at + 64, :] = block[:, part * 128:(part + 1) * 128]
    pack_rows(applied_ref, pack_ref, n_pool)
    image = Exchange("pool", n_pool, pool, pack_ref, image_ref, send_p, recv_p, own_sem.at[1])
    image.start()
    image.wait_recv()
    back.wait_send()
    image.wait_send()


def exchange_scratch(n_tg, n_pool):
    dma = pltpu.SemaphoreType.DMA
    return [dma((n_tg,)), dma((n_tg,)), dma((n_pool,)), dma((n_pool,)), dma((2,))]


def spread(wave, usable, n_tg, n_pool):
    vmem = pl.BlockSpec(memory_space=pltpu.VMEM)
    return pl.pallas_call(
        functools.partial(spread_kernel, n_tg, n_pool),
        out_shape=[jax.ShapeDtypeStruct((n_tg, 64, 128), F32), jax.ShapeDtypeStruct((n_pool, 4, 8, 128), F32)],
        in_specs=[vmem] * 3,
        out_specs=[vmem] * 2,
        scratch_shapes=[pltpu.VMEM((512, 128), F32), pltpu.VMEM((n_tg, 64, 128), F32),
                        pltpu.VMEM((n_pool, 4, 8, 128), F32)] + exchange_scratch(n_tg, n_pool),
        compiler_params=pltpu.CompilerParams(collective_id=0, has_side_effects=True,
                                             vmem_limit_bytes=24 * 2**20),
        name="spread",
    )(wave, usable, as_rhs_rows(row_table(128, 1.0)))


def collect(columns, usable, n_tg, n_pool):
    vmem = pl.BlockSpec(memory_space=pltpu.VMEM)
    return pl.pallas_call(
        functools.partial(collect_kernel, n_tg, n_pool),
        out_shape=[jax.ShapeDtypeStruct((512, 128), F32), jax.ShapeDtypeStruct((n_pool, 4, 8, 128), F32)],
        in_specs=[vmem] * 3,
        out_specs=[vmem] * 2,
        scratch_shapes=[pltpu.VMEM((n_tg, 64, 128), F32),
                        pltpu.VMEM((n_pool, 4, 8, 128), F32)] + exchange_scratch(n_tg, n_pool),
        compiler_params=pltpu.CompilerParams(collective_id=1, has_side_effects=True,
                                             vmem_limit_bytes=24 * 2**20),
        name="collect",
    )(columns, usable, as_rhs_rows(row_table(128, -1.0)))


def local(wave_coef, potential, stick_pos, stick_count, ritz_block, slab_base):
    n_tg, n_pool = lax.axis_size("tg"), lax.axis_size("pool")
    slots = wave_coef.shape[2]
    own_count = stick_count[lax.axis_index("tg")]
    usable = (jnp.arange(slots, dtype=jnp.int32) < own_count).astype(F32).reshape(slots, 1)
    ritz_full = lax.all_gather(ritz_block, "pool", axis=1, tiled=True)
    planes, coef = spread(wave_coef, usable, n_tg, n_pool)
    columns = plane_step(planes.reshape(n_tg * slots, 128), stick_pos, potential)
    applied, image = collect(columns.reshape(n_tg, slots, 128), usable, n_tg, n_pool)
    rotated, applied = rotate(coef, image, ritz_full, slab_base, applied)
    return applied.reshape(wave_coef.shape), rotated


def solution(mesh):
    in_specs = (
        P(None, "pool", "tg", None),
        P("tg", None, None),
        P(),
        P(),
        P(None, "pool", None),
        P(None, ("tg", "pool"), None),
    )
    out_specs = (P(None, "pool", "tg", None), P(None, ("tg", "pool"), None))
    return jax.shard_map(local, mesh=mesh, in_specs=in_specs, out_specs=out_specs, check_vma=False)
```

```python
import functools
import math

import jax
import jax.numpy as jnp
import ml_dtypes
import numpy as np
from jax import lax
from jax.experimental import pallas as pl
from jax.experimental.pallas import tpu as pltpu
from jax.sharding import PartitionSpec as P

NX = 128
NY = 128
BF16 = jnp.bfloat16
F32 = jnp.float32
MESH = pl.DeviceIdType.MESH


def np_split(table):
    high = table.astype(np.float32).astype(ml_dtypes.bfloat16)
    low = (table - high.astype(np.float64)).astype(ml_dtypes.bfloat16)
    return high, low


def np_cs(length):
    idx = np.arange(length)
    ang = (idx[:, None] * idx[None, :] % length) * (2.0 * math.pi / length)
    return np.cos(ang), np.sin(ang)


def row_table(length, sign, scale=1.0):
    cos_t, sin_t = np_cs(length)
    return scale * np.block([[cos_t, sign * sin_t], [-sign * sin_t, cos_t]])


def split(values):
    high = values.astype(BF16)
    low = (values - high.astype(F32)).astype(BF16)
    return high, low


def as_rhs_rows(table):
    high, low = np_split(table)
    return np.concatenate([high, high, low], axis=0)


def as_lhs(table):
    high, low = np_split(table)
    return np.concatenate([high, high, low], axis=1)


def lanes3(values):
    high, low = split(values)
    return jnp.concatenate([high, low, high], axis=1)


def rows3(values):
    high, low = split(values)
    return jnp.concatenate([high, low, high], axis=0)


def dot(a, b):
    return lax.dot_general(a, b, (((1,), (0,)), ((), ())), preferred_element_type=F32)


def dot_nt(a, b):
    return lax.dot_general(a, b, (((1,), (1,)), ((), ())), preferred_element_type=F32)


PITCH = 65
Y_STEP = 16
X_STEP = 2


def plane_kernel(pos_hbm, sticks_ref, pot_hbm, ty_hbm, ax_hbm, bx_hbm,
                 out_ref, pos_ref, pot_ref, ty_ref, ax_ref, bx_ref, grid_ref, re_ref, im_ref, sems):
    slots = sticks_ref.shape[0]
    half = 64
    pairs = [(pos_hbm, pos_ref), (ty_hbm, ty_ref), (ax_hbm, ax_ref), (bx_hbm, bx_ref), (pot_hbm, pot_ref)]
    copies = [pltpu.make_async_copy(src, dst, sems.at[k]) for k, (src, dst) in enumerate(pairs)]
    for copy in copies:
        copy.start()

    @pl.loop(0, 32)
    def _(x):
        grid_ref[pl.ds(pl.multiple_of(x * 512, 512), 512), :] = jnp.zeros((512, 128), F32)

    copies[0].wait()

    @pl.loop(0, slots // 8)
    def _(block):
        base = pl.multiple_of(block * 8, 8)
        rows = sticks_ref[pl.ds(base, 8), :]
        for k in range(8):
            grid_ref[pl.ds(pos_ref[base + k], 1), :] = rows[k:k + 1, :]

    copies[1].wait()

    @pl.loop(0, 128 // Y_STEP)
    def _(step):
        parts = []
        for k in range(Y_STEP):
            x = step * Y_STEP + k
            flipped = grid_ref[pl.ds(pl.multiple_of(x * 128, 128), 128), :].T
            parts.append(jnp.concatenate([flipped[:half], flipped[half:]], axis=1))
        res = dot(lanes3(jnp.concatenate(parts, axis=0)), ty_ref[...])
        for k in range(Y_STEP):
            to = pl.ds((step * Y_STEP + k) * PITCH, half)
            re_ref[to, :] = res[k * half:(k + 1) * half, :128]
            im_ref[to, :] = res[k * half:(k + 1) * half, 128:]

    for copy in copies[2:]:
        copy.wait()

    @pl.loop(0, 16, unroll=2)
    def _(z):
        pot = pot_ref[z]
        wide = jnp.concatenate([pot] * X_STEP, axis=1)
        wide = jnp.concatenate([wide, wide], axis=0)
        for group in range(4 // X_STEP):
            at = [pl.ds((group * X_STEP + k) * 16 + z, 128, PITCH) for k in range(X_STEP)]
            data = jnp.concatenate(
                [jnp.concatenate([re_ref[a, :], im_ref[a, :]], axis=0) for a in at], axis=1)
            field = dot(ax_ref[...], rows3(data))
            back = dot(bx_ref[...], rows3(field * wide))
            for k in range(X_STEP):
                re_ref[at[k], :] = back[:128, k * 128:(k + 1) * 128]
                im_ref[at[k], :] = back[128:, k * 128:(k + 1) * 128]

    @pl.loop(0, 128 // Y_STEP)
    def _(step):
        data = jnp.concatenate(
            [jnp.concatenate([ref[pl.ds((step * Y_STEP + k) * PITCH, half), :] for k in range(Y_STEP)], axis=0)
             for ref in (re_ref, im_ref)], axis=1)
        res = dot_nt(bx_ref[...], lanes3(data))
        for k in range(Y_STEP):
            to = pl.ds(pl.multiple_of((step * Y_STEP + k) * 128, 128), 128)
            grid_ref[to, :] = jnp.concatenate(
                [res[:128, k * half:(k + 1) * half], res[128:, k * half:(k + 1) * half]], axis=1)

    @pl.loop(0, slots // 8)
    def _(block):
        base = pl.multiple_of(block * 8, 8)
        out_ref[pl.ds(base, 8), :] = jnp.concatenate(
            [grid_ref[pl.ds(pos_ref[base + k], 1), :] for k in range(8)], axis=0)


def plane_step(sticks, stick_pos, pot):
    slots = sticks.shape[0]
    volume = 128.0 ** 3
    ty = as_rhs_rows(row_table(128, 1.0))
    ax = as_lhs(row_table(128, 1.0, 1.0 / volume).T)
    bx = as_lhs(row_table(128, -1.0).T)
    vmem = pl.BlockSpec(memory_space=pltpu.VMEM)
    hbm = pl.BlockSpec(memory_space=pltpu.HBM)
    return pl.pallas_call(
        plane_kernel,
        out_shape=jax.ShapeDtypeStruct((slots, 128), F32),
        in_specs=[hbm, vmem] + [hbm] * 4,
        out_specs=vmem,
        scratch_shapes=[
            pltpu.SMEM((slots,), jnp.int32),
            pltpu.VMEM((16, 128, 128), F32),
            pltpu.VMEM((768, 256), BF16),
            pltpu.VMEM((256, 768), BF16),
            pltpu.VMEM((256, 768), BF16),
            pltpu.VMEM((16384, 128), F32),
            pltpu.VMEM((128 * PITCH, 128), F32),
            pltpu.VMEM((128 * PITCH, 128), F32),
            pltpu.SemaphoreType.DMA((5,)),
        ],
        compiler_params=pltpu.CompilerParams(vmem_limit_bytes=52 * 2**20),
        name="planes",
    )(stick_pos, sticks, pot, ty, ax, bx)


COLUMNS = 512


def rotate_kernel(coef_ref, image_ref, applied_ref, ritz_ref, base_ref, out_ref, copy_ref, left_ref):
    @pl.when(pl.program_id(0) == 0)
    def _():
        copy_ref[...] = applied_ref[...]
        for part in range(2):
            for slot in range(4):
                rows = jnp.concatenate(
                    [ref[k, slot, part * 4:part * 4 + 4, :] for k in range(16) for ref in (coef_ref, image_ref)],
                    axis=0).T
                high, low = split(rows)
                at = (part * 4 + slot) * 128
                left_ref[at:at + 128, :] = jnp.concatenate([high, low, high, low], axis=1)

    high, low = split(ritz_ref[...])
    right = jnp.concatenate([high, high, low, low], axis=0)
    for part in range(2):
        out_ref[part] = (base_ref[part].astype(F32)
                         + dot(left_ref[part * 512:(part + 1) * 512, :], right)).astype(BF16)


def rotate(coef, image, ritz, base, applied):
    once = lambda a: pl.BlockSpec(a.shape, lambda j: (0,) * a.ndim)
    slab = pl.BlockSpec((2, base.shape[1], COLUMNS), lambda j: (0, 0, j))
    return pl.pallas_call(
        rotate_kernel,
        grid=(base.shape[2] // COLUMNS,),
        out_shape=[jax.ShapeDtypeStruct(base.shape, BF16), jax.ShapeDtypeStruct(applied.shape, F32)],
        in_specs=[once(coef), once(image), once(applied),
                  pl.BlockSpec((ritz.shape[0], COLUMNS), lambda j: (0, j)), slab],
        out_specs=[slab, once(applied)],
        scratch_shapes=[pltpu.VMEM((1024, 512), BF16)],
        compiler_params=pltpu.CompilerParams(vmem_limit_bytes=56 * 2**20),
        name="rotate",
    )(coef, image, applied, ritz, base)


def greet(n_tg, n_pool, tg, pool):
    barrier = pltpu.get_barrier_semaphore()
    for step in range(1, n_tg):
        pl.semaphore_signal(barrier, inc=1, device_id={"tg": lax.rem(tg + step, n_tg)}, device_id_type=MESH)
    for step in range(1, n_pool):
        pl.semaphore_signal(barrier, inc=1, device_id={"pool": lax.rem(pool + step, n_pool)}, device_id_type=MESH)
    pl.semaphore_wait(barrier, n_tg + n_pool - 2)


class Exchange:
    def __init__(self, axis, size, me, source, target, send_sem, recv_sem, own_sem):
        self.axis, self.size, self.me = axis, size, me
        self.source, self.target = source, target
        self.send_sem, self.recv_sem, self.own_sem = send_sem, recv_sem, own_sem

    def remote(self, step):
        peer = lax.rem(self.me + step, self.size)
        return pltpu.make_async_remote_copy(
            src_ref=self.source.at[peer], dst_ref=self.target.at[self.me],
            send_sem=self.send_sem.at[peer], recv_sem=self.recv_sem.at[self.me],
            device_id={self.axis: peer}, device_id_type=MESH)

    def own(self):
        return pltpu.make_async_copy(self.source.at[self.me], self.target.at[self.me], self.own_sem)

    def start(self):
        for step in range(1, self.size):
            self.remote(step).start()
        self.own().start()

    def wait_recv(self):
        self.own().wait()
        for step in range(1, self.size):
            peer = lax.rem(self.me + step, self.size)
            pltpu.make_async_remote_copy(
                src_ref=self.source.at[peer], dst_ref=self.target.at[peer],
                send_sem=self.send_sem.at[peer], recv_sem=self.recv_sem.at[peer],
                device_id={self.axis: peer}, device_id_type=MESH).wait_recv()

    def wait_send(self):
        for step in range(1, self.size):
            self.remote(step).wait_send()


def pack_rows(flat_ref, pack_ref, n_pool):
    for k in range(n_pool):
        for j in range(4):
            pack_ref[k, j] = flat_ref[pl.ds(k * 4 + j, 8, 64), :]


def spread_kernel(n_tg, n_pool, wave_hbm, count_hbm, table_hbm, ritz_hbm,
                  planes_ref, coef_ref, usable_ref, ritz_ref,
                  wave_ref, count_ref, table_ref, rows_ref, flat_ref, sticks_ref, pack_ref,
                  send_t, recv_t, send_p, recv_p, own_sem, load_sem):
    tg, pool = lax.axis_index("tg"), lax.axis_index("pool")
    pairs = [(count_hbm, count_ref), (wave_hbm, wave_ref), (table_hbm, table_ref), (ritz_hbm, rows_ref)]
    loads = [pltpu.make_async_copy(src, dst, load_sem.at[k]) for k, (src, dst) in enumerate(pairs)]
    for load in loads:
        load.start()
    greet(n_tg, n_pool, tg, pool)
    for load in loads:
        load.wait()
    slot = lax.broadcasted_iota(jnp.int32, (64, 128), 0)
    usable = jnp.where(slot < count_ref[tg], 1.0, 0.0).astype(F32)
    usable_ref[...] = usable
    rows = []
    for band in range(4):
        pair = [wave_ref[part, band] * usable for part in range(2)]
        for part in range(2):
            flat_ref[(part * 4 + band) * 64:(part * 4 + band + 1) * 64, :] = pair[part]
        rows.append(jnp.concatenate(pair, axis=1))
    res = dot(lanes3(jnp.concatenate(rows, axis=0)), table_ref[...])
    for t in range(n_tg):
        sticks_ref[t] = jnp.concatenate(
            [res[band * 64:(band + 1) * 64, part * 128 + t * 16:part * 128 + t * 16 + 16]
             for part in range(2) for band in range(4)], axis=1)
    planes = Exchange("tg", n_tg, tg, sticks_ref, planes_ref, send_t, recv_t, own_sem.at[0])
    planes.start()
    pack_rows(flat_ref, pack_ref, n_pool)
    coef = Exchange("pool", n_pool, pool, pack_ref, coef_ref, send_p, recv_p, own_sem.at[1])
    coef.start()
    for term in range(2):
        ritz_ref[term * 4:term * 4 + 4, :] = rows_ref[term]
    planes.wait_recv()
    coef.wait_recv()
    planes.wait_send()
    coef.wait_send()


def collect_kernel(n_tg, n_pool, cols_ref, usable_ref, table_hbm, applied_ref, image_ref,
                   table_ref, returned_ref, pack_ref, send_t, recv_t, send_p, recv_p, own_sem, load_sem):
    tg, pool = lax.axis_index("tg"), lax.axis_index("pool")
    load = pltpu.make_async_copy(table_hbm, table_ref, load_sem.at[0])
    load.start()
    greet(n_tg, n_pool, tg, pool)
    back = Exchange("tg", n_tg, tg, cols_ref, returned_ref, send_t, recv_t, own_sem.at[0])
    back.start()
    usable = usable_ref[...]
    load.wait()
    back.wait_recv()
    rows = []
    for band in range(4):
        rows.append(jnp.concatenate(
            [returned_ref[t, :, part * 64 + band * 16:part * 64 + band * 16 + 16]
             for part in range(2) for t in range(n_tg)], axis=1))
    res = dot(lanes3(jnp.concatenate(rows, axis=0)), table_ref[...])
    for band in range(4):
        for part in range(2):
            at = (part * 4 + band) * 64
            applied_ref[at:at + 64, :] = res[band * 64:(band + 1) * 64, part * 128:(part + 1) * 128] * usable
    pack_rows(applied_ref, pack_ref, n_pool)
    image = Exchange("pool", n_pool, pool, pack_ref, image_ref, send_p, recv_p, own_sem.at[1])
    image.start()
    image.wait_recv()
    back.wait_send()
    image.wait_send()


def exchange_scratch(n_tg, n_pool):
    dma = pltpu.SemaphoreType.DMA
    return [dma((n_tg,)), dma((n_tg,)), dma((n_pool,)), dma((n_pool,)), dma((2,))]


def spread(wave, count, ritz, n_tg, n_pool):
    vmem = pl.BlockSpec(memory_space=pltpu.VMEM)
    hbm = pl.BlockSpec(memory_space=pltpu.HBM)
    return pl.pallas_call(
        functools.partial(spread_kernel, n_tg, n_pool),
        out_shape=[jax.ShapeDtypeStruct((n_tg, 64, 128), F32), jax.ShapeDtypeStruct((n_pool, 4, 8, 128), F32),
                   jax.ShapeDtypeStruct((64, 128), F32), jax.ShapeDtypeStruct((8, ritz.shape[2]), F32)],
        in_specs=[hbm] * 4,
        out_specs=[vmem] * 4,
        scratch_shapes=[pltpu.VMEM(wave.shape, F32), pltpu.SMEM(count.shape, jnp.int32),
                        pltpu.VMEM((768, 256), BF16), pltpu.VMEM(ritz.shape, F32),
                        pltpu.VMEM((512, 128), F32), pltpu.VMEM((n_tg, 64, 128), F32),
                        pltpu.VMEM((n_pool, 4, 8, 128), F32)] + exchange_scratch(n_tg, n_pool)
        + [pltpu.SemaphoreType.DMA((4,))],
        compiler_params=pltpu.CompilerParams(collective_id=0, has_side_effects=True,
                                             vmem_limit_bytes=48 * 2**20),
        name="spread",
    )(wave, count, as_rhs_rows(row_table(128, 1.0)), ritz)


def collect(columns, usable, n_tg, n_pool):
    vmem = pl.BlockSpec(memory_space=pltpu.VMEM)
    hbm = pl.BlockSpec(memory_space=pltpu.HBM)
    return pl.pallas_call(
        functools.partial(collect_kernel, n_tg, n_pool),
        out_shape=[jax.ShapeDtypeStruct((512, 128), F32), jax.ShapeDtypeStruct((n_pool, 4, 8, 128), F32)],
        in_specs=[vmem, vmem, hbm],
        out_specs=[vmem] * 2,
        scratch_shapes=[pltpu.VMEM((768, 256), BF16), pltpu.VMEM((n_tg, 64, 128), F32),
                        pltpu.VMEM((n_pool, 4, 8, 128), F32)] + exchange_scratch(n_tg, n_pool)
        + [pltpu.SemaphoreType.DMA((1,))],
        compiler_params=pltpu.CompilerParams(collective_id=1, has_side_effects=True,
                                             vmem_limit_bytes=48 * 2**20),
        name="collect",
    )(columns, usable, as_rhs_rows(row_table(128, -1.0)))


def local(wave_coef, potential, stick_pos, stick_count, ritz_block, slab_base):
    n_tg, n_pool = lax.axis_size("tg"), lax.axis_size("pool")
    slots = wave_coef.shape[2]
    planes, coef, usable, ritz_rows = spread(wave_coef, stick_count, ritz_block, n_tg, n_pool)
    ritz_full = lax.all_gather(ritz_rows, "pool", axis=0, tiled=True)
    columns = plane_step(planes.reshape(n_tg * slots, 128), stick_pos, potential)
    applied, image = collect(columns.reshape(n_tg, slots, 128), usable, n_tg, n_pool)
    rotated, applied = rotate(coef, image, ritz_full, slab_base, applied)
    return applied.reshape(wave_coef.shape), rotated


def solution(mesh):
    in_specs = (
        P(None, "pool", "tg", None),
        P("tg", None, None),
        P(),
        P(),
        P(None, "pool", None),
        P(None, ("tg", "pool"), None),
    )
    out_specs = (P(None, "pool", "tg", None), P(None, ("tg", "pool"), None))
    return jax.shard_map(local, mesh=mesh, in_specs=in_specs, out_specs=out_specs, check_vma=False)
```

```python
import functools
import math

import jax
import jax.numpy as jnp
from jax import lax
from jax.experimental import pallas as pl
from jax.experimental.pallas import tpu as pltpu
from jax.sharding import PartitionSpec as P

NX = 128
NY = 128
BF16 = jnp.bfloat16
F32 = jnp.float32
MESH = pl.DeviceIdType.MESH


def cos_sin():
    row = lax.broadcasted_iota(jnp.int32, (128, 128), 0)
    col = lax.broadcasted_iota(jnp.int32, (128, 128), 1)
    angle = ((row * col) & 127).astype(F32) * (2.0 * math.pi / 128)
    return split(jnp.cos(angle)) + split(jnp.sin(angle))


def row_table(cos_t, sin_t, sign):
    plus = sin_t if sign > 0 else -sin_t
    return jnp.concatenate([jnp.concatenate([cos_t, plus], axis=1),
                            jnp.concatenate([-plus, cos_t], axis=1)], axis=0)


def table_pieces(cs, sign):
    return row_table(cs[0], cs[2], sign), row_table(cs[1], cs[3], sign)


def split(values):
    high = values.astype(BF16)
    low = (values - high.astype(F32)).astype(BF16)
    return high, low


def as_rhs_rows(cs, sign):
    high, low = table_pieces(cs, sign)
    return jnp.concatenate([high, high, low], axis=0)


def as_lhs(cs, sign):
    high, low = table_pieces(cs, -sign)
    return jnp.concatenate([high, high, low], axis=1)


def lanes3(values):
    high, low = split(values)
    return jnp.concatenate([high, low, high], axis=1)


def rows3(values):
    high, low = split(values)
    return jnp.concatenate([high, low, high], axis=0)


def dot(a, b):
    return lax.dot_general(a, b, (((1,), (0,)), ((), ())), preferred_element_type=F32)


def dot_nt(a, b):
    return lax.dot_general(a, b, (((1,), (1,)), ((), ())), preferred_element_type=F32)


PITCH = 65
LIMIT = 60 * 2**20
Y_STEP = 16
X_STEP = 2


def plane_kernel(pos_hbm, sticks_hbm, cs_hbm, pot_hbm,
                 out_ref, pos_ref, sticks_ref, cs_ref, pot_ref, ty_ref, ax_ref, bx_ref,
                 grid_ref, re_ref, im_ref, sems):
    slots = sticks_ref.shape[0]
    half = 64
    pairs = [(pos_hbm, pos_ref), (sticks_hbm, sticks_ref), (cs_hbm, cs_ref), (pot_hbm, pot_ref)]
    copies = [pltpu.make_async_copy(src, dst, sems.at[k]) for k, (src, dst) in enumerate(pairs)]
    for copy in copies:
        copy.start()

    @pl.loop(0, 32)
    def _(x):
        grid_ref[pl.ds(pl.multiple_of(x * 512, 512), 512), :] = jnp.zeros((512, 128), F32)

    copies[2].wait()
    cs = [cs_ref[k] for k in range(4)]
    ty_ref[...] = as_rhs_rows(cs, 1)
    ax_ref[...] = as_lhs(cs, 1) * (1.0 / 128.0 ** 3)
    bx_ref[...] = as_lhs(cs, -1)
    copies[0].wait()
    copies[1].wait()

    @pl.loop(0, slots // 8)
    def _(block):
        base = pl.multiple_of(block * 8, 8)
        rows = sticks_ref[pl.ds(base, 8), :]
        for k in range(8):
            grid_ref[pl.ds(pos_ref[base + k], 1), :] = rows[k:k + 1, :]

    @pl.loop(0, 128 // Y_STEP)
    def _(step):
        parts = []
        for k in range(Y_STEP):
            x = step * Y_STEP + k
            flipped = grid_ref[pl.ds(pl.multiple_of(x * 128, 128), 128), :].T
            parts.append(jnp.concatenate([flipped[:half], flipped[half:]], axis=1))
        res = dot(lanes3(jnp.concatenate(parts, axis=0)), ty_ref[...])
        for k in range(Y_STEP):
            to = pl.ds((step * Y_STEP + k) * PITCH, half)
            re_ref[to, :] = res[k * half:(k + 1) * half, :128]
            im_ref[to, :] = res[k * half:(k + 1) * half, 128:]

    copies[3].wait()

    @pl.loop(0, 16, unroll=2)
    def _(z):
        pot = pot_ref[z]
        wide = jnp.concatenate([pot] * X_STEP, axis=1)
        wide = jnp.concatenate([wide, wide], axis=0)
        for group in range(4 // X_STEP):
            at = [pl.ds((group * X_STEP + k) * 16 + z, 128, PITCH) for k in range(X_STEP)]
            data = jnp.concatenate(
                [jnp.concatenate([re_ref[a, :], im_ref[a, :]], axis=0) for a in at], axis=1)
            field = dot(ax_ref[...], rows3(data))
            back = dot(bx_ref[...], rows3(field * wide))
            for k in range(X_STEP):
                re_ref[at[k], :] = back[:128, k * 128:(k + 1) * 128]
                im_ref[at[k], :] = back[128:, k * 128:(k + 1) * 128]

    @pl.loop(0, 128 // Y_STEP)
    def _(step):
        data = jnp.concatenate(
            [jnp.concatenate([ref[pl.ds((step * Y_STEP + k) * PITCH, half), :] for k in range(Y_STEP)], axis=0)
             for ref in (re_ref, im_ref)], axis=1)
        res = dot_nt(bx_ref[...], lanes3(data))
        for k in range(Y_STEP):
            to = pl.ds(pl.multiple_of((step * Y_STEP + k) * 128, 128), 128)
            grid_ref[to, :] = jnp.concatenate(
                [res[:128, k * half:(k + 1) * half], res[128:, k * half:(k + 1) * half]], axis=1)

    @pl.loop(0, slots // 8)
    def _(block):
        base = pl.multiple_of(block * 8, 8)
        out_ref[pl.ds(base, 8), :] = jnp.concatenate(
            [grid_ref[pl.ds(pos_ref[base + k], 1), :] for k in range(8)], axis=0)


def plane_step(sticks, stick_pos, cs, pot):
    slots = sticks.shape[0]
    hbm = pl.BlockSpec(memory_space=pltpu.HBM)
    return pl.pallas_call(
        plane_kernel,
        out_shape=jax.ShapeDtypeStruct((slots, 128), F32),
        in_specs=[hbm] * 4,
        out_specs=pl.BlockSpec(memory_space=pltpu.VMEM),
        scratch_shapes=[
            pltpu.SMEM((slots,), jnp.int32),
            pltpu.VMEM(sticks.shape, F32),
            pltpu.VMEM(cs.shape, BF16),
            pltpu.VMEM((16, 128, 128), F32),
            pltpu.VMEM((768, 256), BF16),
            pltpu.VMEM((256, 768), BF16),
            pltpu.VMEM((256, 768), BF16),
            pltpu.VMEM((16384, 128), F32),
            pltpu.VMEM((128 * PITCH, 128), F32),
            pltpu.VMEM((128 * PITCH, 128), F32),
            pltpu.SemaphoreType.DMA((4,)),
        ],
        compiler_params=pltpu.CompilerParams(vmem_limit_bytes=LIMIT),
        name="planes",
    )(stick_pos, sticks, cs, pot)


COLUMNS = 512


def rotate_kernel(coef_ref, image_ref, applied_ref, ritz_ref, base_ref, out_ref, copy_ref, left_ref):
    @pl.when(pl.program_id(0) == 0)
    def _():
        copy_ref[...] = applied_ref[...]
        for part in range(2):
            for slot in range(4):
                rows = jnp.concatenate(
                    [ref[k, slot, part * 4:part * 4 + 4, :] for k in range(16) for ref in (coef_ref, image_ref)],
                    axis=0).T
                high, low = split(rows)
                at = (part * 4 + slot) * 128
                left_ref[at:at + 128, :] = jnp.concatenate([high, low, high, low], axis=1)

    high, low = split(jnp.concatenate([ritz_ref[k] for k in range(ritz_ref.shape[0])], axis=0))
    right = jnp.concatenate([high, high, low, low], axis=0)
    for part in range(2):
        out_ref[part] = (base_ref[part].astype(F32)
                         + dot(left_ref[part * 512:(part + 1) * 512, :], right)).astype(BF16)


def rotate(coef, image, ritz, base, applied):
    once = lambda a: pl.BlockSpec(a.shape, lambda j: (0,) * a.ndim)
    slab = pl.BlockSpec((2, base.shape[1], COLUMNS), lambda j: (0, 0, j))
    return pl.pallas_call(
        rotate_kernel,
        grid=(base.shape[2] // COLUMNS,),
        out_shape=[jax.ShapeDtypeStruct(base.shape, BF16), jax.ShapeDtypeStruct(applied.shape, F32)],
        in_specs=[once(coef), once(image), once(applied),
                  pl.BlockSpec(ritz.shape[:2] + (COLUMNS,), lambda j: (0, 0, j)), slab],
        out_specs=[slab, once(applied)],
        scratch_shapes=[pltpu.VMEM((1024, 512), BF16)],
        compiler_params=pltpu.CompilerParams(vmem_limit_bytes=LIMIT),
        name="rotate",
    )(coef, image, applied, ritz, base)


def greet(axis, size, me):
    barrier = pltpu.get_barrier_semaphore()
    for step in range(1, size):
        pl.semaphore_signal(barrier, inc=1, device_id={axis: lax.rem(me + step, size)}, device_id_type=MESH)
    return barrier


class Exchange:
    def __init__(self, axis, size, me, source, target, send_sem, recv_sem, own_sem):
        self.axis, self.size, self.me = axis, size, me
        self.source, self.target = source, target
        self.send_sem, self.recv_sem, self.own_sem = send_sem, recv_sem, own_sem

    def remote(self, step):
        peer = lax.rem(self.me + step, self.size)
        return pltpu.make_async_remote_copy(
            src_ref=self.source.at[peer], dst_ref=self.target.at[self.me],
            send_sem=self.send_sem.at[peer], recv_sem=self.recv_sem.at[self.me],
            device_id={self.axis: peer}, device_id_type=MESH)

    def own(self):
        return pltpu.make_async_copy(self.source.at[self.me], self.target.at[self.me], self.own_sem)

    def start(self):
        for step in range(1, self.size):
            self.remote(step).start()
        self.own().start()

    def wait_recv(self):
        self.own().wait()
        for step in range(1, self.size):
            peer = lax.rem(self.me + step, self.size)
            pltpu.make_async_remote_copy(
                src_ref=self.source.at[peer], dst_ref=self.target.at[peer],
                send_sem=self.send_sem.at[peer], recv_sem=self.recv_sem.at[peer],
                device_id={self.axis: peer}, device_id_type=MESH).wait_recv()

    def wait_send(self):
        for step in range(1, self.size):
            self.remote(step).wait_send()


def pack_rows(flat_ref, pack_ref, n_pool):
    for k in range(n_pool):
        for j in range(4):
            pack_ref[k, j] = flat_ref[pl.ds(k * 4 + j, 8, 64), :]


def spread_kernel(n_tg, n_pool, wave_hbm, count_hbm, planes_ref, pack_ref, usable_ref, cs_ref,
                  wave_ref, count_ref, table_ref, flat_ref, sticks_ref, send_t, recv_t, own_sem, load_sem):
    tg = lax.axis_index("tg")
    pairs = [(count_hbm, count_ref), (wave_hbm, wave_ref)]
    loads = [pltpu.make_async_copy(src, dst, load_sem.at[k]) for k, (src, dst) in enumerate(pairs)]
    for load in loads:
        load.start()
    barrier = greet("tg", n_tg, tg)
    cs = cos_sin()
    for k in range(4):
        cs_ref[k] = cs[k]
    table_ref[...] = as_rhs_rows(cs, 1)
    for load in loads:
        load.wait()
    slot = lax.broadcasted_iota(jnp.int32, (64, 128), 0)
    usable = jnp.where(slot < count_ref[tg], 1.0, 0.0).astype(F32)
    usable_ref[...] = usable
    rows = []
    for band in range(4):
        pair = [wave_ref[part, band] * usable for part in range(2)]
        for part in range(2):
            flat_ref[(part * 4 + band) * 64:(part * 4 + band + 1) * 64, :] = pair[part]
        rows.append(jnp.concatenate(pair, axis=1))
    res = dot(lanes3(jnp.concatenate(rows, axis=0)), table_ref[...])
    for t in range(n_tg):
        sticks_ref[t] = jnp.concatenate(
            [res[band * 64:(band + 1) * 64, part * 128 + t * 16:part * 128 + t * 16 + 16]
             for part in range(2) for band in range(4)], axis=1)
    pl.semaphore_wait(barrier, n_tg - 1)
    planes = Exchange("tg", n_tg, tg, sticks_ref, planes_ref, send_t, recv_t, own_sem.at[0])
    planes.start()
    pack_rows(flat_ref, pack_ref, n_pool)
    planes.wait_recv()
    planes.wait_send()


def collect_kernel(n_tg, n_pool, cols_hbm, usable_hbm, cs_hbm, pack_hbm, applied_ref, image_ref, coef_ref,
                   usable_ref, cs_ref, table_ref, returned_ref, pack_ref,
                   send_t, recv_t, send_p, recv_p, send_c, recv_c, own_sem, load_sem):
    tg, pool = lax.axis_index("tg"), lax.axis_index("pool")
    pairs = [(usable_hbm, usable_ref), (cs_hbm, cs_ref)]
    loads = [pltpu.make_async_copy(src, dst, load_sem.at[k]) for k, (src, dst) in enumerate(pairs)]
    for load in loads:
        load.start()
    barrier = greet("tg", n_tg, tg)
    greet("pool", n_pool, pool)
    pl.semaphore_wait(barrier, n_tg + n_pool - 2)
    back = Exchange("tg", n_tg, tg, cols_hbm, returned_ref, send_t, recv_t, own_sem.at[0])
    back.start()
    coef = Exchange("pool", n_pool, pool, pack_hbm, coef_ref, send_c, recv_c, own_sem.at[2])
    coef.start()
    for load in loads:
        load.wait()
    usable = usable_ref[...]
    table_ref[...] = as_rhs_rows([cs_ref[k] for k in range(4)], -1)
    back.wait_recv()
    rows = []
    for band in range(4):
        rows.append(jnp.concatenate(
            [returned_ref[t, :, part * 64 + band * 16:part * 64 + band * 16 + 16]
             for part in range(2) for t in range(n_tg)], axis=1))
    res = dot(lanes3(jnp.concatenate(rows, axis=0)), table_ref[...])
    for band in range(4):
        for part in range(2):
            at = (part * 4 + band) * 64
            applied_ref[at:at + 64, :] = res[band * 64:(band + 1) * 64, part * 128:(part + 1) * 128] * usable
    pack_rows(applied_ref, pack_ref, n_pool)
    image = Exchange("pool", n_pool, pool, pack_ref, image_ref, send_p, recv_p, own_sem.at[1])
    image.start()
    coef.wait_recv()
    image.wait_recv()
    back.wait_send()
    coef.wait_send()
    image.wait_send()


def spread(wave, count, n_tg, n_pool):
    vmem = pl.BlockSpec(memory_space=pltpu.VMEM)
    hbm = pl.BlockSpec(memory_space=pltpu.HBM)
    dma = pltpu.SemaphoreType.DMA
    return pl.pallas_call(
        functools.partial(spread_kernel, n_tg, n_pool),
        out_shape=[jax.ShapeDtypeStruct((n_tg, 64, 128), F32), jax.ShapeDtypeStruct((n_pool, 4, 8, 128), F32),
                   jax.ShapeDtypeStruct((64, 128), F32), jax.ShapeDtypeStruct((4, 128, 128), BF16)],
        in_specs=[hbm] * 2,
        out_specs=[vmem] * 4,
        scratch_shapes=[pltpu.VMEM(wave.shape, F32), pltpu.SMEM(count.shape, jnp.int32),
                        pltpu.VMEM((768, 256), BF16), pltpu.VMEM((512, 128), F32),
                        pltpu.VMEM((n_tg, 64, 128), F32), dma((n_tg,)), dma((n_tg,)), dma((1,)), dma((2,))],
        compiler_params=pltpu.CompilerParams(collective_id=0, has_side_effects=True, vmem_limit_bytes=LIMIT),
        name="spread",
    )(wave, count)


def collect(columns, usable, cs, pack, n_tg, n_pool):
    vmem = pl.BlockSpec(memory_space=pltpu.VMEM)
    hbm = pl.BlockSpec(memory_space=pltpu.HBM)
    dma = pltpu.SemaphoreType.DMA
    return pl.pallas_call(
        functools.partial(collect_kernel, n_tg, n_pool),
        out_shape=[jax.ShapeDtypeStruct((512, 128), F32), jax.ShapeDtypeStruct(pack.shape, F32),
                   jax.ShapeDtypeStruct(pack.shape, F32)],
        in_specs=[hbm] * 4,
        out_specs=[vmem, hbm, hbm],
        scratch_shapes=[pltpu.VMEM(usable.shape, F32), pltpu.VMEM(cs.shape, BF16), pltpu.VMEM((768, 256), BF16),
                        pltpu.VMEM((n_tg, 64, 128), F32), pltpu.VMEM(pack.shape, F32),
                        dma((n_tg,)), dma((n_tg,)), dma((n_pool,)), dma((n_pool,)), dma((n_pool,)), dma((n_pool,)),
                        dma((3,)), dma((2,))],
        compiler_params=pltpu.CompilerParams(collective_id=1, has_side_effects=True, vmem_limit_bytes=LIMIT),
        name="collect",
    )(columns, usable, cs, pack)


def local(wave_coef, potential, stick_pos, stick_count, ritz_block, slab_base):
    n_tg, n_pool = lax.axis_size("tg"), lax.axis_size("pool")
    slots = wave_coef.shape[2]
    ritz_full = lax.all_gather(ritz_block, "pool", axis=0, tiled=True)
    planes, pack, usable, cs = spread(wave_coef, stick_count, n_tg, n_pool)
    columns = plane_step(planes.reshape(n_tg * slots, 128), stick_pos, cs, potential)
    applied, image, coef = collect(columns.reshape(n_tg, slots, 128), usable, cs, pack, n_tg, n_pool)
    rotated, applied = rotate(coef, image, ritz_full, slab_base, applied)
    return applied.reshape(wave_coef.shape), rotated


def solution(mesh):
    in_specs = (
        P(None, "pool", "tg", None),
        P("tg", None, None),
        P(),
        P(),
        P(None, "pool", None),
        P(None, ("tg", "pool"), None),
    )
    out_specs = (P(None, "pool", "tg", None), P(None, ("tg", "pool"), None))
    return jax.shard_map(local, mesh=mesh, in_specs=in_specs, out_specs=out_specs, check_vma=False)
```

```python
import functools
import math

import jax
import jax.numpy as jnp
from jax import lax
from jax.experimental import pallas as pl
from jax.experimental.pallas import tpu as pltpu
from jax.sharding import PartitionSpec as P

NX = 128
NY = 128
BF16 = jnp.bfloat16
F32 = jnp.float32
MESH = pl.DeviceIdType.MESH


def cos_sin():
    row = lax.broadcasted_iota(jnp.int32, (128, 128), 0)
    col = lax.broadcasted_iota(jnp.int32, (128, 128), 1)
    angle = ((row * col) & 127).astype(F32) * (2.0 * math.pi / 128)
    return split(jnp.cos(angle)) + split(jnp.sin(angle))


def row_table(cos_t, sin_t, sign):
    plus = sin_t if sign > 0 else -sin_t
    return jnp.concatenate([jnp.concatenate([cos_t, plus], axis=1),
                            jnp.concatenate([-plus, cos_t], axis=1)], axis=0)


def table_pieces(cs, sign):
    return row_table(cs[0], cs[2], sign), row_table(cs[1], cs[3], sign)


def split(values):
    high = values.astype(BF16)
    low = (values - high.astype(F32)).astype(BF16)
    return high, low


def as_rhs_rows(cs, sign):
    high, low = table_pieces(cs, sign)
    return jnp.concatenate([high, high, low], axis=0)


def as_lhs(cs, sign):
    high, low = table_pieces(cs, -sign)
    return jnp.concatenate([high, high, low], axis=1)


def lanes3(values):
    high, low = split(values)
    return jnp.concatenate([high, low, high], axis=1)


def rows3(values):
    high, low = split(values)
    return jnp.concatenate([high, low, high], axis=0)


def dot(a, b):
    return lax.dot_general(a, b, (((1,), (0,)), ((), ())), preferred_element_type=F32)


def dot_nt(a, b):
    return lax.dot_general(a, b, (((1,), (1,)), ((), ())), preferred_element_type=F32)


PITCH = 65
LIMIT = 60 * 2**20
Y_STEP = 16
X_STEP = 2


def chunk(ref, step):
    rows = Y_STEP * PITCH
    return ref.at[pl.ds(pl.multiple_of(step * rows, 8), rows), :]


def lattice_kernel(pos_hbm, sticks_hbm, cs_hbm, re_hbm, im_hbm,
                   pos_ref, sticks_ref, cs_ref, ty_ref, grid_ref, re_ref, im_ref, sems, out_sems):
    slots = sticks_ref.shape[0]
    half = 64
    pairs = [(pos_hbm, pos_ref), (sticks_hbm, sticks_ref), (cs_hbm, cs_ref)]
    copies = [pltpu.make_async_copy(src, dst, sems.at[k]) for k, (src, dst) in enumerate(pairs)]
    for copy in copies:
        copy.start()

    @pl.loop(0, 32)
    def _(x):
        grid_ref[pl.ds(pl.multiple_of(x * 512, 512), 512), :] = jnp.zeros((512, 128), F32)

    copies[2].wait()
    ty_ref[...] = as_rhs_rows([cs_ref[k] for k in range(4)], 1)
    copies[0].wait()
    copies[1].wait()

    @pl.loop(0, slots // 8)
    def _(block):
        base = pl.multiple_of(block * 8, 8)
        rows = sticks_ref[pl.ds(base, 8), :]
        for k in range(8):
            grid_ref[pl.ds(pos_ref[base + k], 1), :] = rows[k:k + 1, :]

    def stores(step):
        return [pltpu.make_async_copy(chunk(src, step), chunk(dst, step), out_sems.at[k, step])
                for k, (src, dst) in enumerate([(re_ref, re_hbm), (im_ref, im_hbm)])]

    @pl.loop(0, 128 // Y_STEP)
    def _(step):
        parts = []
        for k in range(Y_STEP):
            x = step * Y_STEP + k
            flipped = grid_ref[pl.ds(pl.multiple_of(x * 128, 128), 128), :].T
            parts.append(jnp.concatenate([flipped[:half], flipped[half:]], axis=1))
        res = dot(lanes3(jnp.concatenate(parts, axis=0)), ty_ref[...])
        for k in range(Y_STEP):
            to = pl.ds((step * Y_STEP + k) * PITCH, half)
            re_ref[to, :] = res[k * half:(k + 1) * half, :128]
            im_ref[to, :] = res[k * half:(k + 1) * half, 128:]
        for store in stores(step):
            store.start()

    @pl.loop(0, 128 // Y_STEP)
    def _(step):
        for store in stores(step):
            store.wait()


def lattice(sticks, stick_pos, cs):
    hbm = pl.BlockSpec(memory_space=pltpu.HBM)
    size = (128 * PITCH, 128)
    return pl.pallas_call(
        lattice_kernel,
        out_shape=[jax.ShapeDtypeStruct(size, F32)] * 2,
        in_specs=[hbm] * 3,
        out_specs=[hbm] * 2,
        scratch_shapes=[
            pltpu.SMEM(stick_pos.shape, jnp.int32),
            pltpu.VMEM(sticks.shape, F32),
            pltpu.VMEM(cs.shape, BF16),
            pltpu.VMEM((768, 256), BF16),
            pltpu.VMEM((16384, 128), F32),
            pltpu.VMEM(size, F32),
            pltpu.VMEM(size, F32),
            pltpu.SemaphoreType.DMA((3,)),
            pltpu.SemaphoreType.DMA((2, 128 // Y_STEP)),
        ],
        compiler_params=pltpu.CompilerParams(vmem_limit_bytes=LIMIT),
        name="lattice",
    )(stick_pos, sticks, cs)


def x_transforms(pot_ref, ax_ref, bx_ref, re_ref, im_ref):
    @pl.loop(0, 16, unroll=2)
    def _(z):
        pot = pot_ref[z]
        wide = jnp.concatenate([pot] * X_STEP, axis=1)
        wide = jnp.concatenate([wide, wide], axis=0)
        for group in range(4 // X_STEP):
            at = [pl.ds((group * X_STEP + k) * 16 + z, 128, PITCH) for k in range(X_STEP)]
            data = jnp.concatenate(
                [jnp.concatenate([re_ref[a, :], im_ref[a, :]], axis=0) for a in at], axis=1)
            field = dot(ax_ref[...], rows3(data))
            back = dot(bx_ref[...], rows3(field * wide))
            for k in range(X_STEP):
                re_ref[at[k], :] = back[:128, k * 128:(k + 1) * 128]
                im_ref[at[k], :] = back[128:, k * 128:(k + 1) * 128]


def y_transform_back(bx_ref, re_ref, im_ref, grid_ref):
    half = 64

    @pl.loop(0, 128 // Y_STEP)
    def _(step):
        data = jnp.concatenate(
            [jnp.concatenate([ref[pl.ds((step * Y_STEP + k) * PITCH, half), :] for k in range(Y_STEP)], axis=0)
             for ref in (re_ref, im_ref)], axis=1)
        res = dot_nt(bx_ref[...], lanes3(data))
        for k in range(Y_STEP):
            to = pl.ds(pl.multiple_of((step * Y_STEP + k) * 128, 128), 128)
            grid_ref[to, :] = jnp.concatenate(
                [res[:128, k * half:(k + 1) * half], res[128:, k * half:(k + 1) * half]], axis=1)


COLUMNS = 512


def rotate_kernel(coef_ref, image_ref, applied_ref, ritz_ref, base_ref, out_ref, copy_ref, left_ref):
    @pl.when(pl.program_id(0) == 0)
    def _():
        copy_ref[...] = applied_ref[...]
        for part in range(2):
            for slot in range(4):
                rows = jnp.concatenate(
                    [ref[(y * 4 + z) * 2 + core, slot, part * 4:part * 4 + 4, :]
                     for y in range(2) for core in range(2) for z in range(4) for ref in (coef_ref, image_ref)],
                    axis=0).T
                high, low = split(rows)
                at = (part * 4 + slot) * 128
                left_ref[at:at + 128, :] = jnp.concatenate([high, low, high, low], axis=1)

    high, low = split(jnp.concatenate([ritz_ref[k] for k in range(ritz_ref.shape[0])], axis=0))
    right = jnp.concatenate([high, high, low, low], axis=0)
    for part in range(2):
        out_ref[part] = (base_ref[part].astype(F32)
                         + dot(left_ref[part * 512:(part + 1) * 512, :], right)).astype(BF16)


def rotate(coef, image, ritz, base, applied):
    once = lambda a: pl.BlockSpec(a.shape, lambda j: (0,) * a.ndim)
    slab = pl.BlockSpec((2, base.shape[1], COLUMNS), lambda j: (0, 0, j))
    return pl.pallas_call(
        rotate_kernel,
        grid=(base.shape[2] // COLUMNS,),
        out_shape=[jax.ShapeDtypeStruct(base.shape, BF16), jax.ShapeDtypeStruct(applied.shape, F32)],
        in_specs=[once(coef), once(image), once(applied),
                  pl.BlockSpec(ritz.shape[:2] + (COLUMNS,), lambda j: (0, 0, j)), slab],
        out_specs=[slab, once(applied)],
        scratch_shapes=[pltpu.VMEM((1024, 512), BF16)],
        compiler_params=pltpu.CompilerParams(vmem_limit_bytes=LIMIT),
        name="rotate",
    )(coef, image, applied, ritz, base)


def greet(axis, size, me):
    barrier = pltpu.get_barrier_semaphore()
    for step in range(1, size):
        pl.semaphore_signal(barrier, inc=1, device_id={axis: lax.rem(me + step, size)}, device_id_type=MESH)
    return barrier


class Exchange:
    def __init__(self, axis, size, me, source, target, send_sem, recv_sem, own_sem):
        self.axis, self.size, self.me = axis, size, me
        self.source, self.target = source, target
        self.send_sem, self.recv_sem, self.own_sem = send_sem, recv_sem, own_sem

    def remote(self, step):
        peer = lax.rem(self.me + step, self.size)
        return pltpu.make_async_remote_copy(
            src_ref=self.source.at[peer], dst_ref=self.target.at[self.me],
            send_sem=self.send_sem.at[peer], recv_sem=self.recv_sem.at[self.me],
            device_id={self.axis: peer}, device_id_type=MESH)

    def own(self):
        return pltpu.make_async_copy(self.source.at[self.me], self.target.at[self.me], self.own_sem)

    def start(self, prepare=None):
        for step in range(1, self.size + 1):
            if prepare is not None:
                prepare(lax.rem(self.me + step, self.size))
            if step < self.size:
                self.remote(step).start()
            else:
                self.own().start()

    def wait_recv(self):
        self.own().wait()
        for step in range(1, self.size):
            peer = lax.rem(self.me + step, self.size)
            pltpu.make_async_remote_copy(
                src_ref=self.source.at[peer], dst_ref=self.target.at[peer],
                send_sem=self.send_sem.at[peer], recv_sem=self.recv_sem.at[peer],
                device_id={self.axis: peer}, device_id_type=MESH).wait_recv()

    def wait_send(self):
        for step in range(1, self.size):
            self.remote(step).wait_send()


def pack_rows(flat_ref, pack_ref, n_pool):
    for k in range(n_pool):
        for j in range(4):
            pack_ref[k, j] = flat_ref[pl.ds(k * 4 + j, 8, 64), :]


def pool_parts(pool):
    return pool // 8, lax.rem(pool // 2, 4), lax.rem(pool, 2)


def pool_index(y, z, core):
    return (y * 4 + z) * 2 + core


def remote(src, dst, send, recv, **peer):
    return pltpu.make_async_remote_copy(src_ref=src, dst_ref=dst, send_sem=send, recv_sem=recv,
                                        device_id=peer, device_id_type=MESH)


def spread_kernel(n_tg, n_pool, wave_hbm, count_hbm, ritz_hbm, planes_ref, pack_ref, usable_ref, cs_ref, col_hbm,
                  wave_ref, count_ref, table_ref, flat_ref, sticks_ref, send_t, recv_t, own_sem, load_sem,
                  send_r, recv_r):
    tg, pool = lax.axis_index("tg"), lax.axis_index("pool")
    y, z, core = pool_parts(pool)
    after, before, across = lax.rem(z + 1, 4), lax.rem(z + 3, 4), lax.rem(z + 2, 4)
    up, down = pool_index(y, after, core), pool_index(y, before, core)
    pairs = [(count_hbm, count_ref), (wave_hbm, wave_ref), (ritz_hbm, col_hbm.at[z])]
    loads = [pltpu.make_async_copy(src, dst, load_sem.at[k]) for k, (src, dst) in enumerate(pairs)]
    for load in loads:
        load.start()
    barrier = greet("tg", n_tg, tg)
    for peer in (up, down):
        pl.semaphore_signal(barrier, inc=1, device_id={"pool": peer}, device_id_type=MESH)
    cs = cos_sin()
    for k in range(4):
        cs_ref[k] = cs[k]
    table_ref[...] = as_rhs_rows(cs, 1)
    loads[0].wait()
    loads[1].wait()
    slot = lax.broadcasted_iota(jnp.int32, (64, 128), 0)
    usable = jnp.where(slot < count_ref[tg], 1.0, 0.0).astype(F32)
    usable_ref[...] = usable
    rows = []
    for band in range(4):
        pair = [wave_ref[part, band] * usable for part in range(2)]
        for part in range(2):
            flat_ref[(part * 4 + band) * 64:(part * 4 + band + 1) * 64, :] = pair[part]
        rows.append(jnp.concatenate(pair, axis=1))
    res = dot(lanes3(jnp.concatenate(rows, axis=0)), table_ref[...])
    for t in range(n_tg):
        sticks_ref[t] = jnp.concatenate(
            [res[band * 64:(band + 1) * 64, part * 128 + t * 16:part * 128 + t * 16 + 16]
             for part in range(2) for band in range(4)], axis=1)
    pl.semaphore_wait(barrier, n_tg + 1)
    planes = Exchange("tg", n_tg, tg, sticks_ref, planes_ref, send_t, recv_t, own_sem.at[0])
    planes.start()
    rise = remote(ritz_hbm, col_hbm.at[z], send_r.at[0], recv_r.at[0], pool=up)
    fall = remote(ritz_hbm, col_hbm.at[z], send_r.at[1], recv_r.at[1], pool=down)
    rise.start()
    fall.start()
    pack_rows(flat_ref, pack_ref, n_pool)
    remote(ritz_hbm, col_hbm.at[before], send_r.at[0], recv_r.at[0], pool=up).wait_recv()
    rise_on = remote(col_hbm.at[before, 0], col_hbm.at[before, 0], send_r.at[2], recv_r.at[2], pool=up)
    rise_on.start()
    remote(ritz_hbm, col_hbm.at[after], send_r.at[1], recv_r.at[1], pool=down).wait_recv()
    fall_on = remote(col_hbm.at[after, 1], col_hbm.at[after, 1], send_r.at[3], recv_r.at[3], pool=down)
    fall_on.start()
    planes.wait_recv()
    remote(col_hbm.at[before, 0], col_hbm.at[across, 0], send_r.at[2], recv_r.at[2], pool=up).wait_recv()
    remote(col_hbm.at[after, 1], col_hbm.at[across, 1], send_r.at[3], recv_r.at[3], pool=down).wait_recv()
    loads[2].wait()
    planes.wait_send()
    for copy in (rise, fall, rise_on, fall_on):
        copy.wait_send()


def collect_kernel(n_tg, n_pool, pos_hbm, re_hbm, im_hbm, pot_hbm, usable_hbm, cs_hbm, pack_hbm, col_hbm,
                   applied_ref, image_ref, coef_ref, ritz_ref,
                   pos_ref, re_ref, im_ref, pot_ref, usable_ref, cs_ref,
                   ax_ref, bx_ref, table_ref, grid_ref, cols_ref, returned_ref, pack_ref,
                   send_t, recv_t, send_p, recv_p, send_c, recv_c, own_sem, load_sem, send_r, recv_r):
    tg, pool = lax.axis_index("tg"), lax.axis_index("pool")
    y, z, core = pool_parts(pool)
    pairs = [(cs_hbm, cs_ref), (re_hbm, re_ref), (im_hbm, im_ref), (pot_hbm, pot_ref),
             (usable_hbm, usable_ref), (pos_hbm, pos_ref), (col_hbm, ritz_ref.at[y, core])]
    loads = [pltpu.make_async_copy(src, dst, load_sem.at[k]) for k, (src, dst) in enumerate(pairs)]
    for load in loads:
        load.start()
    barrier = greet("tg", n_tg, tg)
    greet("pool", n_pool, pool)
    loads[0].wait()
    cs = [cs_ref[k] for k in range(4)]
    ax_ref[...] = as_lhs(cs, 1) * (1.0 / 128.0 ** 3)
    bx_ref[...] = as_lhs(cs, -1)
    table_ref[...] = as_rhs_rows(cs, -1)
    pl.semaphore_wait(barrier, n_tg + n_pool - 2)
    next_core = pool_index(y, z, 1 - core)
    next_y = pool_index(1 - y, z, core)
    to_y = remote(col_hbm, ritz_ref.at[y, core], send_r.at[0], recv_r.at[0], pool=next_y)
    to_core = remote(col_hbm, ritz_ref.at[y, core], send_r.at[1], recv_r.at[1], pool=next_core)
    to_y.start()
    to_core.start()
    coef = Exchange("pool", n_pool, pool, pack_hbm, coef_ref, send_c, recv_c, own_sem.at[2])
    coef.start()
    for load in loads[1:4]:
        load.wait()
    x_transforms(pot_ref, ax_ref, bx_ref, re_ref, im_ref)
    remote(col_hbm, ritz_ref.at[1 - y, core], send_r.at[0], recv_r.at[0], pool=next_y).wait_recv()
    on_core = remote(ritz_ref.at[1 - y, core], ritz_ref.at[1 - y, core], send_r.at[2], recv_r.at[2], pool=next_core)
    on_core.start()
    y_transform_back(bx_ref, re_ref, im_ref, grid_ref)
    loads[4].wait()
    loads[5].wait()

    def gather(peer):
        @pl.loop(0, 8)
        def _(block):
            base = pl.multiple_of(block * 8, 8)
            cols_ref[peer, pl.ds(base, 8), :] = jnp.concatenate(
                [grid_ref[pl.ds(pos_ref[peer * 64 + base + k], 1), :] for k in range(8)], axis=0)

    back = Exchange("tg", n_tg, tg, cols_ref, returned_ref, send_t, recv_t, own_sem.at[0])
    back.start(gather)
    usable = usable_ref[...]
    back.wait_recv()
    rows = []
    for band in range(4):
        rows.append(jnp.concatenate(
            [returned_ref[t, :, part * 64 + band * 16:part * 64 + band * 16 + 16]
             for part in range(2) for t in range(n_tg)], axis=1))
    res = dot(lanes3(jnp.concatenate(rows, axis=0)), table_ref[...])
    for band in range(4):
        for part in range(2):
            at = (part * 4 + band) * 64
            applied_ref[at:at + 64, :] = res[band * 64:(band + 1) * 64, part * 128:(part + 1) * 128] * usable
    pack_rows(applied_ref, pack_ref, n_pool)
    image = Exchange("pool", n_pool, pool, pack_ref, image_ref, send_p, recv_p, own_sem.at[1])
    image.start()
    coef.wait_recv()
    loads[6].wait()
    remote(col_hbm, ritz_ref.at[y, 1 - core], send_r.at[1], recv_r.at[1], pool=next_core).wait_recv()
    remote(ritz_ref.at[1 - y, core], ritz_ref.at[1 - y, 1 - core], send_r.at[2], recv_r.at[2],
           pool=next_core).wait_recv()
    image.wait_recv()
    for exchange in (back, coef, image):
        exchange.wait_send()
    for copy in (to_y, to_core, on_core):
        copy.wait_send()


def spread(wave, count, ritz, n_tg, n_pool):
    vmem = pl.BlockSpec(memory_space=pltpu.VMEM)
    hbm = pl.BlockSpec(memory_space=pltpu.HBM)
    dma = pltpu.SemaphoreType.DMA
    return pl.pallas_call(
        functools.partial(spread_kernel, n_tg, n_pool),
        out_shape=[jax.ShapeDtypeStruct((n_tg, 64, 128), F32), jax.ShapeDtypeStruct((n_pool, 4, 8, 128), F32),
                   jax.ShapeDtypeStruct((64, 128), F32), jax.ShapeDtypeStruct((4, 128, 128), BF16),
                   jax.ShapeDtypeStruct((4,) + ritz.shape, F32)],
        in_specs=[hbm] * 3,
        out_specs=[vmem] * 4 + [hbm],
        scratch_shapes=[pltpu.VMEM(wave.shape, F32), pltpu.SMEM(count.shape, jnp.int32),
                        pltpu.VMEM((768, 256), BF16), pltpu.VMEM((512, 128), F32),
                        pltpu.VMEM((n_tg, 64, 128), F32), dma((n_tg,)), dma((n_tg,)), dma((1,)), dma((3,)),
                        dma((4,)), dma((4,))],
        compiler_params=pltpu.CompilerParams(collective_id=0, has_side_effects=True, vmem_limit_bytes=LIMIT),
        name="spread",
    )(wave, count, ritz)


def collect(stick_pos, re, im, pot, usable, cs, pack, col, n_tg, n_pool):
    vmem = pl.BlockSpec(memory_space=pltpu.VMEM)
    hbm = pl.BlockSpec(memory_space=pltpu.HBM)
    dma = pltpu.SemaphoreType.DMA
    return pl.pallas_call(
        functools.partial(collect_kernel, n_tg, n_pool),
        out_shape=[jax.ShapeDtypeStruct((512, 128), F32), jax.ShapeDtypeStruct(pack.shape, F32),
                   jax.ShapeDtypeStruct(pack.shape, F32), jax.ShapeDtypeStruct((2, 2) + col.shape, F32)],
        in_specs=[hbm] * 8,
        out_specs=[vmem, hbm, hbm, hbm],
        scratch_shapes=[pltpu.SMEM(stick_pos.shape, jnp.int32), pltpu.VMEM(re.shape, F32), pltpu.VMEM(im.shape, F32),
                        pltpu.VMEM(pot.shape, F32), pltpu.VMEM(usable.shape, F32), pltpu.VMEM(cs.shape, BF16),
                        pltpu.VMEM((256, 768), BF16), pltpu.VMEM((256, 768), BF16), pltpu.VMEM((768, 256), BF16),
                        pltpu.VMEM((16384, 128), F32), pltpu.VMEM((n_tg, 64, 128), F32),
                        pltpu.VMEM((n_tg, 64, 128), F32), pltpu.VMEM(pack.shape, F32),
                        dma((n_tg,)), dma((n_tg,)), dma((n_pool,)), dma((n_pool,)), dma((n_pool,)), dma((n_pool,)),
                        dma((3,)), dma((7,)), dma((3,)), dma((3,))],
        compiler_params=pltpu.CompilerParams(collective_id=1, has_side_effects=True, vmem_limit_bytes=LIMIT),
        name="collect",
    )(stick_pos, re, im, pot, usable, cs, pack, col)


def local(wave_coef, potential, stick_pos, stick_count, ritz_block, slab_base):
    n_tg, n_pool = lax.axis_size("tg"), lax.axis_size("pool")
    slots = wave_coef.shape[2]
    planes, pack, usable, cs, col = spread(wave_coef, stick_count, ritz_block, n_tg, n_pool)
    re, im = lattice(planes.reshape(n_tg * slots, 128), stick_pos, cs)
    applied, image, coef, ritz = collect(stick_pos, re, im, potential, usable, cs, pack, col, n_tg, n_pool)
    ritz = ritz.reshape((2 * n_pool,) + ritz_block.shape[1:])
    rotated, applied = rotate(coef, image, ritz, slab_base, applied)
    return applied.reshape(wave_coef.shape), rotated


def solution(mesh):
    in_specs = (
        P(None, "pool", "tg", None),
        P("tg", None, None),
        P(),
        P(),
        P(None, "pool", None),
        P(None, ("tg", "pool"), None),
    )
    out_specs = (P(None, "pool", "tg", None), P(None, ("tg", "pool"), None))
    return jax.shard_map(local, mesh=mesh, in_specs=in_specs, out_specs=out_specs, check_vma=False)
```

```python
import functools
import math

import jax
import jax.numpy as jnp
from jax import lax
from jax.experimental import pallas as pl
from jax.experimental.pallas import tpu as pltpu
from jax.sharding import PartitionSpec as P

NX = 128
NY = 128
BF16 = jnp.bfloat16
F32 = jnp.float32
MESH = pl.DeviceIdType.MESH


def cos_sin():
    row = lax.broadcasted_iota(jnp.int32, (128, 128), 0)
    col = lax.broadcasted_iota(jnp.int32, (128, 128), 1)
    angle = ((row * col) & 127).astype(F32) * (2.0 * math.pi / 128)
    return split(jnp.cos(angle)) + split(jnp.sin(angle))


def row_table(cos_t, sin_t, sign):
    plus = sin_t if sign > 0 else -sin_t
    return jnp.concatenate([jnp.concatenate([cos_t, plus], axis=1),
                            jnp.concatenate([-plus, cos_t], axis=1)], axis=0)


def table_pieces(cs, sign):
    return row_table(cs[0], cs[2], sign), row_table(cs[1], cs[3], sign)


def split(values):
    high = values.astype(BF16)
    low = (values - high.astype(F32)).astype(BF16)
    return high, low


def as_rhs_rows(cs, sign):
    high, low = table_pieces(cs, sign)
    return jnp.concatenate([high, high, low], axis=0)


def as_lhs(cs, sign):
    high, low = table_pieces(cs, -sign)
    return jnp.concatenate([high, high, low], axis=1)


def lanes3(values):
    high, low = split(values)
    return jnp.concatenate([high, low, high], axis=1)


def rows3(values):
    high, low = split(values)
    return jnp.concatenate([high, low, high], axis=0)


def dot(a, b):
    return lax.dot_general(a, b, (((1,), (0,)), ((), ())), preferred_element_type=F32)


def dot_nt(a, b):
    return lax.dot_general(a, b, (((1,), (1,)), ((), ())), preferred_element_type=F32)


PITCH = 33
HALF = 128 * PITCH
LIMIT = 60 * 2**20
Y_STEP = 16


def chunk(ref, pair, step):
    rows = Y_STEP * PITCH
    return ref.at[pl.ds(pl.multiple_of(pair * HALF + step * rows, 8), rows), :]


def lattice_kernel(pos_hbm, sticks_hbm, cs_hbm, re_hbm, im_hbm,
                   pos_ref, sticks_ref, cs_ref, ty_ref, grid_ref, re_ref, im_ref, sems, out_sems):
    slots = sticks_ref.shape[0]
    half = 64
    pairs = [(pos_hbm, pos_ref), (sticks_hbm, sticks_ref), (cs_hbm, cs_ref)]
    copies = [pltpu.make_async_copy(src, dst, sems.at[k]) for k, (src, dst) in enumerate(pairs)]
    for copy in copies:
        copy.start()

    @pl.loop(0, 32)
    def _(x):
        grid_ref[pl.ds(pl.multiple_of(x * 512, 512), 512), :] = jnp.zeros((512, 128), F32)

    copies[2].wait()
    ty_ref[...] = as_rhs_rows([cs_ref[k] for k in range(4)], 1)
    copies[0].wait()
    copies[1].wait()

    @pl.loop(0, slots // 8)
    def _(block):
        base = pl.multiple_of(block * 8, 8)
        rows = sticks_ref[pl.ds(base, 8), :]
        for k in range(8):
            grid_ref[pl.ds(pos_ref[base + k], 1), :] = rows[k:k + 1, :]

    def stores(step):
        return [pltpu.make_async_copy(chunk(src, pair, step), chunk(dst, pair, step), out_sems.at[k, pair, step])
                for pair in range(2) for k, (src, dst) in enumerate([(re_ref, re_hbm), (im_ref, im_hbm)])]

    @pl.loop(0, 128 // Y_STEP, unroll=8)
    def _(step):
        parts = []
        for k in range(Y_STEP):
            x = step * Y_STEP + k
            flipped = grid_ref[pl.ds(pl.multiple_of(x * 128, 128), 128), :].T
            parts.append(jnp.concatenate([flipped[:half], flipped[half:]], axis=1))
        res = dot(lanes3(jnp.concatenate(parts, axis=0)), ty_ref[...])
        for k in range(Y_STEP):
            for pair in range(2):
                to = pl.ds(pair * HALF + (step * Y_STEP + k) * PITCH, 32)
                at = k * half + pair * 32
                re_ref[to, :] = res[at:at + 32, :128]
                im_ref[to, :] = res[at:at + 32, 128:]
        for store in stores(step):
            store.start()

    @pl.loop(0, 128 // Y_STEP)
    def _(step):
        for store in stores(step):
            store.wait()


def lattice(sticks, stick_pos, cs):
    hbm = pl.BlockSpec(memory_space=pltpu.HBM)
    size = (2 * HALF, 128)
    return pl.pallas_call(
        lattice_kernel,
        out_shape=[jax.ShapeDtypeStruct(size, F32)] * 2,
        in_specs=[hbm] * 3,
        out_specs=[hbm] * 2,
        scratch_shapes=[
            pltpu.SMEM(stick_pos.shape, jnp.int32),
            pltpu.VMEM(sticks.shape, F32),
            pltpu.VMEM(cs.shape, BF16),
            pltpu.VMEM((768, 256), BF16),
            pltpu.VMEM((16384, 128), F32),
            pltpu.VMEM(size, F32),
            pltpu.VMEM(size, F32),
            pltpu.SemaphoreType.DMA((3,)),
            pltpu.SemaphoreType.DMA((2, 2, 128 // Y_STEP)),
        ],
        compiler_params=pltpu.CompilerParams(vmem_limit_bytes=LIMIT),
        name="lattice",
    )(stick_pos, sticks, cs)


def x_transforms(pair, pot_ref, ax_ref, bx_ref, re_ref, im_ref):
    @pl.loop(0, 16, unroll=16)
    def _(z):
        pot = pot_ref[z]
        wide = jnp.concatenate([pot] * 2, axis=1)
        wide = jnp.concatenate([wide] * 2, axis=0)
        at = [pl.ds(pair * HALF + k * 16 + z, 128, PITCH) for k in range(2)]
        data = jnp.concatenate(
            [jnp.concatenate([re_ref[a, :], im_ref[a, :]], axis=0) for a in at], axis=1)
        field = dot(ax_ref[...], rows3(data))
        back = dot(bx_ref[...], rows3(field * wide))
        for k in range(2):
            re_ref[at[k], :] = back[:128, k * 128:(k + 1) * 128]
            im_ref[at[k], :] = back[128:, k * 128:(k + 1) * 128]


def y_transform_back(bx_ref, re_ref, im_ref, grid_ref):
    half = 64

    @pl.loop(0, 128 // Y_STEP, unroll=4)
    def _(step):
        data = jnp.concatenate(
            [jnp.concatenate([ref[pl.ds(pair * HALF + (step * Y_STEP + k) * PITCH, 32), :]
                              for k in range(Y_STEP) for pair in range(2)], axis=0)
             for ref in (re_ref, im_ref)], axis=1)
        res = dot_nt(bx_ref[...], lanes3(data))
        for k in range(Y_STEP):
            to = pl.ds(pl.multiple_of((step * Y_STEP + k) * 128, 128), 128)
            grid_ref[to, :] = jnp.concatenate(
                [res[:128, k * half:(k + 1) * half], res[128:, k * half:(k + 1) * half]], axis=1)


COLUMNS = 1024


def rotate_kernel(coef_ref, image_ref, applied_ref, ritz_ref, base_ref, out_ref, copy_ref, left_ref):
    @pl.when(pl.program_id(0) == 0)
    def _():
        copy_ref[...] = applied_ref[...]
        for part in range(2):
            for slot in range(4):
                rows = jnp.concatenate(
                    [ref[(y * 4 + z) * 2 + core, slot, part * 4:part * 4 + 4, :]
                     for y in range(2) for core in range(2) for z in range(4) for ref in (coef_ref, image_ref)],
                    axis=0).T
                high, low = split(rows)
                at = (part * 4 + slot) * 128
                left_ref[at:at + 128, :] = jnp.concatenate([high, low, high, low], axis=1)

    high, low = split(jnp.concatenate([ritz_ref[k] for k in range(ritz_ref.shape[0])], axis=0))
    right = jnp.concatenate([high, high, low, low], axis=0)
    for part in range(2):
        out_ref[part] = (base_ref[part].astype(F32)
                         + dot(left_ref[part * 512:(part + 1) * 512, :], right)).astype(BF16)


def rotate(coef, image, ritz, base, applied):
    once = lambda a: pl.BlockSpec(a.shape, lambda j: (0,) * a.ndim)
    slab = pl.BlockSpec((2, base.shape[1], COLUMNS), lambda j: (0, 0, j))
    return pl.pallas_call(
        rotate_kernel,
        grid=(base.shape[2] // COLUMNS,),
        out_shape=[jax.ShapeDtypeStruct(base.shape, BF16), jax.ShapeDtypeStruct(applied.shape, F32)],
        in_specs=[once(coef), once(image), once(applied),
                  pl.BlockSpec(ritz.shape[:2] + (COLUMNS,), lambda j: (0, 0, j)), slab],
        out_specs=[slab, once(applied)],
        scratch_shapes=[pltpu.VMEM((1024, 512), BF16)],
        compiler_params=pltpu.CompilerParams(vmem_limit_bytes=LIMIT),
        name="rotate",
    )(coef, image, applied, ritz, base)


def greet(axis, size, me):
    barrier = pltpu.get_barrier_semaphore()
    for step in range(1, size):
        pl.semaphore_signal(barrier, inc=1, device_id={axis: lax.rem(me + step, size)}, device_id_type=MESH)
    return barrier


class Exchange:
    def __init__(self, axis, size, me, source, target, send_sem, recv_sem, own_sem):
        self.axis, self.size, self.me = axis, size, me
        self.source, self.target = source, target
        self.send_sem, self.recv_sem, self.own_sem = send_sem, recv_sem, own_sem

    def remote(self, step):
        peer = lax.rem(self.me + step, self.size)
        return pltpu.make_async_remote_copy(
            src_ref=self.source.at[peer], dst_ref=self.target.at[self.me],
            send_sem=self.send_sem.at[peer], recv_sem=self.recv_sem.at[self.me],
            device_id={self.axis: peer}, device_id_type=MESH)

    def own(self):
        return pltpu.make_async_copy(self.source.at[self.me], self.target.at[self.me], self.own_sem)

    def start(self, prepare=None):
        for step in range(1, self.size + 1):
            if prepare is not None:
                prepare(lax.rem(self.me + step, self.size))
            if step < self.size:
                self.remote(step).start()
            else:
                self.own().start()

    def wait_recv(self):
        self.own().wait()
        for step in range(1, self.size):
            peer = lax.rem(self.me + step, self.size)
            pltpu.make_async_remote_copy(
                src_ref=self.source.at[peer], dst_ref=self.target.at[peer],
                send_sem=self.send_sem.at[peer], recv_sem=self.recv_sem.at[peer],
                device_id={self.axis: peer}, device_id_type=MESH).wait_recv()

    def wait_send(self):
        for step in range(1, self.size):
            self.remote(step).wait_send()


def pack_rows(flat_ref, pack_ref, n_pool):
    for k in range(n_pool):
        for j in range(4):
            pack_ref[k, j] = flat_ref[pl.ds(k * 4 + j, 8, 64), :]


def pool_parts(pool):
    return pool // 8, lax.rem(pool // 2, 4), lax.rem(pool, 2)


def pool_index(y, z, core):
    return (y * 4 + z) * 2 + core


def remote(src, dst, send, recv, **peer):
    return pltpu.make_async_remote_copy(src_ref=src, dst_ref=dst, send_sem=send, recv_sem=recv,
                                        device_id=peer, device_id_type=MESH)


def spread_kernel(n_tg, n_pool, wave_hbm, count_hbm, ritz_hbm, planes_ref, pack_ref, usable_ref, cs_ref, col_hbm,
                  wave_ref, count_ref, table_ref, flat_ref, sticks_ref, send_t, recv_t, own_sem, load_sem,
                  send_r, recv_r):
    tg, pool = lax.axis_index("tg"), lax.axis_index("pool")
    y, z, core = pool_parts(pool)
    after, before, across = lax.rem(z + 1, 4), lax.rem(z + 3, 4), lax.rem(z + 2, 4)
    up, down = pool_index(y, after, core), pool_index(y, before, core)
    pairs = [(count_hbm, count_ref), (wave_hbm, wave_ref), (ritz_hbm, col_hbm.at[z])]
    loads = [pltpu.make_async_copy(src, dst, load_sem.at[k]) for k, (src, dst) in enumerate(pairs)]
    for load in loads:
        load.start()
    barrier = greet("tg", n_tg, tg)
    for peer in (up, down):
        pl.semaphore_signal(barrier, inc=1, device_id={"pool": peer}, device_id_type=MESH)
    cs = cos_sin()
    for k in range(4):
        cs_ref[k] = cs[k]
    table_ref[...] = as_rhs_rows(cs, 1)
    loads[0].wait()
    loads[1].wait()
    pl.semaphore_wait(barrier, n_tg + 1)
    rise = remote(ritz_hbm, col_hbm.at[z], send_r.at[0], recv_r.at[0], pool=up)
    fall = remote(ritz_hbm, col_hbm.at[z], send_r.at[1], recv_r.at[1], pool=down)
    rise.start()
    fall.start()
    slot = lax.broadcasted_iota(jnp.int32, (64, 128), 0)
    usable = jnp.where(slot < count_ref[tg], 1.0, 0.0).astype(F32)
    usable_ref[...] = usable
    rows = []
    for band in range(4):
        pair = [wave_ref[part, band] * usable for part in range(2)]
        for part in range(2):
            flat_ref[(part * 4 + band) * 64:(part * 4 + band + 1) * 64, :] = pair[part]
        rows.append(jnp.concatenate(pair, axis=1))
    res = dot(lanes3(jnp.concatenate(rows, axis=0)), table_ref[...])
    for t in range(n_tg):
        sticks_ref[t] = jnp.concatenate(
            [res[band * 64:(band + 1) * 64, part * 128 + t * 16:part * 128 + t * 16 + 16]
             for part in range(2) for band in range(4)], axis=1)
    planes = Exchange("tg", n_tg, tg, sticks_ref, planes_ref, send_t, recv_t, own_sem.at[0])
    planes.start()
    pack_rows(flat_ref, pack_ref, n_pool)
    remote(ritz_hbm, col_hbm.at[before], send_r.at[0], recv_r.at[0], pool=up).wait_recv()
    rise_on = remote(col_hbm.at[before, 0], col_hbm.at[before, 0], send_r.at[2], recv_r.at[2], pool=up)
    rise_on.start()
    remote(ritz_hbm, col_hbm.at[after], send_r.at[1], recv_r.at[1], pool=down).wait_recv()
    fall_on = remote(col_hbm.at[after, 1], col_hbm.at[after, 1], send_r.at[3], recv_r.at[3], pool=down)
    fall_on.start()
    planes.wait_recv()
    remote(col_hbm.at[before, 0], col_hbm.at[across, 0], send_r.at[2], recv_r.at[2], pool=up).wait_recv()
    remote(col_hbm.at[after, 1], col_hbm.at[across, 1], send_r.at[3], recv_r.at[3], pool=down).wait_recv()
    loads[2].wait()
    planes.wait_send()
    for copy in (rise, fall, rise_on, fall_on):
        copy.wait_send()


def collect_kernel(n_tg, n_pool, pos_hbm, re_hbm, im_hbm, pot_hbm, usable_hbm, cs_hbm, pack_hbm, col_hbm,
                   applied_ref, image_ref, coef_ref, ritz_ref,
                   pos_ref, re_ref, im_ref, pot_ref, usable_ref, cs_ref,
                   ax_ref, bx_ref, table_ref, grid_ref, cols_ref, returned_ref, pack_ref,
                   send_t, recv_t, send_p, recv_p, send_c, recv_c, own_sem, load_sem, send_r, recv_r):
    tg, pool = lax.axis_index("tg"), lax.axis_index("pool")
    y, z, core = pool_parts(pool)
    halves = [(src.at[pl.ds(pair * HALF, HALF), :], dst.at[pl.ds(pair * HALF, HALF), :])
              for pair in range(2) for src, dst in ((re_hbm, re_ref), (im_hbm, im_ref))]
    pairs = [(cs_hbm, cs_ref), (pot_hbm, pot_ref)] + halves + [
        (usable_hbm, usable_ref), (pos_hbm, pos_ref), (col_hbm, ritz_ref.at[y, core])]
    loads = [pltpu.make_async_copy(src, dst, load_sem.at[k]) for k, (src, dst) in enumerate(pairs)]
    for load in loads:
        load.start()
    barrier = greet("tg", n_tg, tg)
    greet("pool", n_pool, pool)
    loads[0].wait()
    cs = [cs_ref[k] for k in range(4)]
    ax_ref[...] = as_lhs(cs, 1) * (1.0 / 128.0 ** 3)
    bx_ref[...] = as_lhs(cs, -1)
    table_ref[...] = as_rhs_rows(cs, -1)
    pl.semaphore_wait(barrier, n_tg + n_pool - 2)
    next_core = pool_index(y, z, 1 - core)
    next_y = pool_index(1 - y, z, core)
    to_y = remote(col_hbm, ritz_ref.at[y, core], send_r.at[0], recv_r.at[0], pool=next_y)
    to_core = remote(col_hbm, ritz_ref.at[y, core], send_r.at[1], recv_r.at[1], pool=next_core)
    to_y.start()
    to_core.start()
    coef = Exchange("pool", n_pool, pool, pack_hbm, coef_ref, send_c, recv_c, own_sem.at[2])
    coef.start()
    loads[1].wait()
    for pair in range(2):
        loads[2 + 2 * pair].wait()
        loads[3 + 2 * pair].wait()
        x_transforms(pair, pot_ref, ax_ref, bx_ref, re_ref, im_ref)
    y_transform_back(bx_ref, re_ref, im_ref, grid_ref)
    remote(col_hbm, ritz_ref.at[1 - y, core], send_r.at[0], recv_r.at[0], pool=next_y).wait_recv()
    on_core = remote(ritz_ref.at[1 - y, core], ritz_ref.at[1 - y, core], send_r.at[2], recv_r.at[2], pool=next_core)
    on_core.start()
    loads[6].wait()
    loads[7].wait()

    def gather(peer):
        @pl.loop(0, 8)
        def _(block):
            base = pl.multiple_of(block * 8, 8)
            cols_ref[peer, pl.ds(base, 8), :] = jnp.concatenate(
                [grid_ref[pl.ds(pos_ref[peer * 64 + base + k], 1), :] for k in range(8)], axis=0)

    back = Exchange("tg", n_tg, tg, cols_ref, returned_ref, send_t, recv_t, own_sem.at[0])
    back.start(gather)
    usable = usable_ref[...]
    back.wait_recv()
    rows = []
    for band in range(4):
        rows.append(jnp.concatenate(
            [returned_ref[t, :, part * 64 + band * 16:part * 64 + band * 16 + 16]
             for part in range(2) for t in range(n_tg)], axis=1))
    res = dot(lanes3(jnp.concatenate(rows, axis=0)), table_ref[...])
    for band in range(4):
        for part in range(2):
            at = (part * 4 + band) * 64
            applied_ref[at:at + 64, :] = res[band * 64:(band + 1) * 64, part * 128:(part + 1) * 128] * usable
    pack_rows(applied_ref, pack_ref, n_pool)
    image = Exchange("pool", n_pool, pool, pack_ref, image_ref, send_p, recv_p, own_sem.at[1])
    image.start()
    coef.wait_recv()
    loads[8].wait()
    remote(col_hbm, ritz_ref.at[y, 1 - core], send_r.at[1], recv_r.at[1], pool=next_core).wait_recv()
    remote(ritz_ref.at[1 - y, core], ritz_ref.at[1 - y, 1 - core], send_r.at[2], recv_r.at[2],
           pool=next_core).wait_recv()
    image.wait_recv()
    for exchange in (back, coef, image):
        exchange.wait_send()
    for copy in (to_y, to_core, on_core):
        copy.wait_send()


def spread(wave, count, ritz, n_tg, n_pool):
    vmem = pl.BlockSpec(memory_space=pltpu.VMEM)
    hbm = pl.BlockSpec(memory_space=pltpu.HBM)
    dma = pltpu.SemaphoreType.DMA
    return pl.pallas_call(
        functools.partial(spread_kernel, n_tg, n_pool),
        out_shape=[jax.ShapeDtypeStruct((n_tg, 64, 128), F32), jax.ShapeDtypeStruct((n_pool, 4, 8, 128), F32),
                   jax.ShapeDtypeStruct((64, 128), F32), jax.ShapeDtypeStruct((4, 128, 128), BF16),
                   jax.ShapeDtypeStruct((4,) + ritz.shape, F32)],
        in_specs=[hbm] * 3,
        out_specs=[vmem] * 4 + [hbm],
        scratch_shapes=[pltpu.VMEM(wave.shape, F32), pltpu.SMEM(count.shape, jnp.int32),
                        pltpu.VMEM((768, 256), BF16), pltpu.VMEM((512, 128), F32),
                        pltpu.VMEM((n_tg, 64, 128), F32), dma((n_tg,)), dma((n_tg,)), dma((1,)), dma((3,)),
                        dma((4,)), dma((4,))],
        compiler_params=pltpu.CompilerParams(collective_id=0, has_side_effects=True, vmem_limit_bytes=LIMIT),
        name="spread",
    )(wave, count, ritz)


def collect(stick_pos, re, im, pot, usable, cs, pack, col, n_tg, n_pool):
    vmem = pl.BlockSpec(memory_space=pltpu.VMEM)
    hbm = pl.BlockSpec(memory_space=pltpu.HBM)
    dma = pltpu.SemaphoreType.DMA
    return pl.pallas_call(
        functools.partial(collect_kernel, n_tg, n_pool),
        out_shape=[jax.ShapeDtypeStruct((512, 128), F32), jax.ShapeDtypeStruct(pack.shape, F32),
                   jax.ShapeDtypeStruct(pack.shape, F32), jax.ShapeDtypeStruct((2, 2) + col.shape, F32)],
        in_specs=[hbm] * 8,
        out_specs=[vmem, hbm, hbm, hbm],
        scratch_shapes=[pltpu.SMEM(stick_pos.shape, jnp.int32), pltpu.VMEM(re.shape, F32), pltpu.VMEM(im.shape, F32),
                        pltpu.VMEM(pot.shape, F32), pltpu.VMEM(usable.shape, F32), pltpu.VMEM(cs.shape, BF16),
                        pltpu.VMEM((256, 768), BF16), pltpu.VMEM((256, 768), BF16), pltpu.VMEM((768, 256), BF16),
                        pltpu.VMEM((16384, 128), F32), pltpu.VMEM((n_tg, 64, 128), F32),
                        pltpu.VMEM((n_tg, 64, 128), F32), pltpu.VMEM(pack.shape, F32),
                        dma((n_tg,)), dma((n_tg,)), dma((n_pool,)), dma((n_pool,)), dma((n_pool,)), dma((n_pool,)),
                        dma((3,)), dma((9,)), dma((3,)), dma((3,))],
        compiler_params=pltpu.CompilerParams(collective_id=1, has_side_effects=True, vmem_limit_bytes=LIMIT),
        name="collect",
    )(stick_pos, re, im, pot, usable, cs, pack, col)


def local(wave_coef, potential, stick_pos, stick_count, ritz_block, slab_base):
    n_tg, n_pool = lax.axis_size("tg"), lax.axis_size("pool")
    slots = wave_coef.shape[2]
    planes, pack, usable, cs, col = spread(wave_coef, stick_count, ritz_block, n_tg, n_pool)
    re, im = lattice(planes.reshape(n_tg * slots, 128), stick_pos, cs)
    applied, image, coef, ritz = collect(stick_pos, re, im, potential, usable, cs, pack, col, n_tg, n_pool)
    ritz = ritz.reshape((2 * n_pool,) + ritz_block.shape[1:])
    rotated, applied = rotate(coef, image, ritz, slab_base, applied)
    return applied.reshape(wave_coef.shape), rotated


def solution(mesh):
    in_specs = (
        P(None, "pool", "tg", None),
        P("tg", None, None),
        P(),
        P(),
        P(None, "pool", None),
        P(None, ("tg", "pool"), None),
    )
    out_specs = (P(None, "pool", "tg", None), P(None, ("tg", "pool"), None))
    return jax.shard_map(local, mesh=mesh, in_specs=in_specs, out_specs=out_specs, check_vma=False)
```

```python
import functools
import math

import jax
import jax.numpy as jnp
from jax import lax
from jax.experimental import pallas as pl
from jax.experimental.pallas import tpu as pltpu
from jax.sharding import PartitionSpec as P

NX = 128
NY = 128
BF16 = jnp.bfloat16
F32 = jnp.float32
MESH = pl.DeviceIdType.MESH


def cos_sin():
    row = lax.broadcasted_iota(jnp.int32, (128, 128), 0)
    col = lax.broadcasted_iota(jnp.int32, (128, 128), 1)
    angle = ((row * col) & 127).astype(F32) * (2.0 * math.pi / 128)
    return split(jnp.cos(angle)) + split(jnp.sin(angle))


def row_table(cos_t, sin_t, sign):
    plus = sin_t if sign > 0 else -sin_t
    return jnp.concatenate([jnp.concatenate([cos_t, plus], axis=1),
                            jnp.concatenate([-plus, cos_t], axis=1)], axis=0)


def table_pieces(cs, sign):
    return row_table(cs[0], cs[2], sign), row_table(cs[1], cs[3], sign)


def split(values):
    high = values.astype(BF16)
    low = (values - high.astype(F32)).astype(BF16)
    return high, low


def as_rhs_rows(cs, sign):
    high, low = table_pieces(cs, sign)
    return jnp.concatenate([high, high, low], axis=0)


def as_lhs(cs, sign):
    high, low = table_pieces(cs, -sign)
    return jnp.concatenate([high, high, low], axis=1)


def lanes3(values):
    high, low = split(values)
    return jnp.concatenate([high, low, high], axis=1)


def rows3(values):
    high, low = split(values)
    return jnp.concatenate([high, low, high], axis=0)


def dot(a, b):
    return lax.dot_general(a, b, (((1,), (0,)), ((), ())), preferred_element_type=F32)


def dot_nt(a, b):
    return lax.dot_general(a, b, (((1,), (1,)), ((), ())), preferred_element_type=F32)


PITCH = 33
HALF = 128 * PITCH
LIMIT = 60 * 2**20
Y_STEP = 16


def chunk(ref, pair, step):
    rows = Y_STEP * PITCH
    return ref.at[pl.ds(pl.multiple_of(pair * HALF + step * rows, 8), rows), :]


def lattice_kernel(pos_hbm, sticks_hbm, cs_hbm, re_hbm, im_hbm,
                   pos_ref, sticks_ref, cs_ref, ty_ref, grid_ref, re_ref, im_ref, sems, out_sems):
    slots = sticks_ref.shape[0]
    half = 64
    pairs = [(pos_hbm, pos_ref), (sticks_hbm, sticks_ref), (cs_hbm, cs_ref)]
    copies = [pltpu.make_async_copy(src, dst, sems.at[k]) for k, (src, dst) in enumerate(pairs)]
    for copy in copies:
        copy.start()

    @pl.loop(0, 32)
    def _(x):
        grid_ref[pl.ds(pl.multiple_of(x * 512, 512), 512), :] = jnp.zeros((512, 128), F32)

    copies[2].wait()
    ty_ref[...] = as_rhs_rows([cs_ref[k] for k in range(4)], 1)
    copies[0].wait()
    copies[1].wait()

    @pl.loop(0, slots // 8)
    def _(block):
        base = pl.multiple_of(block * 8, 8)
        rows = sticks_ref[pl.ds(base, 8), :]
        for k in range(8):
            grid_ref[pl.ds(pos_ref[base + k], 1), :] = rows[k:k + 1, :]

    def stores(step):
        return [pltpu.make_async_copy(chunk(src, pair, step), chunk(dst, pair, step), out_sems.at[k, pair, step])
                for pair in range(2) for k, (src, dst) in enumerate([(re_ref, re_hbm), (im_ref, im_hbm)])]

    @pl.loop(0, 128 // Y_STEP, unroll=8)
    def _(step):
        parts = []
        for k in range(Y_STEP):
            x = step * Y_STEP + k
            flipped = grid_ref[pl.ds(pl.multiple_of(x * 128, 128), 128), :].T
            parts.append(jnp.concatenate([flipped[:half], flipped[half:]], axis=1))
        res = dot(lanes3(jnp.concatenate(parts, axis=0)), ty_ref[...])
        for k in range(Y_STEP):
            for pair in range(2):
                to = pl.ds(pair * HALF + (step * Y_STEP + k) * PITCH, 32)
                at = k * half + pair * 32
                re_ref[to, :] = res[at:at + 32, :128]
                im_ref[to, :] = res[at:at + 32, 128:]
        for store in stores(step):
            store.start()

    @pl.loop(0, 128 // Y_STEP)
    def _(step):
        for store in stores(step):
            store.wait()


def lattice(sticks, stick_pos, cs):
    hbm = pl.BlockSpec(memory_space=pltpu.HBM)
    size = (2 * HALF, 128)
    return pl.pallas_call(
        lattice_kernel,
        out_shape=[jax.ShapeDtypeStruct(size, F32)] * 2,
        in_specs=[hbm] * 3,
        out_specs=[hbm] * 2,
        scratch_shapes=[
            pltpu.SMEM(stick_pos.shape, jnp.int32),
            pltpu.VMEM(sticks.shape, F32),
            pltpu.VMEM(cs.shape, BF16),
            pltpu.VMEM((768, 256), BF16),
            pltpu.VMEM((16384, 128), F32),
            pltpu.VMEM(size, F32),
            pltpu.VMEM(size, F32),
            pltpu.SemaphoreType.DMA((3,)),
            pltpu.SemaphoreType.DMA((2, 2, 128 // Y_STEP)),
        ],
        compiler_params=pltpu.CompilerParams(vmem_limit_bytes=LIMIT),
        name="lattice",
    )(stick_pos, sticks, cs)


def x_transforms(pair, pot_ref, ax_ref, bx_ref, re_ref, im_ref):
    @pl.loop(0, 16, unroll=16)
    def _(z):
        pot = pot_ref[z]
        wide = jnp.concatenate([pot] * 2, axis=1)
        wide = jnp.concatenate([wide] * 2, axis=0)
        at = [pl.ds(pair * HALF + k * 16 + z, 128, PITCH) for k in range(2)]
        data = jnp.concatenate(
            [jnp.concatenate([re_ref[a, :], im_ref[a, :]], axis=0) for a in at], axis=1)
        field = dot(ax_ref[...], rows3(data))
        back = dot(bx_ref[...], rows3(field * wide))
        for k in range(2):
            re_ref[at[k], :] = back[:128, k * 128:(k + 1) * 128]
            im_ref[at[k], :] = back[128:, k * 128:(k + 1) * 128]


def y_transform_back(bx_ref, re_ref, im_ref, grid_ref):
    half = 64

    @pl.loop(0, 128 // Y_STEP, unroll=4)
    def _(step):
        data = jnp.concatenate(
            [jnp.concatenate([ref[pl.ds(pair * HALF + (step * Y_STEP + k) * PITCH, 32), :]
                              for k in range(Y_STEP) for pair in range(2)], axis=0)
             for ref in (re_ref, im_ref)], axis=1)
        res = dot_nt(bx_ref[...], lanes3(data))
        for k in range(Y_STEP):
            to = pl.ds(pl.multiple_of((step * Y_STEP + k) * 128, 128), 128)
            grid_ref[to, :] = jnp.concatenate(
                [res[:128, k * half:(k + 1) * half], res[128:, k * half:(k + 1) * half]], axis=1)


COLUMNS = 1024
DEPTH = 2


def rotate_kernel(coef_hbm, image_hbm, applied_hbm, ritz_hbm, base_hbm, out_hbm, copy_hbm,
                  coef_ref, image_ref, ritz_ref, slab_ref, left_ref, small_sem, ritz_sem, in_sem, out_sem):
    steps = slab_ref.shape[2] // COLUMNS

    def at(step):
        return pl.ds(pl.multiple_of(step * COLUMNS, COLUMNS), COLUMNS)

    def load_ritz(step):
        return pltpu.make_async_copy(ritz_hbm.at[:, :, at(step)], ritz_ref.at[:, :, at(step)], ritz_sem.at[step])

    def load(step):
        return pltpu.make_async_copy(base_hbm.at[:, :, at(step)], slab_ref.at[:, :, at(step)], in_sem.at[step])

    def store(step):
        return pltpu.make_async_copy(slab_ref.at[:, :, at(step)], out_hbm.at[:, :, at(step)], out_sem.at[step])

    pairs = [(coef_hbm, coef_ref), (image_hbm, image_ref), (applied_hbm, copy_hbm)]
    small = [pltpu.make_async_copy(src, dst, small_sem.at[k]) for k, (src, dst) in enumerate(pairs)]
    small[0].start()
    small[1].start()
    for step in range(DEPTH):
        load_ritz(step).start()
        load(step).start()
    small[2].start()
    small[0].wait()
    small[1].wait()
    for part in range(2):
        for slot in range(4):
            rows = jnp.concatenate(
                [ref[(y * 4 + z) * 2 + core, slot, part * 4:part * 4 + 4, :]
                 for y in range(2) for core in range(2) for z in range(4) for ref in (coef_ref, image_ref)],
                axis=0).T
            high, low = split(rows)
            to = (part * 4 + slot) * 128
            left_ref[to:to + 128, :] = jnp.concatenate([high, low, high, low], axis=1)

    @pl.loop(0, steps)
    def _(step):
        load_ritz(step).wait()
        high, low = split(jnp.concatenate([ritz_ref[k, :, at(step)] for k in range(ritz_ref.shape[0])], axis=0))
        right = jnp.concatenate([high, high, low, low], axis=0)
        load(step).wait()

        @pl.when(step + DEPTH < steps)
        def _():
            load_ritz(step + DEPTH).start()
            load(step + DEPTH).start()

        for part in range(2):
            res = dot(left_ref[part * 512:(part + 1) * 512, :], right)
            slab_ref[part, :, at(step)] = (slab_ref[part, :, at(step)].astype(F32) + res).astype(BF16)
        store(step).start()

    @pl.loop(0, steps)
    def _(step):
        store(step).wait()

    small[2].wait()


def rotate(coef, image, ritz, base, applied):
    hbm = pl.BlockSpec(memory_space=pltpu.HBM)
    dma = pltpu.SemaphoreType.DMA
    steps = base.shape[2] // COLUMNS
    return pl.pallas_call(
        rotate_kernel,
        out_shape=[jax.ShapeDtypeStruct(base.shape, BF16), jax.ShapeDtypeStruct(applied.shape, F32)],
        in_specs=[hbm] * 5,
        out_specs=[hbm] * 2,
        scratch_shapes=[pltpu.VMEM(coef.shape, F32), pltpu.VMEM(image.shape, F32), pltpu.VMEM(ritz.shape, F32),
                        pltpu.VMEM(base.shape, BF16), pltpu.VMEM((1024, 512), BF16),
                        dma((3,)), dma((steps,)), dma((steps,)), dma((steps,))],
        compiler_params=pltpu.CompilerParams(vmem_limit_bytes=LIMIT),
        name="rotate",
    )(coef, image, applied, ritz, base)


def greet(axis, size, me):
    barrier = pltpu.get_barrier_semaphore()
    for step in range(1, size):
        pl.semaphore_signal(barrier, inc=1, device_id={axis: lax.rem(me + step, size)}, device_id_type=MESH)
    return barrier


class Exchange:
    def __init__(self, axis, size, me, source, target, send_sem, recv_sem, own_sem):
        self.axis, self.size, self.me = axis, size, me
        self.source, self.target = source, target
        self.send_sem, self.recv_sem, self.own_sem = send_sem, recv_sem, own_sem

    def remote(self, step):
        peer = lax.rem(self.me + step, self.size)
        return pltpu.make_async_remote_copy(
            src_ref=self.source.at[peer], dst_ref=self.target.at[self.me],
            send_sem=self.send_sem.at[peer], recv_sem=self.recv_sem.at[self.me],
            device_id={self.axis: peer}, device_id_type=MESH)

    def own(self):
        return pltpu.make_async_copy(self.source.at[self.me], self.target.at[self.me], self.own_sem)

    def start(self, prepare=None):
        for step in range(1, self.size + 1):
            if prepare is not None:
                prepare(lax.rem(self.me + step, self.size))
            if step < self.size:
                self.remote(step).start()
            else:
                self.own().start()

    def wait_recv(self):
        self.own().wait()
        for step in range(1, self.size):
            peer = lax.rem(self.me + step, self.size)
            pltpu.make_async_remote_copy(
                src_ref=self.source.at[peer], dst_ref=self.target.at[peer],
                send_sem=self.send_sem.at[peer], recv_sem=self.recv_sem.at[peer],
                device_id={self.axis: peer}, device_id_type=MESH).wait_recv()

    def wait_send(self):
        for step in range(1, self.size):
            self.remote(step).wait_send()


def pack_rows(flat_ref, pack_ref, n_pool):
    for k in range(n_pool):
        for j in range(4):
            pack_ref[k, j] = flat_ref[pl.ds(k * 4 + j, 8, 64), :]


def pool_parts(pool):
    return pool // 8, lax.rem(pool // 2, 4), lax.rem(pool, 2)


def pool_index(y, z, core):
    return (y * 4 + z) * 2 + core


def remote(src, dst, send, recv, **peer):
    return pltpu.make_async_remote_copy(src_ref=src, dst_ref=dst, send_sem=send, recv_sem=recv,
                                        device_id=peer, device_id_type=MESH)


def spread_kernel(n_tg, n_pool, wave_hbm, count_hbm, ritz_hbm, planes_ref, pack_ref, usable_ref, cs_ref, col_hbm,
                  wave_ref, count_ref, table_ref, flat_ref, sticks_ref, send_t, recv_t, own_sem, load_sem,
                  send_r, recv_r):
    tg, pool = lax.axis_index("tg"), lax.axis_index("pool")
    y, z, core = pool_parts(pool)
    after, before, across = lax.rem(z + 1, 4), lax.rem(z + 3, 4), lax.rem(z + 2, 4)
    up, down = pool_index(y, after, core), pool_index(y, before, core)
    pairs = [(count_hbm, count_ref), (wave_hbm, wave_ref), (ritz_hbm, col_hbm.at[z])]
    loads = [pltpu.make_async_copy(src, dst, load_sem.at[k]) for k, (src, dst) in enumerate(pairs)]
    for load in loads:
        load.start()
    barrier = greet("tg", n_tg, tg)
    for peer in (up, down):
        pl.semaphore_signal(barrier, inc=1, device_id={"pool": peer}, device_id_type=MESH)
    cs = cos_sin()
    for k in range(4):
        cs_ref[k] = cs[k]
    table_ref[...] = as_rhs_rows(cs, 1)
    loads[0].wait()
    loads[1].wait()
    pl.semaphore_wait(barrier, n_tg + 1)
    rise = remote(ritz_hbm, col_hbm.at[z], send_r.at[0], recv_r.at[0], pool=up)
    fall = remote(ritz_hbm, col_hbm.at[z], send_r.at[1], recv_r.at[1], pool=down)
    rise.start()
    fall.start()
    slot = lax.broadcasted_iota(jnp.int32, (64, 128), 0)
    usable = jnp.where(slot < count_ref[tg], 1.0, 0.0).astype(F32)
    usable_ref[...] = usable
    rows = []
    for band in range(4):
        pair = [wave_ref[part, band] * usable for part in range(2)]
        for part in range(2):
            flat_ref[(part * 4 + band) * 64:(part * 4 + band + 1) * 64, :] = pair[part]
        rows.append(jnp.concatenate(pair, axis=1))
    res = dot(lanes3(jnp.concatenate(rows, axis=0)), table_ref[...])
    for t in range(n_tg):
        sticks_ref[t] = jnp.concatenate(
            [res[band * 64:(band + 1) * 64, part * 128 + t * 16:part * 128 + t * 16 + 16]
             for part in range(2) for band in range(4)], axis=1)
    planes = Exchange("tg", n_tg, tg, sticks_ref, planes_ref, send_t, recv_t, own_sem.at[0])
    planes.start()
    pack_rows(flat_ref, pack_ref, n_pool)
    remote(ritz_hbm, col_hbm.at[before], send_r.at[0], recv_r.at[0], pool=up).wait_recv()
    rise_on = remote(col_hbm.at[before, 0], col_hbm.at[before, 0], send_r.at[2], recv_r.at[2], pool=up)
    rise_on.start()
    remote(ritz_hbm, col_hbm.at[after], send_r.at[1], recv_r.at[1], pool=down).wait_recv()
    fall_on = remote(col_hbm.at[after, 1], col_hbm.at[after, 1], send_r.at[3], recv_r.at[3], pool=down)
    fall_on.start()
    planes.wait_recv()
    remote(col_hbm.at[before, 0], col_hbm.at[across, 0], send_r.at[2], recv_r.at[2], pool=up).wait_recv()
    remote(col_hbm.at[after, 1], col_hbm.at[across, 1], send_r.at[3], recv_r.at[3], pool=down).wait_recv()
    loads[2].wait()
    planes.wait_send()
    for copy in (rise, fall, rise_on, fall_on):
        copy.wait_send()


def collect_kernel(n_tg, n_pool, pos_hbm, re_hbm, im_hbm, pot_hbm, usable_hbm, cs_hbm, pack_hbm, col_hbm,
                   applied_ref, image_ref, coef_ref, ritz_ref,
                   pos_ref, re_ref, im_ref, pot_ref, usable_ref, cs_ref,
                   ax_ref, bx_ref, table_ref, grid_ref, cols_ref, returned_ref, pack_ref,
                   send_t, recv_t, send_p, recv_p, send_c, recv_c, own_sem, load_sem, send_r, recv_r):
    tg, pool = lax.axis_index("tg"), lax.axis_index("pool")
    y, z, core = pool_parts(pool)
    halves = [(src.at[pl.ds(pair * HALF, HALF), :], dst.at[pl.ds(pair * HALF, HALF), :])
              for pair in range(2) for src, dst in ((re_hbm, re_ref), (im_hbm, im_ref))]
    pairs = [(cs_hbm, cs_ref), (pot_hbm, pot_ref)] + halves + [
        (usable_hbm, usable_ref), (pos_hbm, pos_ref), (col_hbm, ritz_ref.at[y, core])]
    loads = [pltpu.make_async_copy(src, dst, load_sem.at[k]) for k, (src, dst) in enumerate(pairs)]
    for load in loads:
        load.start()
    barrier = greet("tg", n_tg, tg)
    greet("pool", n_pool, pool)
    loads[0].wait()
    cs = [cs_ref[k] for k in range(4)]
    ax_ref[...] = as_lhs(cs, 1) * (1.0 / 128.0 ** 3)
    bx_ref[...] = as_lhs(cs, -1)
    table_ref[...] = as_rhs_rows(cs, -1)
    loads[1].wait()
    loads[2].wait()
    loads[3].wait()
    x_transforms(0, pot_ref, ax_ref, bx_ref, re_ref, im_ref)
    pl.semaphore_wait(barrier, n_tg + n_pool - 2)
    next_core = pool_index(y, z, 1 - core)
    next_y = pool_index(1 - y, z, core)
    to_y = remote(col_hbm, ritz_ref.at[y, core], send_r.at[0], recv_r.at[0], pool=next_y)
    to_core = remote(col_hbm, ritz_ref.at[y, core], send_r.at[1], recv_r.at[1], pool=next_core)
    to_y.start()
    to_core.start()
    coef = Exchange("pool", n_pool, pool, pack_hbm, coef_ref, send_c, recv_c, own_sem.at[2])
    coef.start()
    loads[4].wait()
    loads[5].wait()
    x_transforms(1, pot_ref, ax_ref, bx_ref, re_ref, im_ref)
    y_transform_back(bx_ref, re_ref, im_ref, grid_ref)
    remote(col_hbm, ritz_ref.at[1 - y, core], send_r.at[0], recv_r.at[0], pool=next_y).wait_recv()
    on_core = remote(ritz_ref.at[1 - y, core], ritz_ref.at[1 - y, core], send_r.at[2], recv_r.at[2], pool=next_core)
    on_core.start()
    loads[6].wait()
    loads[7].wait()

    def gather(peer):
        @pl.loop(0, 8)
        def _(block):
            base = pl.multiple_of(block * 8, 8)
            cols_ref[peer, pl.ds(base, 8), :] = jnp.concatenate(
                [grid_ref[pl.ds(pos_ref[peer * 64 + base + k], 1), :] for k in range(8)], axis=0)

    back = Exchange("tg", n_tg, tg, cols_ref, returned_ref, send_t, recv_t, own_sem.at[0])
    back.start(gather)
    usable = usable_ref[...]
    back.wait_recv()
    rows = []
    for band in range(4):
        rows.append(jnp.concatenate(
            [returned_ref[t, :, part * 64 + band * 16:part * 64 + band * 16 + 16]
             for part in range(2) for t in range(n_tg)], axis=1))
    res = dot(lanes3(jnp.concatenate(rows, axis=0)), table_ref[...])
    for band in range(4):
        for part in range(2):
            at = (part * 4 + band) * 64
            applied_ref[at:at + 64, :] = res[band * 64:(band + 1) * 64, part * 128:(part + 1) * 128] * usable
    pack_rows(applied_ref, pack_ref, n_pool)
    image = Exchange("pool", n_pool, pool, pack_ref, image_ref, send_p, recv_p, own_sem.at[1])
    image.start()
    coef.wait_recv()
    loads[8].wait()
    remote(col_hbm, ritz_ref.at[y, 1 - core], send_r.at[1], recv_r.at[1], pool=next_core).wait_recv()
    remote(ritz_ref.at[1 - y, core], ritz_ref.at[1 - y, 1 - core], send_r.at[2], recv_r.at[2],
           pool=next_core).wait_recv()
    image.wait_recv()
    for exchange in (back, coef, image):
        exchange.wait_send()
    for copy in (to_y, to_core, on_core):
        copy.wait_send()


def spread(wave, count, ritz, n_tg, n_pool):
    vmem = pl.BlockSpec(memory_space=pltpu.VMEM)
    hbm = pl.BlockSpec(memory_space=pltpu.HBM)
    dma = pltpu.SemaphoreType.DMA
    return pl.pallas_call(
        functools.partial(spread_kernel, n_tg, n_pool),
        out_shape=[jax.ShapeDtypeStruct((n_tg, 64, 128), F32), jax.ShapeDtypeStruct((n_pool, 4, 8, 128), F32),
                   jax.ShapeDtypeStruct((64, 128), F32), jax.ShapeDtypeStruct((4, 128, 128), BF16),
                   jax.ShapeDtypeStruct((4,) + ritz.shape, F32)],
        in_specs=[hbm] * 3,
        out_specs=[vmem] * 4 + [hbm],
        scratch_shapes=[pltpu.VMEM(wave.shape, F32), pltpu.SMEM(count.shape, jnp.int32),
                        pltpu.VMEM((768, 256), BF16), pltpu.VMEM((512, 128), F32),
                        pltpu.VMEM((n_tg, 64, 128), F32), dma((n_tg,)), dma((n_tg,)), dma((1,)), dma((3,)),
                        dma((4,)), dma((4,))],
        compiler_params=pltpu.CompilerParams(collective_id=0, has_side_effects=True, vmem_limit_bytes=LIMIT),
        name="spread",
    )(wave, count, ritz)


def collect(stick_pos, re, im, pot, usable, cs, pack, col, n_tg, n_pool):
    vmem = pl.BlockSpec(memory_space=pltpu.VMEM)
    hbm = pl.BlockSpec(memory_space=pltpu.HBM)
    dma = pltpu.SemaphoreType.DMA
    return pl.pallas_call(
        functools.partial(collect_kernel, n_tg, n_pool),
        out_shape=[jax.ShapeDtypeStruct((512, 128), F32), jax.ShapeDtypeStruct(pack.shape, F32),
                   jax.ShapeDtypeStruct(pack.shape, F32), jax.ShapeDtypeStruct((2, 2) + col.shape, F32)],
        in_specs=[hbm] * 8,
        out_specs=[vmem, hbm, hbm, hbm],
        scratch_shapes=[pltpu.SMEM(stick_pos.shape, jnp.int32), pltpu.VMEM(re.shape, F32), pltpu.VMEM(im.shape, F32),
                        pltpu.VMEM(pot.shape, F32), pltpu.VMEM(usable.shape, F32), pltpu.VMEM(cs.shape, BF16),
                        pltpu.VMEM((256, 768), BF16), pltpu.VMEM((256, 768), BF16), pltpu.VMEM((768, 256), BF16),
                        pltpu.VMEM((16384, 128), F32), pltpu.VMEM((n_tg, 64, 128), F32),
                        pltpu.VMEM((n_tg, 64, 128), F32), pltpu.VMEM(pack.shape, F32),
                        dma((n_tg,)), dma((n_tg,)), dma((n_pool,)), dma((n_pool,)), dma((n_pool,)), dma((n_pool,)),
                        dma((3,)), dma((9,)), dma((3,)), dma((3,))],
        compiler_params=pltpu.CompilerParams(collective_id=1, has_side_effects=True, vmem_limit_bytes=LIMIT),
        name="collect",
    )(stick_pos, re, im, pot, usable, cs, pack, col)


def local(wave_coef, potential, stick_pos, stick_count, ritz_block, slab_base):
    n_tg, n_pool = lax.axis_size("tg"), lax.axis_size("pool")
    slots = wave_coef.shape[2]
    planes, pack, usable, cs, col = spread(wave_coef, stick_count, ritz_block, n_tg, n_pool)
    re, im = lattice(planes.reshape(n_tg * slots, 128), stick_pos, cs)
    applied, image, coef, ritz = collect(stick_pos, re, im, potential, usable, cs, pack, col, n_tg, n_pool)
    ritz = ritz.reshape((2 * n_pool,) + ritz_block.shape[1:])
    rotated, applied = rotate(coef, image, ritz, slab_base, applied)
    return applied.reshape(wave_coef.shape), rotated


def solution(mesh):
    in_specs = (
        P(None, "pool", "tg", None),
        P("tg", None, None),
        P(),
        P(),
        P(None, "pool", None),
        P(None, ("tg", "pool"), None),
    )
    out_specs = (P(None, "pool", "tg", None), P(None, ("tg", "pool"), None))
    return jax.shard_map(local, mesh=mesh, in_specs=in_specs, out_specs=out_specs, check_vma=False)
```

```python
import functools
import math

import jax
import jax.numpy as jnp
from jax import lax
from jax.experimental import pallas as pl
from jax.experimental.pallas import tpu as pltpu
from jax.sharding import PartitionSpec as P

NX = 128
NY = 128
BF16 = jnp.bfloat16
F32 = jnp.float32
MESH = pl.DeviceIdType.MESH


def cos_sin():
    row = lax.broadcasted_iota(jnp.int32, (128, 128), 0)
    col = lax.broadcasted_iota(jnp.int32, (128, 128), 1)
    angle = ((row * col) & 127).astype(F32) * (2.0 * math.pi / 128)
    return split(jnp.cos(angle)) + split(jnp.sin(angle))


def row_table(cos_t, sin_t, sign):
    plus = sin_t if sign > 0 else -sin_t
    return jnp.concatenate([jnp.concatenate([cos_t, plus], axis=1),
                            jnp.concatenate([-plus, cos_t], axis=1)], axis=0)


def table_pieces(cs, sign):
    return row_table(cs[0], cs[2], sign), row_table(cs[1], cs[3], sign)


def split(values):
    high = values.astype(BF16)
    low = (values - high.astype(F32)).astype(BF16)
    return high, low


def as_rhs_rows(cs, sign):
    high, low = table_pieces(cs, sign)
    return jnp.concatenate([high, high, low], axis=0)


def as_lhs(cs, sign):
    high, low = table_pieces(cs, -sign)
    return jnp.concatenate([high, high, low], axis=1)


def lanes3(values):
    high, low = split(values)
    return jnp.concatenate([high, low, high], axis=1)


def rows3(values):
    high, low = split(values)
    return jnp.concatenate([high, low, high], axis=0)


def dot(a, b):
    return lax.dot_general(a, b, (((1,), (0,)), ((), ())), preferred_element_type=F32)


def dot_nt(a, b):
    return lax.dot_general(a, b, (((1,), (1,)), ((), ())), preferred_element_type=F32)


PITCH = 33
HALF = 128 * PITCH
LIMIT = 60 * 2**20
Y_STEP = 16


def chunk(ref, pair, step):
    rows = Y_STEP * PITCH
    return ref.at[pl.ds(pl.multiple_of(pair * HALF + step * rows, 8), rows), :]


def lattice_kernel(pos_hbm, sticks_hbm, cs_hbm, re_hbm, im_hbm,
                   pos_ref, sticks_ref, cs_ref, ty_ref, grid_ref, re_ref, im_ref, sems, out_sems):
    slots = sticks_ref.shape[0]
    half = 64
    pairs = [(pos_hbm, pos_ref), (sticks_hbm, sticks_ref), (cs_hbm, cs_ref)]
    copies = [pltpu.make_async_copy(src, dst, sems.at[k]) for k, (src, dst) in enumerate(pairs)]
    for copy in copies:
        copy.start()

    @pl.loop(0, 32)
    def _(x):
        grid_ref[pl.ds(pl.multiple_of(x * 512, 512), 512), :] = jnp.zeros((512, 128), F32)

    copies[2].wait()
    ty_ref[...] = as_rhs_rows([cs_ref[k] for k in range(4)], 1)
    copies[0].wait()
    copies[1].wait()

    @pl.loop(0, slots // 8)
    def _(block):
        base = pl.multiple_of(block * 8, 8)
        rows = sticks_ref[pl.ds(base, 8), :]
        for k in range(8):
            grid_ref[pl.ds(pos_ref[base + k], 1), :] = rows[k:k + 1, :]

    def stores(step):
        return [pltpu.make_async_copy(chunk(src, pair, step), chunk(dst, pair, step), out_sems.at[k, pair, step])
                for pair in range(2) for k, (src, dst) in enumerate([(re_ref, re_hbm), (im_ref, im_hbm)])]

    @pl.loop(0, 128 // Y_STEP, unroll=8)
    def _(step):
        parts = []
        for k in range(Y_STEP):
            x = step * Y_STEP + k
            flipped = grid_ref[pl.ds(pl.multiple_of(x * 128, 128), 128), :].T
            parts.append(jnp.concatenate([flipped[:half], flipped[half:]], axis=1))
        res = dot(lanes3(jnp.concatenate(parts, axis=0)), ty_ref[...])
        for k in range(Y_STEP):
            for pair in range(2):
                to = pl.ds(pair * HALF + (step * Y_STEP + k) * PITCH, 32)
                at = k * half + pair * 32
                re_ref[to, :] = res[at:at + 32, :128]
                im_ref[to, :] = res[at:at + 32, 128:]
        for store in stores(step):
            store.start()

    @pl.loop(0, 128 // Y_STEP)
    def _(step):
        for store in stores(step):
            store.wait()


def lattice(sticks, stick_pos, cs):
    hbm = pl.BlockSpec(memory_space=pltpu.HBM)
    size = (2 * HALF, 128)
    return pl.pallas_call(
        lattice_kernel,
        out_shape=[jax.ShapeDtypeStruct(size, F32)] * 2,
        in_specs=[hbm] * 3,
        out_specs=[hbm] * 2,
        scratch_shapes=[
            pltpu.SMEM(stick_pos.shape, jnp.int32),
            pltpu.VMEM(sticks.shape, F32),
            pltpu.VMEM(cs.shape, BF16),
            pltpu.VMEM((768, 256), BF16),
            pltpu.VMEM((16384, 128), F32),
            pltpu.VMEM(size, F32),
            pltpu.VMEM(size, F32),
            pltpu.SemaphoreType.DMA((3,)),
            pltpu.SemaphoreType.DMA((2, 2, 128 // Y_STEP)),
        ],
        compiler_params=pltpu.CompilerParams(vmem_limit_bytes=LIMIT),
        name="lattice",
    )(stick_pos, sticks, cs)


def x_transforms(pair, pot_ref, ax_ref, bx_ref, re_ref, im_ref):
    @pl.loop(0, 16, unroll=16)
    def _(z):
        pot = pot_ref[z]
        wide = jnp.concatenate([pot] * 2, axis=1)
        wide = jnp.concatenate([wide] * 2, axis=0)
        at = [pl.ds(pair * HALF + k * 16 + z, 128, PITCH) for k in range(2)]
        data = jnp.concatenate(
            [jnp.concatenate([re_ref[a, :], im_ref[a, :]], axis=0) for a in at], axis=1)
        field = dot(ax_ref[...], rows3(data))
        back = dot(bx_ref[...], rows3(field * wide))
        for k in range(2):
            re_ref[at[k], :] = back[:128, k * 128:(k + 1) * 128]
            im_ref[at[k], :] = back[128:, k * 128:(k + 1) * 128]


def y_transform_back(bx_ref, re_ref, im_ref, grid_ref):
    half = 64

    @pl.loop(0, 128 // Y_STEP, unroll=4)
    def _(step):
        data = jnp.concatenate(
            [jnp.concatenate([ref[pl.ds(pair * HALF + (step * Y_STEP + k) * PITCH, 32), :]
                              for k in range(Y_STEP) for pair in range(2)], axis=0)
             for ref in (re_ref, im_ref)], axis=1)
        res = dot_nt(bx_ref[...], lanes3(data))
        for k in range(Y_STEP):
            to = pl.ds(pl.multiple_of((step * Y_STEP + k) * 128, 128), 128)
            grid_ref[to, :] = jnp.concatenate(
                [res[:128, k * half:(k + 1) * half], res[128:, k * half:(k + 1) * half]], axis=1)


COLUMNS = 1024
DEPTH = 2


def rotate_kernel(coef_hbm, image_hbm, applied_hbm, ritz_hbm, base_hbm, out_hbm, copy_hbm,
                  coef_ref, image_ref, ritz_ref, slab_ref, left_ref, small_sem, ritz_sem, in_sem, out_sem):
    steps = slab_ref.shape[2] // COLUMNS

    def at(step):
        return pl.ds(pl.multiple_of(step * COLUMNS, COLUMNS), COLUMNS)

    def load_ritz(step):
        return pltpu.make_async_copy(ritz_hbm.at[:, :, at(step)], ritz_ref.at[:, :, at(step)], ritz_sem.at[step])

    def load(step):
        return pltpu.make_async_copy(base_hbm.at[:, :, at(step)], slab_ref.at[:, :, at(step)], in_sem.at[step])

    def store(step):
        return pltpu.make_async_copy(slab_ref.at[:, :, at(step)], out_hbm.at[:, :, at(step)], out_sem.at[step])

    pairs = [(coef_hbm, coef_ref), (image_hbm, image_ref), (applied_hbm, copy_hbm)]
    small = [pltpu.make_async_copy(src, dst, small_sem.at[k]) for k, (src, dst) in enumerate(pairs)]
    small[0].start()
    small[1].start()
    for step in range(DEPTH):
        load_ritz(step).start()
        load(step).start()
    small[2].start()
    small[0].wait()
    small[1].wait()
    for part in range(2):
        for slot in range(4):
            rows = jnp.concatenate(
                [ref[(y * 4 + z) * 2 + core, slot, part * 4:part * 4 + 4, :]
                 for y in range(2) for core in range(2) for z in range(4) for ref in (coef_ref, image_ref)],
                axis=0).T
            high, low = split(rows)
            to = (part * 4 + slot) * 128
            left_ref[to:to + 128, :] = jnp.concatenate([high, low, high, low], axis=1)

    @pl.loop(0, steps)
    def _(step):
        load_ritz(step).wait()
        high, low = split(jnp.concatenate([ritz_ref[k, :, at(step)] for k in range(ritz_ref.shape[0])], axis=0))
        right = jnp.concatenate([high, high, low, low], axis=0)
        load(step).wait()

        @pl.when(step + DEPTH < steps)
        def _():
            load_ritz(step + DEPTH).start()
            load(step + DEPTH).start()

        for part in range(2):
            res = dot(left_ref[part * 512:(part + 1) * 512, :], right)
            slab_ref[part, :, at(step)] = (slab_ref[part, :, at(step)].astype(F32) + res).astype(BF16)
        store(step).start()

    @pl.loop(0, steps)
    def _(step):
        store(step).wait()

    small[2].wait()


def rotate(coef, image, ritz, base, applied):
    hbm = pl.BlockSpec(memory_space=pltpu.HBM)
    dma = pltpu.SemaphoreType.DMA
    steps = base.shape[2] // COLUMNS
    return pl.pallas_call(
        rotate_kernel,
        out_shape=[jax.ShapeDtypeStruct(base.shape, BF16), jax.ShapeDtypeStruct(applied.shape, F32)],
        in_specs=[hbm] * 5,
        out_specs=[hbm] * 2,
        scratch_shapes=[pltpu.VMEM(coef.shape, F32), pltpu.VMEM(image.shape, F32), pltpu.VMEM(ritz.shape, F32),
                        pltpu.VMEM(base.shape, BF16), pltpu.VMEM((1024, 512), BF16),
                        dma((3,)), dma((steps,)), dma((steps,)), dma((steps,))],
        compiler_params=pltpu.CompilerParams(vmem_limit_bytes=LIMIT),
        name="rotate",
    )(coef, image, applied, ritz, base)


def greet(axis, size, me):
    barrier = pltpu.get_barrier_semaphore()
    for step in range(1, size):
        pl.semaphore_signal(barrier, inc=1, device_id={axis: lax.rem(me + step, size)}, device_id_type=MESH)
    return barrier


class Exchange:
    def __init__(self, axis, size, me, source, target, send_sem, recv_sem, own_sem):
        self.axis, self.size, self.me = axis, size, me
        self.source, self.target = source, target
        self.send_sem, self.recv_sem, self.own_sem = send_sem, recv_sem, own_sem

    def remote(self, step):
        peer = lax.rem(self.me + step, self.size)
        return pltpu.make_async_remote_copy(
            src_ref=self.source.at[peer], dst_ref=self.target.at[self.me],
            send_sem=self.send_sem.at[peer], recv_sem=self.recv_sem.at[self.me],
            device_id={self.axis: peer}, device_id_type=MESH)

    def own(self):
        return pltpu.make_async_copy(self.source.at[self.me], self.target.at[self.me], self.own_sem)

    def start(self, prepare=None):
        for step in range(1, self.size + 1):
            if prepare is not None:
                prepare(lax.rem(self.me + step, self.size))
            if step < self.size:
                self.remote(step).start()
            else:
                self.own().start()

    def wait_recv(self):
        self.own().wait()
        for step in range(1, self.size):
            peer = lax.rem(self.me + step, self.size)
            pltpu.make_async_remote_copy(
                src_ref=self.source.at[peer], dst_ref=self.target.at[peer],
                send_sem=self.send_sem.at[peer], recv_sem=self.recv_sem.at[peer],
                device_id={self.axis: peer}, device_id_type=MESH).wait_recv()

    def wait_send(self):
        for step in range(1, self.size):
            self.remote(step).wait_send()


def pack_rows(flat_ref, pack_ref, n_pool):
    for k in range(n_pool):
        for j in range(4):
            pack_ref[k, j] = flat_ref[pl.ds(k * 4 + j, 8, 64), :]


def pool_parts(pool):
    return pool // 8, lax.rem(pool // 2, 4), lax.rem(pool, 2)


def pool_index(y, z, core):
    return (y * 4 + z) * 2 + core


def remote(src, dst, send, recv, **peer):
    return pltpu.make_async_remote_copy(src_ref=src, dst_ref=dst, send_sem=send, recv_sem=recv,
                                        device_id=peer, device_id_type=MESH)


def spread_kernel(n_tg, n_pool, wave_hbm, count_hbm, ritz_hbm, planes_ref, pack_ref, usable_ref, cs_ref, col_hbm,
                  wave_ref, count_ref, table_ref, flat_ref, sticks_ref, send_t, recv_t, own_sem, load_sem,
                  send_r, recv_r):
    tg, pool = lax.axis_index("tg"), lax.axis_index("pool")
    y, z, core = pool_parts(pool)
    after, before = lax.rem(z + 1, 4), lax.rem(z + 3, 4)
    up, down = pool_index(y, after, core), pool_index(y, before, core)
    pairs = [(count_hbm, count_ref), (wave_hbm, wave_ref), (ritz_hbm, col_hbm.at[z])]
    loads = [pltpu.make_async_copy(src, dst, load_sem.at[k]) for k, (src, dst) in enumerate(pairs)]
    for load in loads:
        load.start()
    barrier = greet("tg", n_tg, tg)
    for peer in (up, down):
        pl.semaphore_signal(barrier, inc=1, device_id={"pool": peer}, device_id_type=MESH)
    cs = cos_sin()
    for k in range(4):
        cs_ref[k] = cs[k]
    table_ref[...] = as_rhs_rows(cs, 1)
    loads[0].wait()
    loads[1].wait()
    pl.semaphore_wait(barrier, n_tg + 1)
    rise = remote(ritz_hbm, col_hbm.at[z], send_r.at[0], recv_r.at[0], pool=up)
    fall = remote(ritz_hbm, col_hbm.at[z], send_r.at[1], recv_r.at[1], pool=down)
    rise.start()
    fall.start()
    slot = lax.broadcasted_iota(jnp.int32, (64, 128), 0)
    usable = jnp.where(slot < count_ref[tg], 1.0, 0.0).astype(F32)
    usable_ref[...] = usable
    rows = []
    for band in range(4):
        pair = [wave_ref[part, band] * usable for part in range(2)]
        for part in range(2):
            flat_ref[(part * 4 + band) * 64:(part * 4 + band + 1) * 64, :] = pair[part]
        rows.append(jnp.concatenate(pair, axis=1))
    res = dot(lanes3(jnp.concatenate(rows, axis=0)), table_ref[...])
    for t in range(n_tg):
        sticks_ref[t] = jnp.concatenate(
            [res[band * 64:(band + 1) * 64, part * 128 + t * 16:part * 128 + t * 16 + 16]
             for part in range(2) for band in range(4)], axis=1)
    planes = Exchange("tg", n_tg, tg, sticks_ref, planes_ref, send_t, recv_t, own_sem.at[0])
    planes.start()
    pack_rows(flat_ref, pack_ref, n_pool)
    planes.wait_recv()
    remote(ritz_hbm, col_hbm.at[before], send_r.at[0], recv_r.at[0], pool=up).wait_recv()
    remote(ritz_hbm, col_hbm.at[after], send_r.at[1], recv_r.at[1], pool=down).wait_recv()
    loads[2].wait()
    planes.wait_send()
    rise.wait_send()
    fall.wait_send()


def collect_kernel(n_tg, n_pool, pos_hbm, re_hbm, im_hbm, pot_hbm, usable_hbm, cs_hbm, pack_hbm, col_hbm,
                   applied_ref, image_ref, coef_ref, ritz_ref,
                   pos_ref, re_ref, im_ref, pot_ref, usable_ref, cs_ref,
                   ax_ref, bx_ref, table_ref, grid_ref, cols_ref, returned_ref, pack_ref,
                   send_t, recv_t, send_p, recv_p, send_c, recv_c, own_sem, load_sem, send_r, recv_r):
    tg, pool = lax.axis_index("tg"), lax.axis_index("pool")
    y, z, core = pool_parts(pool)
    after, before, across = lax.rem(z + 1, 4), lax.rem(z + 3, 4), lax.rem(z + 2, 4)
    up, down = pool_index(y, after, core), pool_index(y, before, core)
    next_core, next_y = pool_index(y, z, 1 - core), pool_index(1 - y, z, core)
    own, other = ritz_ref.at[y, core], ritz_ref.at[1 - y, core]
    halves = [(src.at[pl.ds(pair * HALF, HALF), :], dst.at[pl.ds(pair * HALF, HALF), :])
              for pair in range(2) for src, dst in ((re_hbm, re_ref), (im_hbm, im_ref))]
    pairs = [(cs_hbm, cs_ref), (pot_hbm, pot_ref)] + halves + [
        (usable_hbm, usable_ref), (pos_hbm, pos_ref)] + [(col_hbm.at[k], own.at[k]) for k in (z, before, after)]
    loads = [pltpu.make_async_copy(src, dst, load_sem.at[k]) for k, (src, dst) in enumerate(pairs)]
    for load in loads:
        load.start()
    barrier = greet("tg", n_tg, tg)
    greet("pool", n_pool, pool)
    loads[0].wait()
    cs = [cs_ref[k] for k in range(4)]
    ax_ref[...] = as_lhs(cs, 1) * (1.0 / 128.0 ** 3)
    bx_ref[...] = as_lhs(cs, -1)
    table_ref[...] = as_rhs_rows(cs, -1)
    pl.semaphore_wait(barrier, n_tg + n_pool - 2)

    def ritz(k, src, dst, peer):
        return remote(src, dst, send_r.at[k], recv_r.at[k], pool=peer)

    sent = [ritz(0, col_hbm.at[z], own.at[z], next_y),
            ritz(1, col_hbm.at[before, 0], own.at[before, 0], up),
            ritz(2, col_hbm.at[after, 1], own.at[after, 1], down)]
    for copy in sent:
        copy.start()
    coef = Exchange("pool", n_pool, pool, pack_hbm, coef_ref, send_c, recv_c, own_sem.at[2])
    coef.start()
    for load in loads[1:4]:
        load.wait()
    x_transforms(0, pot_ref, ax_ref, bx_ref, re_ref, im_ref)
    for load in loads[8:11]:
        load.wait()
    ritz(0, other.at[z], other.at[z], next_y).wait_recv()
    ritz(1, own.at[across, 0], own.at[across, 0], up).wait_recv()
    ritz(2, own.at[across, 1], own.at[across, 1], down).wait_recv()
    stage = [ritz(3, other.at[z], other.at[z], up), ritz(4, other.at[z], other.at[z], down),
             ritz(5, own, own, next_core)]
    for copy in stage:
        copy.start()
    sent += stage
    loads[4].wait()
    loads[5].wait()
    x_transforms(1, pot_ref, ax_ref, bx_ref, re_ref, im_ref)
    ritz(3, other.at[before], other.at[before], up).wait_recv()
    ritz(4, other.at[after], other.at[after], down).wait_recv()
    stage = [ritz(6, other.at[before, 0], other.at[before, 0], up),
             ritz(7, other.at[after, 1], other.at[after, 1], down)]
    for copy in stage:
        copy.start()
    sent += stage
    y_transform_back(bx_ref, re_ref, im_ref, grid_ref)
    ritz(6, other.at[across, 0], other.at[across, 0], up).wait_recv()
    ritz(7, other.at[across, 1], other.at[across, 1], down).wait_recv()
    stage = [ritz(8, other, other, next_core)]
    stage[0].start()
    sent += stage
    loads[6].wait()
    loads[7].wait()

    def gather(peer):
        @pl.loop(0, 8)
        def _(block):
            base = pl.multiple_of(block * 8, 8)
            cols_ref[peer, pl.ds(base, 8), :] = jnp.concatenate(
                [grid_ref[pl.ds(pos_ref[peer * 64 + base + k], 1), :] for k in range(8)], axis=0)

    back = Exchange("tg", n_tg, tg, cols_ref, returned_ref, send_t, recv_t, own_sem.at[0])
    back.start(gather)
    usable = usable_ref[...]
    back.wait_recv()
    rows = []
    for band in range(4):
        rows.append(jnp.concatenate(
            [returned_ref[t, :, part * 64 + band * 16:part * 64 + band * 16 + 16]
             for part in range(2) for t in range(n_tg)], axis=1))
    res = dot(lanes3(jnp.concatenate(rows, axis=0)), table_ref[...])
    for band in range(4):
        for part in range(2):
            at = (part * 4 + band) * 64
            applied_ref[at:at + 64, :] = res[band * 64:(band + 1) * 64, part * 128:(part + 1) * 128] * usable
    pack_rows(applied_ref, pack_ref, n_pool)
    image = Exchange("pool", n_pool, pool, pack_ref, image_ref, send_p, recv_p, own_sem.at[1])
    image.start()
    coef.wait_recv()
    ritz(5, own, ritz_ref.at[y, 1 - core], next_core).wait_recv()
    ritz(8, other, ritz_ref.at[1 - y, 1 - core], next_core).wait_recv()
    image.wait_recv()
    for exchange in (back, coef, image):
        exchange.wait_send()
    for copy in sent:
        copy.wait_send()


def spread(wave, count, ritz, n_tg, n_pool):
    vmem = pl.BlockSpec(memory_space=pltpu.VMEM)
    hbm = pl.BlockSpec(memory_space=pltpu.HBM)
    dma = pltpu.SemaphoreType.DMA
    return pl.pallas_call(
        functools.partial(spread_kernel, n_tg, n_pool),
        out_shape=[jax.ShapeDtypeStruct((n_tg, 64, 128), F32), jax.ShapeDtypeStruct((n_pool, 4, 8, 128), F32),
                   jax.ShapeDtypeStruct((64, 128), F32), jax.ShapeDtypeStruct((4, 128, 128), BF16),
                   jax.ShapeDtypeStruct((4,) + ritz.shape, F32)],
        in_specs=[hbm] * 3,
        out_specs=[vmem] * 4 + [hbm],
        scratch_shapes=[pltpu.VMEM(wave.shape, F32), pltpu.SMEM(count.shape, jnp.int32),
                        pltpu.VMEM((768, 256), BF16), pltpu.VMEM((512, 128), F32),
                        pltpu.VMEM((n_tg, 64, 128), F32), dma((n_tg,)), dma((n_tg,)), dma((1,)), dma((3,)),
                        dma((2,)), dma((2,))],
        compiler_params=pltpu.CompilerParams(collective_id=0, has_side_effects=True, vmem_limit_bytes=LIMIT),
        name="spread",
    )(wave, count, ritz)


def collect(stick_pos, re, im, pot, usable, cs, pack, col, n_tg, n_pool):
    vmem = pl.BlockSpec(memory_space=pltpu.VMEM)
    hbm = pl.BlockSpec(memory_space=pltpu.HBM)
    dma = pltpu.SemaphoreType.DMA
    return pl.pallas_call(
        functools.partial(collect_kernel, n_tg, n_pool),
        out_shape=[jax.ShapeDtypeStruct((512, 128), F32), jax.ShapeDtypeStruct(pack.shape, F32),
                   jax.ShapeDtypeStruct(pack.shape, F32), jax.ShapeDtypeStruct((2, 2) + col.shape, F32)],
        in_specs=[hbm] * 8,
        out_specs=[vmem, hbm, hbm, hbm],
        scratch_shapes=[pltpu.SMEM(stick_pos.shape, jnp.int32), pltpu.VMEM(re.shape, F32), pltpu.VMEM(im.shape, F32),
                        pltpu.VMEM(pot.shape, F32), pltpu.VMEM(usable.shape, F32), pltpu.VMEM(cs.shape, BF16),
                        pltpu.VMEM((256, 768), BF16), pltpu.VMEM((256, 768), BF16), pltpu.VMEM((768, 256), BF16),
                        pltpu.VMEM((16384, 128), F32), pltpu.VMEM((n_tg, 64, 128), F32),
                        pltpu.VMEM((n_tg, 64, 128), F32), pltpu.VMEM(pack.shape, F32),
                        dma((n_tg,)), dma((n_tg,)), dma((n_pool,)), dma((n_pool,)), dma((n_pool,)), dma((n_pool,)),
                        dma((3,)), dma((11,)), dma((9,)), dma((9,))],
        compiler_params=pltpu.CompilerParams(collective_id=1, has_side_effects=True, vmem_limit_bytes=LIMIT),
        name="collect",
    )(stick_pos, re, im, pot, usable, cs, pack, col)


def local(wave_coef, potential, stick_pos, stick_count, ritz_block, slab_base):
    n_tg, n_pool = lax.axis_size("tg"), lax.axis_size("pool")
    slots = wave_coef.shape[2]
    planes, pack, usable, cs, col = spread(wave_coef, stick_count, ritz_block, n_tg, n_pool)
    re, im = lattice(planes.reshape(n_tg * slots, 128), stick_pos, cs)
    applied, image, coef, ritz = collect(stick_pos, re, im, potential, usable, cs, pack, col, n_tg, n_pool)
    ritz = ritz.reshape((2 * n_pool,) + ritz_block.shape[1:])
    rotated, applied = rotate(coef, image, ritz, slab_base, applied)
    return applied.reshape(wave_coef.shape), rotated


def solution(mesh):
    in_specs = (
        P(None, "pool", "tg", None),
        P("tg", None, None),
        P(),
        P(),
        P(None, "pool", None),
        P(None, ("tg", "pool"), None),
    )
    out_specs = (P(None, "pool", "tg", None), P(None, ("tg", "pool"), None))
    return jax.shard_map(local, mesh=mesh, in_specs=in_specs, out_specs=out_specs, check_vma=False)
```

```python
import functools
import math

import jax
import jax.numpy as jnp
from jax import lax
from jax.experimental import pallas as pl
from jax.experimental.pallas import tpu as pltpu
from jax.sharding import PartitionSpec as P

NX = 128
NY = 128
BF16 = jnp.bfloat16
F32 = jnp.float32
MESH = pl.DeviceIdType.MESH


def cos_sin():
    row = lax.broadcasted_iota(jnp.int32, (128, 128), 0)
    col = lax.broadcasted_iota(jnp.int32, (128, 128), 1)
    angle = ((row * col) & 127).astype(F32) * (2.0 * math.pi / 128)
    return split(jnp.cos(angle)) + split(jnp.sin(angle))


def row_table(cos_t, sin_t, sign):
    plus = sin_t if sign > 0 else -sin_t
    return jnp.concatenate([jnp.concatenate([cos_t, plus], axis=1),
                            jnp.concatenate([-plus, cos_t], axis=1)], axis=0)


def table_pieces(cs, sign):
    return row_table(cs[0], cs[2], sign), row_table(cs[1], cs[3], sign)


def split(values):
    high = values.astype(BF16)
    low = (values - high.astype(F32)).astype(BF16)
    return high, low


def as_rhs_rows(cs, sign):
    high, low = table_pieces(cs, sign)
    return jnp.concatenate([high, high, low], axis=0)


def as_lhs(cs, sign):
    high, low = table_pieces(cs, -sign)
    return jnp.concatenate([high, high, low], axis=1)


def lanes3(values):
    high, low = split(values)
    return jnp.concatenate([high, low, high], axis=1)


def rows3(values):
    high, low = split(values)
    return jnp.concatenate([high, low, high], axis=0)


def dot(a, b):
    return lax.dot_general(a, b, (((1,), (0,)), ((), ())), preferred_element_type=F32)


def dot_nt(a, b):
    return lax.dot_general(a, b, (((1,), (1,)), ((), ())), preferred_element_type=F32)


PITCH = 33
HALF = 128 * PITCH
LIMIT = 60 * 2**20
Y_STEP = 16


def chunk(ref, pair, step):
    rows = Y_STEP * PITCH
    return ref.at[pl.ds(pl.multiple_of(pair * HALF + step * rows, 8), rows), :]


def lattice_kernel(pos_hbm, sticks_hbm, cs_hbm, re_hbm, im_hbm,
                   pos_ref, sticks_ref, cs_ref, ty_ref, grid_ref, re_ref, im_ref, sems, out_sems):
    slots = sticks_ref.shape[0]
    half = 64
    pairs = [(pos_hbm, pos_ref), (sticks_hbm, sticks_ref), (cs_hbm, cs_ref)]
    copies = [pltpu.make_async_copy(src, dst, sems.at[k]) for k, (src, dst) in enumerate(pairs)]
    for copy in copies:
        copy.start()

    @pl.loop(0, 32)
    def _(x):
        grid_ref[pl.ds(pl.multiple_of(x * 512, 512), 512), :] = jnp.zeros((512, 128), F32)

    copies[2].wait()
    ty_ref[...] = as_rhs_rows([cs_ref[k] for k in range(4)], 1)
    copies[0].wait()
    copies[1].wait()

    @pl.loop(0, slots // 8)
    def _(block):
        base = pl.multiple_of(block * 8, 8)
        rows = sticks_ref[pl.ds(base, 8), :]
        for k in range(8):
            grid_ref[pl.ds(pos_ref[base + k], 1), :] = rows[k:k + 1, :]

    def stores(step):
        return [pltpu.make_async_copy(chunk(src, pair, step), chunk(dst, pair, step), out_sems.at[k, pair, step])
                for pair in range(2) for k, (src, dst) in enumerate([(re_ref, re_hbm), (im_ref, im_hbm)])]

    @pl.loop(0, 128 // Y_STEP, unroll=8)
    def _(step):
        parts = []
        for k in range(Y_STEP):
            x = step * Y_STEP + k
            flipped = grid_ref[pl.ds(pl.multiple_of(x * 128, 128), 128), :].T
            parts.append(jnp.concatenate([flipped[:half], flipped[half:]], axis=1))
        res = dot(lanes3(jnp.concatenate(parts, axis=0)), ty_ref[...])
        for k in range(Y_STEP):
            for pair in range(2):
                to = pl.ds(pair * HALF + (step * Y_STEP + k) * PITCH, 32)
                at = k * half + pair * 32
                re_ref[to, :] = res[at:at + 32, :128]
                im_ref[to, :] = res[at:at + 32, 128:]
        for store in stores(step):
            store.start()

    @pl.loop(0, 128 // Y_STEP)
    def _(step):
        for store in stores(step):
            store.wait()


def lattice(sticks, stick_pos, cs):
    hbm = pl.BlockSpec(memory_space=pltpu.HBM)
    size = (2 * HALF, 128)
    return pl.pallas_call(
        lattice_kernel,
        out_shape=[jax.ShapeDtypeStruct(size, F32)] * 2,
        in_specs=[hbm] * 3,
        out_specs=[hbm] * 2,
        scratch_shapes=[
            pltpu.SMEM(stick_pos.shape, jnp.int32),
            pltpu.VMEM(sticks.shape, F32),
            pltpu.VMEM(cs.shape, BF16),
            pltpu.VMEM((768, 256), BF16),
            pltpu.VMEM((16384, 128), F32),
            pltpu.VMEM(size, F32),
            pltpu.VMEM(size, F32),
            pltpu.SemaphoreType.DMA((3,)),
            pltpu.SemaphoreType.DMA((2, 2, 128 // Y_STEP)),
        ],
        compiler_params=pltpu.CompilerParams(vmem_limit_bytes=LIMIT),
        name="lattice",
    )(stick_pos, sticks, cs)


def x_transforms(pair, pot_ref, ax_ref, bx_ref, re_ref, im_ref):
    @pl.loop(0, 16, unroll=16)
    def _(z):
        pot = pot_ref[z]
        wide = jnp.concatenate([pot] * 2, axis=1)
        wide = jnp.concatenate([wide] * 2, axis=0)
        at = [pl.ds(pair * HALF + k * 16 + z, 128, PITCH) for k in range(2)]
        data = jnp.concatenate(
            [jnp.concatenate([re_ref[a, :], im_ref[a, :]], axis=0) for a in at], axis=1)
        field = dot(ax_ref[...], rows3(data))
        back = dot(bx_ref[...], rows3(field * wide))
        for k in range(2):
            re_ref[at[k], :] = back[:128, k * 128:(k + 1) * 128]
            im_ref[at[k], :] = back[128:, k * 128:(k + 1) * 128]


def y_transform_back(bx_ref, re_ref, im_ref, grid_ref):
    half = 64

    @pl.loop(0, 128 // Y_STEP, unroll=4)
    def _(step):
        data = jnp.concatenate(
            [jnp.concatenate([ref[pl.ds(pair * HALF + (step * Y_STEP + k) * PITCH, 32), :]
                              for k in range(Y_STEP) for pair in range(2)], axis=0)
             for ref in (re_ref, im_ref)], axis=1)
        res = dot_nt(bx_ref[...], lanes3(data))
        for k in range(Y_STEP):
            to = pl.ds(pl.multiple_of((step * Y_STEP + k) * 128, 128), 128)
            grid_ref[to, :] = jnp.concatenate(
                [res[:128, k * half:(k + 1) * half], res[128:, k * half:(k + 1) * half]], axis=1)


COLUMNS = 1024
DEPTH = 2


def rotate_kernel(coef_hbm, image_hbm, applied_hbm, ritz_hbm, base_hbm, out_hbm, copy_hbm,
                  coef_ref, image_ref, ritz_ref, slab_ref, left_ref, small_sem, ritz_sem, in_sem, out_sem):
    steps = slab_ref.shape[2] // COLUMNS

    def at(step):
        return pl.ds(pl.multiple_of(step * COLUMNS, COLUMNS), COLUMNS)

    def load_ritz(step):
        return pltpu.make_async_copy(ritz_hbm.at[:, :, at(step)], ritz_ref.at[:, :, at(step)], ritz_sem.at[step])

    def load(step):
        return pltpu.make_async_copy(base_hbm.at[:, :, at(step)], slab_ref.at[:, :, at(step)], in_sem.at[step])

    def store(step):
        return pltpu.make_async_copy(slab_ref.at[:, :, at(step)], out_hbm.at[:, :, at(step)], out_sem.at[step])

    pairs = [(coef_hbm, coef_ref), (image_hbm, image_ref), (applied_hbm, copy_hbm)]
    small = [pltpu.make_async_copy(src, dst, small_sem.at[k]) for k, (src, dst) in enumerate(pairs)]
    small[0].start()
    small[1].start()
    for step in range(DEPTH):
        load_ritz(step).start()
        load(step).start()
    small[2].start()
    small[0].wait()
    small[1].wait()
    for part in range(2):
        for slot in range(4):
            rows = jnp.concatenate(
                [ref[(y * 4 + z) * 2 + core, slot, part * 4:part * 4 + 4, :]
                 for y in range(2) for core in range(2) for z in range(4) for ref in (coef_ref, image_ref)],
                axis=0).T
            high, low = split(rows)
            to = (part * 4 + slot) * 128
            left_ref[to:to + 128, :] = jnp.concatenate([high, low, high, low], axis=1)

    @pl.loop(0, steps)
    def _(step):
        load_ritz(step).wait()
        high, low = split(jnp.concatenate([ritz_ref[k, :, at(step)] for k in range(ritz_ref.shape[0])], axis=0))
        right = jnp.concatenate([high, high, low, low], axis=0)
        load(step).wait()

        @pl.when(step + DEPTH < steps)
        def _():
            load_ritz(step + DEPTH).start()
            load(step + DEPTH).start()

        for part in range(2):
            res = dot(left_ref[part * 512:(part + 1) * 512, :], right)
            slab_ref[part, :, at(step)] = (slab_ref[part, :, at(step)].astype(F32) + res).astype(BF16)
        store(step).start()

    @pl.loop(0, steps)
    def _(step):
        store(step).wait()

    small[2].wait()


def rotate(coef, image, ritz, base, applied):
    hbm = pl.BlockSpec(memory_space=pltpu.HBM)
    dma = pltpu.SemaphoreType.DMA
    steps = base.shape[2] // COLUMNS
    return pl.pallas_call(
        rotate_kernel,
        out_shape=[jax.ShapeDtypeStruct(base.shape, BF16), jax.ShapeDtypeStruct(applied.shape, F32)],
        in_specs=[hbm] * 5,
        out_specs=[hbm] * 2,
        scratch_shapes=[pltpu.VMEM(coef.shape, F32), pltpu.VMEM(image.shape, F32), pltpu.VMEM(ritz.shape, F32),
                        pltpu.VMEM(base.shape, BF16), pltpu.VMEM((1024, 512), BF16),
                        dma((3,)), dma((steps,)), dma((steps,)), dma((steps,))],
        compiler_params=pltpu.CompilerParams(vmem_limit_bytes=LIMIT),
        name="rotate",
    )(coef, image, applied, ritz, base)


def greet(axis, size, me):
    barrier = pltpu.get_barrier_semaphore()
    for step in range(1, size):
        pl.semaphore_signal(barrier, inc=1, device_id={axis: lax.rem(me + step, size)}, device_id_type=MESH)
    return barrier


class Exchange:
    def __init__(self, axis, size, me, source, target, send_sem, recv_sem, own_sem):
        self.axis, self.size, self.me = axis, size, me
        self.source, self.target = source, target
        self.send_sem, self.recv_sem, self.own_sem = send_sem, recv_sem, own_sem

    def remote(self, step):
        peer = lax.rem(self.me + step, self.size)
        return pltpu.make_async_remote_copy(
            src_ref=self.source.at[peer], dst_ref=self.target.at[self.me],
            send_sem=self.send_sem.at[peer], recv_sem=self.recv_sem.at[self.me],
            device_id={self.axis: peer}, device_id_type=MESH)

    def own(self):
        return pltpu.make_async_copy(self.source.at[self.me], self.target.at[self.me], self.own_sem)

    def start(self, prepare=None):
        for step in range(1, self.size + 1):
            if prepare is not None:
                prepare(lax.rem(self.me + step, self.size))
            if step < self.size:
                self.remote(step).start()
            else:
                self.own().start()

    def wait_recv(self):
        self.own().wait()
        for step in range(1, self.size):
            peer = lax.rem(self.me + step, self.size)
            pltpu.make_async_remote_copy(
                src_ref=self.source.at[peer], dst_ref=self.target.at[peer],
                send_sem=self.send_sem.at[peer], recv_sem=self.recv_sem.at[peer],
                device_id={self.axis: peer}, device_id_type=MESH).wait_recv()

    def wait_send(self):
        for step in range(1, self.size):
            self.remote(step).wait_send()


def pack_rows(flat_ref, pack_ref, n_pool):
    for k in range(n_pool):
        for j in range(4):
            pack_ref[k, j] = flat_ref[pl.ds(k * 4 + j, 8, 64), :]


def pool_parts(pool):
    return pool // 8, lax.rem(pool // 2, 4), lax.rem(pool, 2)


def pool_index(y, z, core):
    return (y * 4 + z) * 2 + core


def remote(src, dst, send, recv, **peer):
    return pltpu.make_async_remote_copy(src_ref=src, dst_ref=dst, send_sem=send, recv_sem=recv,
                                        device_id=peer, device_id_type=MESH)


def spread_kernel(n_tg, n_pool, wave_hbm, count_hbm, ritz_hbm, planes_ref, pack_ref, usable_ref, cs_ref, col_hbm,
                  wave_ref, count_ref, table_ref, flat_ref, sticks_ref, send_t, recv_t, own_sem, load_sem,
                  send_r, recv_r):
    tg, pool = lax.axis_index("tg"), lax.axis_index("pool")
    y, z, core = pool_parts(pool)
    after, before = lax.rem(z + 1, 4), lax.rem(z + 3, 4)
    up, down = pool_index(y, after, core), pool_index(y, before, core)
    pairs = [(count_hbm, count_ref), (wave_hbm, wave_ref), (ritz_hbm, col_hbm.at[z])]
    loads = [pltpu.make_async_copy(src, dst, load_sem.at[k]) for k, (src, dst) in enumerate(pairs)]
    for load in loads:
        load.start()
    barrier = greet("tg", n_tg, tg)
    for peer in (up, down):
        pl.semaphore_signal(barrier, inc=1, device_id={"pool": peer}, device_id_type=MESH)
    cs = cos_sin()
    for k in range(4):
        cs_ref[k] = cs[k]
    table_ref[...] = as_rhs_rows(cs, 1)
    loads[0].wait()
    loads[1].wait()
    pl.semaphore_wait(barrier, n_tg + 1)
    rise = remote(ritz_hbm, col_hbm.at[z], send_r.at[0], recv_r.at[0], pool=up)
    fall = remote(ritz_hbm, col_hbm.at[z], send_r.at[1], recv_r.at[1], pool=down)
    rise.start()
    fall.start()
    slot = lax.broadcasted_iota(jnp.int32, (64, 128), 0)
    usable = jnp.where(slot < count_ref[tg], 1.0, 0.0).astype(F32)
    usable_ref[...] = usable
    rows = []
    for band in range(4):
        pair = [wave_ref[part, band] * usable for part in range(2)]
        for part in range(2):
            flat_ref[(part * 4 + band) * 64:(part * 4 + band + 1) * 64, :] = pair[part]
        rows.append(jnp.concatenate(pair, axis=1))
    res = dot(lanes3(jnp.concatenate(rows, axis=0)), table_ref[...])
    for t in range(n_tg):
        sticks_ref[t] = jnp.concatenate(
            [res[band * 64:(band + 1) * 64, part * 128 + t * 16:part * 128 + t * 16 + 16]
             for part in range(2) for band in range(4)], axis=1)
    planes = Exchange("tg", n_tg, tg, sticks_ref, planes_ref, send_t, recv_t, own_sem.at[0])
    planes.start()
    pack_rows(flat_ref, pack_ref, n_pool)
    planes.wait_recv()
    remote(ritz_hbm, col_hbm.at[before], send_r.at[0], recv_r.at[0], pool=up).wait_recv()
    remote(ritz_hbm, col_hbm.at[after], send_r.at[1], recv_r.at[1], pool=down).wait_recv()
    loads[2].wait()
    planes.wait_send()
    rise.wait_send()
    fall.wait_send()


def collect_kernel(n_tg, n_pool, pos_hbm, re_hbm, im_hbm, pot_hbm, usable_hbm, cs_hbm, pack_hbm, col_hbm,
                   applied_ref, image_ref, coef_ref, ritz_ref,
                   pos_ref, re_ref, im_ref, pot_ref, usable_ref, cs_ref,
                   ax_ref, bx_ref, table_ref, grid_ref, cols_ref, returned_ref, pack_ref,
                   send_t, recv_t, send_p, recv_p, send_c, recv_c, own_sem, load_sem, send_r, recv_r):
    tg, pool = lax.axis_index("tg"), lax.axis_index("pool")
    y, z, core = pool_parts(pool)
    after, before, across = lax.rem(z + 1, 4), lax.rem(z + 3, 4), lax.rem(z + 2, 4)
    up, down = pool_index(y, after, core), pool_index(y, before, core)
    next_core, next_y = pool_index(y, z, 1 - core), pool_index(1 - y, z, core)
    own, other = ritz_ref.at[y, core], ritz_ref.at[1 - y, core]
    halves = [(src.at[pl.ds(pair * HALF, HALF), :], dst.at[pl.ds(pair * HALF, HALF), :])
              for pair in range(2) for src, dst in ((re_hbm, re_ref), (im_hbm, im_ref))]
    pairs = [(cs_hbm, cs_ref), (pot_hbm, pot_ref)] + halves + [
        (usable_hbm, usable_ref), (pos_hbm, pos_ref)] + [(col_hbm.at[k], own.at[k]) for k in (z, before, after)]
    loads = [pltpu.make_async_copy(src, dst, load_sem.at[k]) for k, (src, dst) in enumerate(pairs)]
    later = loads[4:6]
    for load in loads[:4] + loads[6:]:
        load.start()
    barrier = greet("tg", n_tg, tg)
    greet("pool", n_pool, pool)
    loads[0].wait()
    cs = [cs_ref[k] for k in range(4)]
    ax_ref[...] = as_lhs(cs, 1) * (1.0 / 128.0 ** 3)
    bx_ref[...] = as_lhs(cs, -1)
    table_ref[...] = as_rhs_rows(cs, -1)
    pl.semaphore_wait(barrier, n_tg + n_pool - 2)

    def ritz(k, src, dst, peer):
        return remote(src, dst, send_r.at[k], recv_r.at[k], pool=peer)

    sent = [ritz(0, col_hbm.at[before, 0], own.at[before, 0], up),
            ritz(1, col_hbm.at[after, 1], own.at[after, 1], down)]
    for k, block in enumerate((z, before, after)):
        sent += [ritz(2 + k, col_hbm.at[block], own.at[block], next_y),
                 ritz(6 + k, col_hbm.at[block], own.at[block], next_core)]
    for copy in sent:
        copy.start()
    for load in loads[1:4]:
        load.wait()
    for load in later:
        load.start()
    x_transforms(0, pot_ref, ax_ref, bx_ref, re_ref, im_ref)
    ritz(0, own.at[across, 0], own.at[across, 0], up).wait_recv()
    ritz(1, own.at[across, 1], own.at[across, 1], down).wait_recv()
    stage = [ritz(5, own.at[across], own.at[across], next_y), ritz(9, own.at[across], own.at[across], next_core)]
    for copy in stage:
        copy.start()
    sent += stage
    for load in later:
        load.wait()
    x_transforms(1, pot_ref, ax_ref, bx_ref, re_ref, im_ref)
    y_transform_back(bx_ref, re_ref, im_ref, grid_ref)
    coef = Exchange("pool", n_pool, pool, pack_hbm, coef_ref, send_c, recv_c, own_sem.at[2])
    coef.start()
    for k, block in enumerate((z, before, after, across)):
        ritz(2 + k, other.at[block], other.at[block], next_y).wait_recv()
    on_core = ritz(10, other, other, next_core)
    on_core.start()
    sent.append(on_core)
    loads[6].wait()
    loads[7].wait()

    def gather(peer):
        @pl.loop(0, 8)
        def _(block):
            base = pl.multiple_of(block * 8, 8)
            cols_ref[peer, pl.ds(base, 8), :] = jnp.concatenate(
                [grid_ref[pl.ds(pos_ref[peer * 64 + base + k], 1), :] for k in range(8)], axis=0)

    back = Exchange("tg", n_tg, tg, cols_ref, returned_ref, send_t, recv_t, own_sem.at[0])
    back.start(gather)
    usable = usable_ref[...]
    back.wait_recv()
    rows = []
    for band in range(4):
        rows.append(jnp.concatenate(
            [returned_ref[t, :, part * 64 + band * 16:part * 64 + band * 16 + 16]
             for part in range(2) for t in range(n_tg)], axis=1))
    res = dot(lanes3(jnp.concatenate(rows, axis=0)), table_ref[...])
    for band in range(4):
        for part in range(2):
            at = (part * 4 + band) * 64
            applied_ref[at:at + 64, :] = res[band * 64:(band + 1) * 64, part * 128:(part + 1) * 128] * usable
    pack_rows(applied_ref, pack_ref, n_pool)
    image = Exchange("pool", n_pool, pool, pack_ref, image_ref, send_p, recv_p, own_sem.at[1])
    image.start()
    coef.wait_recv()
    for load in loads[8:]:
        load.wait()
    theirs = ritz_ref.at[y, 1 - core]
    for k, block in enumerate((z, before, after, across)):
        ritz(6 + k, own.at[block], theirs.at[block], next_core).wait_recv()
    ritz(10, other, ritz_ref.at[1 - y, 1 - core], next_core).wait_recv()
    image.wait_recv()
    for exchange in (back, coef, image):
        exchange.wait_send()
    for copy in sent:
        copy.wait_send()


def spread(wave, count, ritz, n_tg, n_pool):
    vmem = pl.BlockSpec(memory_space=pltpu.VMEM)
    hbm = pl.BlockSpec(memory_space=pltpu.HBM)
    dma = pltpu.SemaphoreType.DMA
    return pl.pallas_call(
        functools.partial(spread_kernel, n_tg, n_pool),
        out_shape=[jax.ShapeDtypeStruct((n_tg, 64, 128), F32), jax.ShapeDtypeStruct((n_pool, 4, 8, 128), F32),
                   jax.ShapeDtypeStruct((64, 128), F32), jax.ShapeDtypeStruct((4, 128, 128), BF16),
                   jax.ShapeDtypeStruct((4,) + ritz.shape, F32)],
        in_specs=[hbm] * 3,
        out_specs=[vmem] * 4 + [hbm],
        scratch_shapes=[pltpu.VMEM(wave.shape, F32), pltpu.SMEM(count.shape, jnp.int32),
                        pltpu.VMEM((768, 256), BF16), pltpu.VMEM((512, 128), F32),
                        pltpu.VMEM((n_tg, 64, 128), F32), dma((n_tg,)), dma((n_tg,)), dma((1,)), dma((3,)),
                        dma((2,)), dma((2,))],
        compiler_params=pltpu.CompilerParams(collective_id=0, has_side_effects=True, vmem_limit_bytes=LIMIT),
        name="spread",
    )(wave, count, ritz)


def collect(stick_pos, re, im, pot, usable, cs, pack, col, n_tg, n_pool):
    vmem = pl.BlockSpec(memory_space=pltpu.VMEM)
    hbm = pl.BlockSpec(memory_space=pltpu.HBM)
    dma = pltpu.SemaphoreType.DMA
    return pl.pallas_call(
        functools.partial(collect_kernel, n_tg, n_pool),
        out_shape=[jax.ShapeDtypeStruct((512, 128), F32), jax.ShapeDtypeStruct(pack.shape, F32),
                   jax.ShapeDtypeStruct(pack.shape, F32), jax.ShapeDtypeStruct((2, 2) + col.shape, F32)],
        in_specs=[hbm] * 8,
        out_specs=[vmem, hbm, hbm, hbm],
        scratch_shapes=[pltpu.SMEM(stick_pos.shape, jnp.int32), pltpu.VMEM(re.shape, F32), pltpu.VMEM(im.shape, F32),
                        pltpu.VMEM(pot.shape, F32), pltpu.VMEM(usable.shape, F32), pltpu.VMEM(cs.shape, BF16),
                        pltpu.VMEM((256, 768), BF16), pltpu.VMEM((256, 768), BF16), pltpu.VMEM((768, 256), BF16),
                        pltpu.VMEM((16384, 128), F32), pltpu.VMEM((n_tg, 64, 128), F32),
                        pltpu.VMEM((n_tg, 64, 128), F32), pltpu.VMEM(pack.shape, F32),
                        dma((n_tg,)), dma((n_tg,)), dma((n_pool,)), dma((n_pool,)), dma((n_pool,)), dma((n_pool,)),
                        dma((3,)), dma((11,)), dma((11,)), dma((11,))],
        compiler_params=pltpu.CompilerParams(collective_id=1, has_side_effects=True, vmem_limit_bytes=LIMIT),
        name="collect",
    )(stick_pos, re, im, pot, usable, cs, pack, col)


def local(wave_coef, potential, stick_pos, stick_count, ritz_block, slab_base):
    n_tg, n_pool = lax.axis_size("tg"), lax.axis_size("pool")
    slots = wave_coef.shape[2]
    planes, pack, usable, cs, col = spread(wave_coef, stick_count, ritz_block, n_tg, n_pool)
    re, im = lattice(planes.reshape(n_tg * slots, 128), stick_pos, cs)
    applied, image, coef, ritz = collect(stick_pos, re, im, potential, usable, cs, pack, col, n_tg, n_pool)
    ritz = ritz.reshape((2 * n_pool,) + ritz_block.shape[1:])
    rotated, applied = rotate(coef, image, ritz, slab_base, applied)
    return applied.reshape(wave_coef.shape), rotated


def solution(mesh):
    in_specs = (
        P(None, "pool", "tg", None),
        P("tg", None, None),
        P(),
        P(),
        P(None, "pool", None),
        P(None, ("tg", "pool"), None),
    )
    out_specs = (P(None, "pool", "tg", None), P(None, ("tg", "pool"), None))
    return jax.shard_map(local, mesh=mesh, in_specs=in_specs, out_specs=out_specs, check_vma=False)
```

```python
import functools
import math

import jax
import jax.numpy as jnp
from jax import lax
from jax.experimental import pallas as pl
from jax.experimental.pallas import tpu as pltpu
from jax.sharding import PartitionSpec as P

NX = 128
NY = 128
BF16 = jnp.bfloat16
F32 = jnp.float32
MESH = pl.DeviceIdType.MESH


def cos_sin():
    row = lax.broadcasted_iota(jnp.int32, (128, 128), 0)
    col = lax.broadcasted_iota(jnp.int32, (128, 128), 1)
    angle = ((row * col) & 127).astype(F32) * (2.0 * math.pi / 128)
    return split(jnp.cos(angle)) + split(jnp.sin(angle))


def row_table(cos_t, sin_t, sign):
    plus = sin_t if sign > 0 else -sin_t
    return jnp.concatenate([jnp.concatenate([cos_t, plus], axis=1),
                            jnp.concatenate([-plus, cos_t], axis=1)], axis=0)


def table_pieces(cs, sign):
    return row_table(cs[0], cs[2], sign), row_table(cs[1], cs[3], sign)


def split(values):
    high = values.astype(BF16)
    low = (values - high.astype(F32)).astype(BF16)
    return high, low


def as_rhs_rows(cs, sign):
    high, low = table_pieces(cs, sign)
    return jnp.concatenate([high, high, low], axis=0)


def as_lhs(cs, sign):
    high, low = table_pieces(cs, -sign)
    return jnp.concatenate([high, high, low], axis=1)


def lanes3(values):
    high, low = split(values)
    return jnp.concatenate([high, low, high], axis=1)


def rows3(values):
    high, low = split(values)
    return jnp.concatenate([high, low, high], axis=0)


def dot(a, b):
    return lax.dot_general(a, b, (((1,), (0,)), ((), ())), preferred_element_type=F32)


def dot_nt(a, b):
    return lax.dot_general(a, b, (((1,), (1,)), ((), ())), preferred_element_type=F32)


PITCH = 33
HALF = 128 * PITCH
LIMIT = 60 * 2**20
Y_STEP = 16


def chunk(ref, pair, step):
    rows = Y_STEP * PITCH
    return ref.at[pl.ds(pl.multiple_of(pair * HALF + step * rows, 8), rows), :]


def lattice_kernel(pos_hbm, sticks_hbm, cs_hbm, re_hbm, im_hbm,
                   pos_ref, sticks_ref, cs_ref, ty_ref, grid_ref, re_ref, im_ref, sems, out_sems):
    slots = sticks_ref.shape[0]
    half = 64
    pairs = [(pos_hbm, pos_ref), (sticks_hbm, sticks_ref), (cs_hbm, cs_ref)]
    copies = [pltpu.make_async_copy(src, dst, sems.at[k]) for k, (src, dst) in enumerate(pairs)]
    for copy in copies:
        copy.start()

    @pl.loop(0, 32)
    def _(x):
        grid_ref[pl.ds(pl.multiple_of(x * 512, 512), 512), :] = jnp.zeros((512, 128), F32)

    copies[2].wait()
    ty_ref[...] = as_rhs_rows([cs_ref[k] for k in range(4)], 1)
    copies[0].wait()
    copies[1].wait()

    @pl.loop(0, slots // 8)
    def _(block):
        base = pl.multiple_of(block * 8, 8)
        rows = sticks_ref[pl.ds(base, 8), :]
        for k in range(8):
            grid_ref[pl.ds(pos_ref[base + k], 1), :] = rows[k:k + 1, :]

    def stores(step):
        return [pltpu.make_async_copy(chunk(src, pair, step), chunk(dst, pair, step), out_sems.at[k, pair, step])
                for pair in range(2) for k, (src, dst) in enumerate([(re_ref, re_hbm), (im_ref, im_hbm)])]

    @pl.loop(0, 128 // Y_STEP, unroll=8)
    def _(step):
        parts = []
        for k in range(Y_STEP):
            x = step * Y_STEP + k
            flipped = grid_ref[pl.ds(pl.multiple_of(x * 128, 128), 128), :].T
            parts.append(jnp.concatenate([flipped[:half], flipped[half:]], axis=1))
        res = dot(lanes3(jnp.concatenate(parts, axis=0)), ty_ref[...])
        for k in range(Y_STEP):
            for pair in range(2):
                to = pl.ds(pair * HALF + (step * Y_STEP + k) * PITCH, 32)
                at = k * half + pair * 32
                re_ref[to, :] = res[at:at + 32, :128]
                im_ref[to, :] = res[at:at + 32, 128:]
        for store in stores(step):
            store.start()

    @pl.loop(0, 128 // Y_STEP)
    def _(step):
        for store in stores(step):
            store.wait()


def lattice(sticks, stick_pos, cs):
    hbm = pl.BlockSpec(memory_space=pltpu.HBM)
    size = (2 * HALF, 128)
    return pl.pallas_call(
        lattice_kernel,
        out_shape=[jax.ShapeDtypeStruct(size, F32)] * 2,
        in_specs=[hbm] * 3,
        out_specs=[hbm] * 2,
        scratch_shapes=[
            pltpu.SMEM(stick_pos.shape, jnp.int32),
            pltpu.VMEM(sticks.shape, F32),
            pltpu.VMEM(cs.shape, BF16),
            pltpu.VMEM((768, 256), BF16),
            pltpu.VMEM((16384, 128), F32),
            pltpu.VMEM(size, F32),
            pltpu.VMEM(size, F32),
            pltpu.SemaphoreType.DMA((3,)),
            pltpu.SemaphoreType.DMA((2, 2, 128 // Y_STEP)),
        ],
        compiler_params=pltpu.CompilerParams(vmem_limit_bytes=LIMIT),
        name="lattice",
    )(stick_pos, sticks, cs)


def x_transforms(pair, pot_ref, ax_ref, bx_ref, re_ref, im_ref):
    @pl.loop(0, 16, unroll=16)
    def _(z):
        pot = pot_ref[z]
        wide = jnp.concatenate([pot] * 2, axis=1)
        wide = jnp.concatenate([wide] * 2, axis=0)
        at = [pl.ds(pair * HALF + k * 16 + z, 128, PITCH) for k in range(2)]
        data = jnp.concatenate(
            [jnp.concatenate([re_ref[a, :], im_ref[a, :]], axis=0) for a in at], axis=1)
        field = dot(ax_ref[...], rows3(data))
        back = dot(bx_ref[...], rows3(field * wide))
        for k in range(2):
            re_ref[at[k], :] = back[:128, k * 128:(k + 1) * 128]
            im_ref[at[k], :] = back[128:, k * 128:(k + 1) * 128]


def y_transform_back(bx_ref, re_ref, im_ref, grid_ref):
    half = 64

    @pl.loop(0, 128 // Y_STEP, unroll=4)
    def _(step):
        data = jnp.concatenate(
            [jnp.concatenate([ref[pl.ds(pair * HALF + (step * Y_STEP + k) * PITCH, 32), :]
                              for k in range(Y_STEP) for pair in range(2)], axis=0)
             for ref in (re_ref, im_ref)], axis=1)
        res = dot_nt(bx_ref[...], lanes3(data))
        for k in range(Y_STEP):
            to = pl.ds(pl.multiple_of((step * Y_STEP + k) * 128, 128), 128)
            grid_ref[to, :] = jnp.concatenate(
                [res[:128, k * half:(k + 1) * half], res[128:, k * half:(k + 1) * half]], axis=1)


COLUMNS = 1024
DEPTH = 2


def rotate_kernel(coef_hbm, image_hbm, applied_hbm, ritz_hbm, base_hbm, out_hbm, copy_hbm,
                  coef_ref, image_ref, ritz_ref, slab_ref, left_ref, small_sem, ritz_sem, in_sem, out_sem):
    steps = slab_ref.shape[2] // COLUMNS

    def at(step):
        return pl.ds(pl.multiple_of(step * COLUMNS, COLUMNS), COLUMNS)

    def load_ritz(step):
        return pltpu.make_async_copy(ritz_hbm.at[:, :, at(step)], ritz_ref.at[:, :, at(step)], ritz_sem.at[step])

    def load(step):
        return pltpu.make_async_copy(base_hbm.at[:, :, at(step)], slab_ref.at[:, :, at(step)], in_sem.at[step])

    def store(step):
        return pltpu.make_async_copy(slab_ref.at[:, :, at(step)], out_hbm.at[:, :, at(step)], out_sem.at[step])

    pairs = [(coef_hbm, coef_ref), (image_hbm, image_ref), (applied_hbm, copy_hbm)]
    small = [pltpu.make_async_copy(src, dst, small_sem.at[k]) for k, (src, dst) in enumerate(pairs)]
    small[0].start()
    small[1].start()
    for step in range(DEPTH):
        load_ritz(step).start()
        load(step).start()
    small[2].start()
    small[0].wait()
    small[1].wait()
    for part in range(2):
        for slot in range(4):
            rows = jnp.concatenate(
                [ref[(y * 4 + z) * 2 + core, slot, part * 4:part * 4 + 4, :]
                 for y in range(2) for core in range(2) for z in range(4) for ref in (coef_ref, image_ref)],
                axis=0).T
            high, low = split(rows)
            to = (part * 4 + slot) * 128
            left_ref[to:to + 128, :] = jnp.concatenate([high, low, high, low], axis=1)

    @pl.loop(0, steps)
    def _(step):
        load_ritz(step).wait()
        high, low = split(jnp.concatenate([ritz_ref[k, :, at(step)] for k in range(ritz_ref.shape[0])], axis=0))
        right = jnp.concatenate([high, high, low, low], axis=0)
        load(step).wait()

        @pl.when(step + DEPTH < steps)
        def _():
            load_ritz(step + DEPTH).start()
            load(step + DEPTH).start()

        for part in range(2):
            res = dot(left_ref[part * 512:(part + 1) * 512, :], right)
            slab_ref[part, :, at(step)] = (slab_ref[part, :, at(step)].astype(F32) + res).astype(BF16)
        store(step).start()

    @pl.loop(0, steps)
    def _(step):
        store(step).wait()

    small[2].wait()


def rotate(coef, image, ritz, base, applied):
    hbm = pl.BlockSpec(memory_space=pltpu.HBM)
    dma = pltpu.SemaphoreType.DMA
    steps = base.shape[2] // COLUMNS
    return pl.pallas_call(
        rotate_kernel,
        out_shape=[jax.ShapeDtypeStruct(base.shape, BF16), jax.ShapeDtypeStruct(applied.shape, F32)],
        in_specs=[hbm] * 5,
        out_specs=[hbm] * 2,
        scratch_shapes=[pltpu.VMEM(coef.shape, F32), pltpu.VMEM(image.shape, F32), pltpu.VMEM(ritz.shape, F32),
                        pltpu.VMEM(base.shape, BF16), pltpu.VMEM((1024, 512), BF16),
                        dma((3,)), dma((steps,)), dma((steps,)), dma((steps,))],
        compiler_params=pltpu.CompilerParams(vmem_limit_bytes=LIMIT),
        name="rotate",
    )(coef, image, applied, ritz, base)


def greet(axis, size, me):
    barrier = pltpu.get_barrier_semaphore()
    for step in range(1, size):
        pl.semaphore_signal(barrier, inc=1, device_id={axis: lax.rem(me + step, size)}, device_id_type=MESH)
    return barrier


class Exchange:
    def __init__(self, axis, size, me, source, target, send_sem, recv_sem, own_sem):
        self.axis, self.size, self.me = axis, size, me
        self.source, self.target = source, target
        self.send_sem, self.recv_sem, self.own_sem = send_sem, recv_sem, own_sem

    def remote(self, step):
        peer = lax.rem(self.me + step, self.size)
        return pltpu.make_async_remote_copy(
            src_ref=self.source.at[peer], dst_ref=self.target.at[self.me],
            send_sem=self.send_sem.at[peer], recv_sem=self.recv_sem.at[self.me],
            device_id={self.axis: peer}, device_id_type=MESH)

    def own(self):
        return pltpu.make_async_copy(self.source.at[self.me], self.target.at[self.me], self.own_sem)

    def start(self, prepare=None):
        for step in range(1, self.size + 1):
            if prepare is not None:
                prepare(lax.rem(self.me + step, self.size))
            if step < self.size:
                self.remote(step).start()
            else:
                self.own().start()

    def wait_recv(self):
        self.own().wait()
        for step in range(1, self.size):
            peer = lax.rem(self.me + step, self.size)
            pltpu.make_async_remote_copy(
                src_ref=self.source.at[peer], dst_ref=self.target.at[peer],
                send_sem=self.send_sem.at[peer], recv_sem=self.recv_sem.at[peer],
                device_id={self.axis: peer}, device_id_type=MESH).wait_recv()

    def wait_send(self):
        for step in range(1, self.size):
            self.remote(step).wait_send()


def pack_rows(flat_ref, pack_ref, owners):
    for k in owners:
        for j in range(4):
            pack_ref[k, j] = flat_ref[pl.ds(k * 4 + j, 8, 64), :]


def pool_parts(pool):
    return pool // 8, lax.rem(pool // 2, 4), lax.rem(pool, 2)


def pool_index(y, z, core):
    return (y * 4 + z) * 2 + core


def remote(src, dst, send, recv, **peer):
    return pltpu.make_async_remote_copy(src_ref=src, dst_ref=dst, send_sem=send, recv_sem=recv,
                                        device_id=peer, device_id_type=MESH)


def spread_kernel(n_tg, n_pool, wave_hbm, count_hbm, ritz_hbm, planes_ref, pack_ref, usable_ref, cs_ref, col_hbm,
                  wave_ref, count_ref, table_ref, flat_ref, sticks_ref, send_t, recv_t, own_sem, load_sem,
                  send_r, recv_r):
    tg, pool = lax.axis_index("tg"), lax.axis_index("pool")
    y, z, core = pool_parts(pool)
    after, before = lax.rem(z + 1, 4), lax.rem(z + 3, 4)
    up, down = pool_index(y, after, core), pool_index(y, before, core)
    pairs = [(count_hbm, count_ref), (wave_hbm, wave_ref), (ritz_hbm, col_hbm.at[z])]
    loads = [pltpu.make_async_copy(src, dst, load_sem.at[k]) for k, (src, dst) in enumerate(pairs)]
    for load in loads:
        load.start()
    barrier = greet("tg", n_tg, tg)
    for peer in (up, down):
        pl.semaphore_signal(barrier, inc=1, device_id={"pool": peer}, device_id_type=MESH)
    cs = cos_sin()
    for k in range(4):
        cs_ref[k] = cs[k]
    table_ref[...] = as_rhs_rows(cs, 1)
    loads[0].wait()
    loads[1].wait()
    pl.semaphore_wait(barrier, n_tg + 1)
    rise = remote(ritz_hbm, col_hbm.at[z], send_r.at[0], recv_r.at[0], pool=up)
    fall = remote(ritz_hbm, col_hbm.at[z], send_r.at[1], recv_r.at[1], pool=down)
    rise.start()
    fall.start()
    slot = lax.broadcasted_iota(jnp.int32, (64, 128), 0)
    usable = jnp.where(slot < count_ref[tg], 1.0, 0.0).astype(F32)
    usable_ref[...] = usable
    rows = []
    for band in range(4):
        pair = [wave_ref[part, band] * usable for part in range(2)]
        for part in range(2):
            flat_ref[(part * 4 + band) * 64:(part * 4 + band + 1) * 64, :] = pair[part]
        rows.append(jnp.concatenate(pair, axis=1))
    res = dot(lanes3(jnp.concatenate(rows, axis=0)), table_ref[...])
    for t in range(n_tg):
        sticks_ref[t] = jnp.concatenate(
            [res[band * 64:(band + 1) * 64, part * 128 + t * 16:part * 128 + t * 16 + 16]
             for part in range(2) for band in range(4)], axis=1)
    planes = Exchange("tg", n_tg, tg, sticks_ref, planes_ref, send_t, recv_t, own_sem.at[0])
    planes.start()
    pack_rows(flat_ref, pack_ref, range(n_pool))
    planes.wait_recv()
    remote(ritz_hbm, col_hbm.at[before], send_r.at[0], recv_r.at[0], pool=up).wait_recv()
    remote(ritz_hbm, col_hbm.at[after], send_r.at[1], recv_r.at[1], pool=down).wait_recv()
    loads[2].wait()
    planes.wait_send()
    rise.wait_send()
    fall.wait_send()


def collect_kernel(n_tg, n_pool, pos_hbm, re_hbm, im_hbm, pot_hbm, usable_hbm, cs_hbm, pack_hbm, col_hbm,
                   applied_ref, image_ref, coef_ref, ritz_ref,
                   pos_ref, re_ref, im_ref, pot_ref, usable_ref, cs_ref,
                   ax_ref, bx_ref, table_ref, grid_ref, cols_ref, returned_ref, pack_ref,
                   send_t, recv_t, send_p, recv_p, send_c, recv_c, own_sem, load_sem, send_r, recv_r):
    tg, pool = lax.axis_index("tg"), lax.axis_index("pool")
    y, z, core = pool_parts(pool)
    after, before, across = lax.rem(z + 1, 4), lax.rem(z + 3, 4), lax.rem(z + 2, 4)
    up, down = pool_index(y, after, core), pool_index(y, before, core)
    next_core, next_y = pool_index(y, z, 1 - core), pool_index(1 - y, z, core)
    own, other = ritz_ref.at[y, core], ritz_ref.at[1 - y, core]
    halves = [(src.at[pl.ds(pair * HALF, HALF), :], dst.at[pl.ds(pair * HALF, HALF), :])
              for pair in range(2) for src, dst in ((re_hbm, re_ref), (im_hbm, im_ref))]
    pairs = [(cs_hbm, cs_ref), (pot_hbm, pot_ref)] + halves + [
        (usable_hbm, usable_ref), (pos_hbm, pos_ref)] + [(col_hbm.at[k], own.at[k]) for k in (z, before, after)]
    loads = [pltpu.make_async_copy(src, dst, load_sem.at[k]) for k, (src, dst) in enumerate(pairs)]
    later = loads[4:6]
    for load in loads[:4] + loads[6:]:
        load.start()
    barrier = greet("tg", n_tg, tg)
    greet("pool", n_pool, pool)
    loads[0].wait()
    cs = [cs_ref[k] for k in range(4)]
    ax_ref[...] = as_lhs(cs, 1) * (1.0 / 128.0 ** 3)
    bx_ref[...] = as_lhs(cs, -1)
    table_ref[...] = as_rhs_rows(cs, -1)
    pl.semaphore_wait(barrier, n_tg + n_pool - 2)

    def ritz(k, src, dst, peer):
        return remote(src, dst, send_r.at[k], recv_r.at[k], pool=peer)

    sent = [ritz(0, col_hbm.at[before, 0], own.at[before, 0], up),
            ritz(1, col_hbm.at[after, 1], own.at[after, 1], down)]
    for k, block in enumerate((z, before, after)):
        sent += [ritz(2 + k, col_hbm.at[block], own.at[block], next_y),
                 ritz(6 + k, col_hbm.at[block], own.at[block], next_core)]
    for copy in sent:
        copy.start()
    for load in loads[1:4]:
        load.wait()
    for load in later:
        load.start()
    x_transforms(0, pot_ref, ax_ref, bx_ref, re_ref, im_ref)
    ritz(0, own.at[across, 0], own.at[across, 0], up).wait_recv()
    ritz(1, own.at[across, 1], own.at[across, 1], down).wait_recv()
    stage = [ritz(5, own.at[across], own.at[across], next_y), ritz(9, own.at[across], own.at[across], next_core)]
    for copy in stage:
        copy.start()
    sent += stage
    for load in later:
        load.wait()
    x_transforms(1, pot_ref, ax_ref, bx_ref, re_ref, im_ref)
    y_transform_back(bx_ref, re_ref, im_ref, grid_ref)
    for k, block in enumerate((z, before, after, across)):
        ritz(2 + k, other.at[block], other.at[block], next_y).wait_recv()
    on_core = ritz(10, other, other, next_core)
    on_core.start()
    sent.append(on_core)
    loads[6].wait()
    loads[7].wait()

    backs = [Exchange("tg", n_tg, tg, cols_ref.at[half], returned_ref.at[half], send_t.at[half], recv_t.at[half],
                      own_sem.at[2 + half]) for half in range(2)]
    for half in range(2):
        def gather(peer):
            for block in range(4):
                first = peer * 64 + block // 2 * 32 + half * 16 + block % 2 * 8
                cols_ref[half, peer, block * 8:block * 8 + 8, :] = jnp.concatenate(
                    [grid_ref[pl.ds(pos_ref[first + k], 1), :] for k in range(8)], axis=0)

        backs[half].start(gather)
    coef = Exchange("pool", n_pool, pool, pack_hbm, coef_ref, send_c, recv_c, own_sem.at[0])
    coef.start()
    image = Exchange("pool", n_pool, pool, pack_ref, image_ref, send_p, recv_p, own_sem.at[1])
    for half in range(2):
        backs[half].wait_recv()
        rows = []
        for band in range(4):
            rows.append(jnp.concatenate(
                [returned_ref[half, t, :, part * 64 + band * 16:part * 64 + band * 16 + 16]
                 for part in range(2) for t in range(n_tg)], axis=1))
        res = dot(lanes3(jnp.concatenate(rows, axis=0)), table_ref[...])
        for high in range(2):
            slot = high * 32 + half * 16
            usable = usable_ref[slot:slot + 16, :]
            for band in range(4):
                for part in range(2):
                    at = (part * 4 + band) * 64 + slot
                    row = band * 32 + high * 16
                    applied_ref[at:at + 16, :] = res[row:row + 16, part * 128:(part + 1) * 128] * usable
        owners = [high * 8 + half * 4 + k for high in range(2) for k in range(4)]
        pack_rows(applied_ref, pack_ref, owners)
        for step in range(8):
            turn = lax.rem(pool + step, 8)
            owner = turn // 4 * 8 + half * 4 + lax.rem(turn, 4)

            @pl.when(owner != pool)
            def _():
                image.remote(lax.rem(owner + n_pool - pool, n_pool)).start()

            @pl.when(owner == pool)
            def _():
                image.own().start()

    coef.wait_recv()
    for load in loads[8:]:
        load.wait()
    theirs = ritz_ref.at[y, 1 - core]
    for k, block in enumerate((z, before, after, across)):
        ritz(6 + k, own.at[block], theirs.at[block], next_core).wait_recv()
    ritz(10, other, ritz_ref.at[1 - y, 1 - core], next_core).wait_recv()
    image.wait_recv()
    for exchange in backs + [coef, image]:
        exchange.wait_send()
    for copy in sent:
        copy.wait_send()


def spread(wave, count, ritz, n_tg, n_pool):
    vmem = pl.BlockSpec(memory_space=pltpu.VMEM)
    hbm = pl.BlockSpec(memory_space=pltpu.HBM)
    dma = pltpu.SemaphoreType.DMA
    return pl.pallas_call(
        functools.partial(spread_kernel, n_tg, n_pool),
        out_shape=[jax.ShapeDtypeStruct((n_tg, 64, 128), F32), jax.ShapeDtypeStruct((n_pool, 4, 8, 128), F32),
                   jax.ShapeDtypeStruct((64, 128), F32), jax.ShapeDtypeStruct((4, 128, 128), BF16),
                   jax.ShapeDtypeStruct((4,) + ritz.shape, F32)],
        in_specs=[hbm] * 3,
        out_specs=[vmem] * 4 + [hbm],
        scratch_shapes=[pltpu.VMEM(wave.shape, F32), pltpu.SMEM(count.shape, jnp.int32),
                        pltpu.VMEM((768, 256), BF16), pltpu.VMEM((512, 128), F32),
                        pltpu.VMEM((n_tg, 64, 128), F32), dma((n_tg,)), dma((n_tg,)), dma((1,)), dma((3,)),
                        dma((2,)), dma((2,))],
        compiler_params=pltpu.CompilerParams(collective_id=0, has_side_effects=True, vmem_limit_bytes=LIMIT),
        name="spread",
    )(wave, count, ritz)


def collect(stick_pos, re, im, pot, usable, cs, pack, col, n_tg, n_pool):
    vmem = pl.BlockSpec(memory_space=pltpu.VMEM)
    hbm = pl.BlockSpec(memory_space=pltpu.HBM)
    dma = pltpu.SemaphoreType.DMA
    return pl.pallas_call(
        functools.partial(collect_kernel, n_tg, n_pool),
        out_shape=[jax.ShapeDtypeStruct((512, 128), F32), jax.ShapeDtypeStruct(pack.shape, F32),
                   jax.ShapeDtypeStruct(pack.shape, F32), jax.ShapeDtypeStruct((2, 2) + col.shape, F32)],
        in_specs=[hbm] * 8,
        out_specs=[vmem, hbm, hbm, hbm],
        scratch_shapes=[pltpu.SMEM(stick_pos.shape, jnp.int32), pltpu.VMEM(re.shape, F32), pltpu.VMEM(im.shape, F32),
                        pltpu.VMEM(pot.shape, F32), pltpu.VMEM(usable.shape, F32), pltpu.VMEM(cs.shape, BF16),
                        pltpu.VMEM((256, 768), BF16), pltpu.VMEM((256, 768), BF16), pltpu.VMEM((768, 256), BF16),
                        pltpu.VMEM((16384, 128), F32), pltpu.VMEM((2, n_tg, 32, 128), F32),
                        pltpu.VMEM((2, n_tg, 32, 128), F32), pltpu.VMEM(pack.shape, F32),
                        dma((2, n_tg)), dma((2, n_tg)), dma((n_pool,)), dma((n_pool,)), dma((n_pool,)), dma((n_pool,)),
                        dma((4,)), dma((11,)), dma((11,)), dma((11,))],
        compiler_params=pltpu.CompilerParams(collective_id=1, has_side_effects=True, vmem_limit_bytes=LIMIT),
        name="collect",
    )(stick_pos, re, im, pot, usable, cs, pack, col)


def local(wave_coef, potential, stick_pos, stick_count, ritz_block, slab_base):
    n_tg, n_pool = lax.axis_size("tg"), lax.axis_size("pool")
    slots = wave_coef.shape[2]
    planes, pack, usable, cs, col = spread(wave_coef, stick_count, ritz_block, n_tg, n_pool)
    re, im = lattice(planes.reshape(n_tg * slots, 128), stick_pos, cs)
    applied, image, coef, ritz = collect(stick_pos, re, im, potential, usable, cs, pack, col, n_tg, n_pool)
    ritz = ritz.reshape((2 * n_pool,) + ritz_block.shape[1:])
    rotated, applied = rotate(coef, image, ritz, slab_base, applied)
    return applied.reshape(wave_coef.shape), rotated


def solution(mesh):
    in_specs = (
        P(None, "pool", "tg", None),
        P("tg", None, None),
        P(),
        P(),
        P(None, "pool", None),
        P(None, ("tg", "pool"), None),
    )
    out_specs = (P(None, "pool", "tg", None), P(None, ("tg", "pool"), None))
    return jax.shard_map(local, mesh=mesh, in_specs=in_specs, out_specs=out_specs, check_vma=False)
```

```python
import functools
import math

import jax
import jax.numpy as jnp
from jax import lax
from jax.experimental import pallas as pl
from jax.experimental.pallas import tpu as pltpu
from jax.sharding import PartitionSpec as P

NX = 128
NY = 128
BF16 = jnp.bfloat16
F32 = jnp.float32
MESH = pl.DeviceIdType.MESH


def cos_sin():
    row = lax.broadcasted_iota(jnp.int32, (128, 128), 0)
    col = lax.broadcasted_iota(jnp.int32, (128, 128), 1)
    angle = ((row * col) & 127).astype(F32) * (2.0 * math.pi / 128)
    return split(jnp.cos(angle)) + split(jnp.sin(angle))


def row_table(cos_t, sin_t, sign):
    plus = sin_t if sign > 0 else -sin_t
    return jnp.concatenate([jnp.concatenate([cos_t, plus], axis=1),
                            jnp.concatenate([-plus, cos_t], axis=1)], axis=0)


def table_pieces(cs, sign):
    return row_table(cs[0], cs[2], sign), row_table(cs[1], cs[3], sign)


def split(values):
    high = values.astype(BF16)
    low = (values - high.astype(F32)).astype(BF16)
    return high, low


def as_rhs_rows(cs, sign):
    high, low = table_pieces(cs, sign)
    return jnp.concatenate([high, high, low], axis=0)


def as_lhs(cs, sign):
    high, low = table_pieces(cs, -sign)
    return jnp.concatenate([high, high, low], axis=1)


def lanes3(values):
    high, low = split(values)
    return jnp.concatenate([high, low, high], axis=1)


def rows3(values):
    high, low = split(values)
    return jnp.concatenate([high, low, high], axis=0)


def dot(a, b):
    return lax.dot_general(a, b, (((1,), (0,)), ((), ())), preferred_element_type=F32)


def dot_nt(a, b):
    return lax.dot_general(a, b, (((1,), (1,)), ((), ())), preferred_element_type=F32)


PITCH = 33
HALF = 128 * PITCH
LIMIT = 60 * 2**20
Y_STEP = 16


def chunk(ref, pair, step):
    rows = Y_STEP * PITCH
    return ref.at[pl.ds(pl.multiple_of(pair * HALF + step * rows, 8), rows), :]


def lattice_kernel(pos_hbm, sticks_hbm, cs_hbm, re_hbm, im_hbm,
                   pos_ref, sticks_ref, cs_ref, ty_ref, grid_ref, re_ref, im_ref, sems, out_sems):
    slots = sticks_ref.shape[0]
    half = 64
    pairs = [(pos_hbm, pos_ref), (sticks_hbm, sticks_ref), (cs_hbm, cs_ref)]
    copies = [pltpu.make_async_copy(src, dst, sems.at[k]) for k, (src, dst) in enumerate(pairs)]
    for copy in copies:
        copy.start()

    @pl.loop(0, 32)
    def _(x):
        grid_ref[pl.ds(pl.multiple_of(x * 512, 512), 512), :] = jnp.zeros((512, 128), F32)

    copies[2].wait()
    ty_ref[...] = as_rhs_rows([cs_ref[k] for k in range(4)], 1)
    copies[0].wait()
    copies[1].wait()

    @pl.loop(0, slots // 8)
    def _(block):
        base = pl.multiple_of(block * 8, 8)
        rows = sticks_ref[pl.ds(base, 8), :]
        for k in range(8):
            grid_ref[pl.ds(pos_ref[base + k], 1), :] = rows[k:k + 1, :]

    def stores(step):
        return [pltpu.make_async_copy(chunk(src, pair, step), chunk(dst, pair, step), out_sems.at[k, pair, step])
                for pair in range(2) for k, (src, dst) in enumerate([(re_ref, re_hbm), (im_ref, im_hbm)])]

    @pl.loop(0, 128 // Y_STEP, unroll=8)
    def _(step):
        parts = []
        for k in range(Y_STEP):
            x = step * Y_STEP + k
            flipped = grid_ref[pl.ds(pl.multiple_of(x * 128, 128), 128), :].T
            parts.append(jnp.concatenate([flipped[:half], flipped[half:]], axis=1))
        res = dot(lanes3(jnp.concatenate(parts, axis=0)), ty_ref[...])
        for k in range(Y_STEP):
            for pair in range(2):
                to = pl.ds(pair * HALF + (step * Y_STEP + k) * PITCH, 32)
                at = k * half + pair * 32
                re_ref[to, :] = res[at:at + 32, :128]
                im_ref[to, :] = res[at:at + 32, 128:]
        for store in stores(step):
            store.start()

    @pl.loop(0, 128 // Y_STEP)
    def _(step):
        for store in stores(step):
            store.wait()


def lattice(sticks, stick_pos, cs):
    hbm = pl.BlockSpec(memory_space=pltpu.HBM)
    size = (2 * HALF, 128)
    return pl.pallas_call(
        lattice_kernel,
        out_shape=[jax.ShapeDtypeStruct(size, F32)] * 2,
        in_specs=[hbm] * 3,
        out_specs=[hbm] * 2,
        scratch_shapes=[
            pltpu.SMEM(stick_pos.shape, jnp.int32),
            pltpu.VMEM(sticks.shape, F32),
            pltpu.VMEM(cs.shape, BF16),
            pltpu.VMEM((768, 256), BF16),
            pltpu.VMEM((16384, 128), F32),
            pltpu.VMEM(size, F32),
            pltpu.VMEM(size, F32),
            pltpu.SemaphoreType.DMA((3,)),
            pltpu.SemaphoreType.DMA((2, 2, 128 // Y_STEP)),
        ],
        compiler_params=pltpu.CompilerParams(vmem_limit_bytes=LIMIT),
        name="lattice",
    )(stick_pos, sticks, cs)


def x_transforms(pair, pot_ref, ax_ref, bx_ref, re_ref, im_ref):
    @pl.loop(0, 16, unroll=16)
    def _(z):
        pot = pot_ref[z]
        wide = jnp.concatenate([pot] * 2, axis=1)
        wide = jnp.concatenate([wide] * 2, axis=0)
        at = [pl.ds(pair * HALF + k * 16 + z, 128, PITCH) for k in range(2)]
        data = jnp.concatenate(
            [jnp.concatenate([re_ref[a, :], im_ref[a, :]], axis=0) for a in at], axis=1)
        field = dot(ax_ref[...], rows3(data))
        back = dot(bx_ref[...], rows3(field * wide))
        for k in range(2):
            re_ref[at[k], :] = back[:128, k * 128:(k + 1) * 128]
            im_ref[at[k], :] = back[128:, k * 128:(k + 1) * 128]


def y_transform_back(bx_ref, re_ref, im_ref, grid_ref):
    half = 64

    @pl.loop(0, 128 // Y_STEP, unroll=4)
    def _(step):
        data = jnp.concatenate(
            [jnp.concatenate([ref[pl.ds(pair * HALF + (step * Y_STEP + k) * PITCH, 32), :]
                              for k in range(Y_STEP) for pair in range(2)], axis=0)
             for ref in (re_ref, im_ref)], axis=1)
        res = dot_nt(bx_ref[...], lanes3(data))
        for k in range(Y_STEP):
            to = pl.ds(pl.multiple_of((step * Y_STEP + k) * 128, 128), 128)
            grid_ref[to, :] = jnp.concatenate(
                [res[:128, k * half:(k + 1) * half], res[128:, k * half:(k + 1) * half]], axis=1)


COLUMNS = 1024
DEPTH = 2


def rotate_kernel(coef_hbm, image_hbm, applied_hbm, ritz_hbm, base_hbm, out_hbm, copy_hbm,
                  coef_ref, image_ref, ritz_ref, slab_ref, left_ref, small_sem, ritz_sem, in_sem, out_sem):
    steps = slab_ref.shape[2] // COLUMNS

    def at(step):
        return pl.ds(pl.multiple_of(step * COLUMNS, COLUMNS), COLUMNS)

    def load_ritz(step):
        return pltpu.make_async_copy(ritz_hbm.at[:, :, at(step)], ritz_ref.at[:, :, at(step)], ritz_sem.at[step])

    def load(step):
        return pltpu.make_async_copy(base_hbm.at[:, :, at(step)], slab_ref.at[:, :, at(step)], in_sem.at[step])

    def store(step):
        return pltpu.make_async_copy(slab_ref.at[:, :, at(step)], out_hbm.at[:, :, at(step)], out_sem.at[step])

    pairs = [(coef_hbm, coef_ref), (image_hbm, image_ref), (applied_hbm, copy_hbm)]
    small = [pltpu.make_async_copy(src, dst, small_sem.at[k]) for k, (src, dst) in enumerate(pairs)]
    small[0].start()
    small[1].start()
    for step in range(DEPTH):
        load_ritz(step).start()
        load(step).start()
    small[2].start()
    small[0].wait()
    small[1].wait()
    for part in range(2):
        for slot in range(4):
            rows = jnp.concatenate(
                [ref[(y * 4 + z) * 2 + core, slot, part * 4:part * 4 + 4, :]
                 for y in range(2) for core in range(2) for z in range(4) for ref in (coef_ref, image_ref)],
                axis=0).T
            high, low = split(rows)
            to = (part * 4 + slot) * 128
            left_ref[to:to + 128, :] = jnp.concatenate([high, low, high, low], axis=1)

    @pl.loop(0, steps)
    def _(step):
        load_ritz(step).wait()
        high, low = split(jnp.concatenate([ritz_ref[k, :, at(step)] for k in range(ritz_ref.shape[0])], axis=0))
        right = jnp.concatenate([high, high, low, low], axis=0)
        load(step).wait()

        @pl.when(step + DEPTH < steps)
        def _():
            load_ritz(step + DEPTH).start()
            load(step + DEPTH).start()

        for part in range(2):
            res = dot(left_ref[part * 512:(part + 1) * 512, :], right)
            slab_ref[part, :, at(step)] = (slab_ref[part, :, at(step)].astype(F32) + res).astype(BF16)
        store(step).start()

    @pl.loop(0, steps)
    def _(step):
        store(step).wait()

    small[2].wait()


def rotate(coef, image, ritz, base, applied):
    hbm = pl.BlockSpec(memory_space=pltpu.HBM)
    dma = pltpu.SemaphoreType.DMA
    steps = base.shape[2] // COLUMNS
    return pl.pallas_call(
        rotate_kernel,
        out_shape=[jax.ShapeDtypeStruct(base.shape, BF16), jax.ShapeDtypeStruct(applied.shape, F32)],
        in_specs=[hbm] * 5,
        out_specs=[hbm] * 2,
        scratch_shapes=[pltpu.VMEM(coef.shape, F32), pltpu.VMEM(image.shape, F32), pltpu.VMEM(ritz.shape, F32),
                        pltpu.VMEM(base.shape, BF16), pltpu.VMEM((1024, 512), BF16),
                        dma((3,)), dma((steps,)), dma((steps,)), dma((steps,))],
        compiler_params=pltpu.CompilerParams(vmem_limit_bytes=LIMIT),
        name="rotate",
    )(coef, image, applied, ritz, base)


def greet(axis, size, me):
    barrier = pltpu.get_barrier_semaphore()
    for step in range(1, size):
        pl.semaphore_signal(barrier, inc=1, device_id={axis: lax.rem(me + step, size)}, device_id_type=MESH)
    return barrier


class Exchange:
    def __init__(self, axis, size, me, source, target, send_sem, recv_sem, own_sem):
        self.axis, self.size, self.me = axis, size, me
        self.source, self.target = source, target
        self.send_sem, self.recv_sem, self.own_sem = send_sem, recv_sem, own_sem

    def remote(self, step):
        peer = lax.rem(self.me + step, self.size)
        return pltpu.make_async_remote_copy(
            src_ref=self.source.at[peer], dst_ref=self.target.at[self.me],
            send_sem=self.send_sem.at[peer], recv_sem=self.recv_sem.at[self.me],
            device_id={self.axis: peer}, device_id_type=MESH)

    def own(self):
        return pltpu.make_async_copy(self.source.at[self.me], self.target.at[self.me], self.own_sem)

    def start(self, prepare=None):
        for step in range(1, self.size + 1):
            if prepare is not None:
                prepare(lax.rem(self.me + step, self.size))
            if step < self.size:
                self.remote(step).start()
            else:
                self.own().start()

    def wait_recv(self):
        self.own().wait()
        for step in range(1, self.size):
            peer = lax.rem(self.me + step, self.size)
            pltpu.make_async_remote_copy(
                src_ref=self.source.at[peer], dst_ref=self.target.at[peer],
                send_sem=self.send_sem.at[peer], recv_sem=self.recv_sem.at[peer],
                device_id={self.axis: peer}, device_id_type=MESH).wait_recv()

    def wait_send(self):
        for step in range(1, self.size):
            self.remote(step).wait_send()


def pack_rows(flat_ref, pack_ref, owners):
    for k in owners:
        for j in range(4):
            pack_ref[k, j] = flat_ref[pl.ds(k * 4 + j, 8, 64), :]


def pool_parts(pool):
    return pool // 8, lax.rem(pool // 2, 4), lax.rem(pool, 2)


def pool_index(y, z, core):
    return (y * 4 + z) * 2 + core


def remote(src, dst, send, recv, **peer):
    return pltpu.make_async_remote_copy(src_ref=src, dst_ref=dst, send_sem=send, recv_sem=recv,
                                        device_id=peer, device_id_type=MESH)


def spread_kernel(n_tg, n_pool, wave_hbm, count_hbm, ritz_hbm, planes_ref, pack_ref, usable_ref, cs_ref, col_hbm,
                  wave_ref, count_ref, table_ref, flat_ref, sticks_ref, send_t, recv_t, own_sem, load_sem,
                  send_r, recv_r):
    tg, pool = lax.axis_index("tg"), lax.axis_index("pool")
    y, z, core = pool_parts(pool)
    after, before = lax.rem(z + 1, 4), lax.rem(z + 3, 4)
    up, down = pool_index(y, after, core), pool_index(y, before, core)
    pairs = [(count_hbm, count_ref), (wave_hbm, wave_ref), (ritz_hbm, col_hbm.at[z])]
    loads = [pltpu.make_async_copy(src, dst, load_sem.at[k]) for k, (src, dst) in enumerate(pairs)]
    for load in loads:
        load.start()
    barrier = greet("tg", n_tg, tg)
    for peer in (up, down):
        pl.semaphore_signal(barrier, inc=1, device_id={"pool": peer}, device_id_type=MESH)
    cs = cos_sin()
    for k in range(4):
        cs_ref[k] = cs[k]
    table_ref[...] = as_rhs_rows(cs, 1)
    loads[0].wait()
    loads[1].wait()
    pl.semaphore_wait(barrier, n_tg + 1)
    rise = remote(ritz_hbm, col_hbm.at[z], send_r.at[0], recv_r.at[0], pool=up)
    fall = remote(ritz_hbm, col_hbm.at[z], send_r.at[1], recv_r.at[1], pool=down)
    rise.start()
    fall.start()
    slot = lax.broadcasted_iota(jnp.int32, (64, 128), 0)
    usable = jnp.where(slot < count_ref[tg], 1.0, 0.0).astype(F32)
    usable_ref[...] = usable
    rows = []
    for band in range(4):
        pair = [wave_ref[part, band] * usable for part in range(2)]
        for part in range(2):
            flat_ref[(part * 4 + band) * 64:(part * 4 + band + 1) * 64, :] = pair[part]
        rows.append(jnp.concatenate(pair, axis=1))
    res = dot(lanes3(jnp.concatenate(rows, axis=0)), table_ref[...])
    for t in range(n_tg):
        sticks_ref[t] = jnp.concatenate(
            [res[band * 64:(band + 1) * 64, part * 128 + t * 16:part * 128 + t * 16 + 16]
             for part in range(2) for band in range(4)], axis=1)
    planes = Exchange("tg", n_tg, tg, sticks_ref, planes_ref, send_t, recv_t, own_sem.at[0])
    planes.start()
    pack_rows(flat_ref, pack_ref, range(n_pool))
    planes.wait_recv()
    remote(ritz_hbm, col_hbm.at[before], send_r.at[0], recv_r.at[0], pool=up).wait_recv()
    remote(ritz_hbm, col_hbm.at[after], send_r.at[1], recv_r.at[1], pool=down).wait_recv()
    loads[2].wait()
    planes.wait_send()
    rise.wait_send()
    fall.wait_send()


def collect_kernel(n_tg, n_pool, pos_hbm, re_hbm, im_hbm, pot_hbm, usable_hbm, cs_hbm, pack_hbm, col_hbm,
                   applied_ref, image_ref, coef_ref, ritz_ref,
                   pos_ref, re_ref, im_ref, pot_ref, usable_ref, cs_ref,
                   ax_ref, bx_ref, table_ref, grid_ref, cols_ref, returned_ref, pack_ref,
                   send_t, recv_t, send_p, recv_p, send_c, recv_c, own_sem, load_sem, send_r, recv_r):
    tg, pool = lax.axis_index("tg"), lax.axis_index("pool")
    y, z, core = pool_parts(pool)
    after, before, across = lax.rem(z + 1, 4), lax.rem(z + 3, 4), lax.rem(z + 2, 4)
    up, down = pool_index(y, after, core), pool_index(y, before, core)
    next_core, next_y = pool_index(y, z, 1 - core), pool_index(1 - y, z, core)
    own, other = ritz_ref.at[y, core], ritz_ref.at[1 - y, core]
    halves = [(src.at[pl.ds(pair * HALF, HALF), :], dst.at[pl.ds(pair * HALF, HALF), :])
              for pair in range(2) for src, dst in ((re_hbm, re_ref), (im_hbm, im_ref))]
    pairs = [(cs_hbm, cs_ref), (pot_hbm, pot_ref)] + halves + [
        (usable_hbm, usable_ref), (pos_hbm, pos_ref)] + [(col_hbm.at[k], own.at[k]) for k in (z, before, after)]
    loads = [pltpu.make_async_copy(src, dst, load_sem.at[k]) for k, (src, dst) in enumerate(pairs)]
    later = loads[4:6]
    for load in loads[:4] + loads[6:]:
        load.start()
    barrier = greet("tg", n_tg, tg)
    greet("pool", n_pool, pool)
    loads[0].wait()
    cs = [cs_ref[k] for k in range(4)]
    ax_ref[...] = as_lhs(cs, 1) * (1.0 / 128.0 ** 3)
    bx_ref[...] = as_lhs(cs, -1)
    table_ref[...] = as_rhs_rows(cs, -1)
    pl.semaphore_wait(barrier, n_tg + n_pool - 2)

    def ritz(k, src, dst, peer):
        return remote(src, dst, send_r.at[k], recv_r.at[k], pool=peer)

    sent = [ritz(0, col_hbm.at[before, 0], own.at[before, 0], up),
            ritz(1, col_hbm.at[after, 1], own.at[after, 1], down)]
    for k, block in enumerate((z, before, after)):
        sent += [ritz(2 + k, col_hbm.at[block], own.at[block], next_y),
                 ritz(6 + k, col_hbm.at[block], own.at[block], next_core)]
    for copy in sent:
        copy.start()
    for load in loads[1:4]:
        load.wait()
    for load in later:
        load.start()
    x_transforms(0, pot_ref, ax_ref, bx_ref, re_ref, im_ref)
    ritz(0, own.at[across, 0], own.at[across, 0], up).wait_recv()
    ritz(1, own.at[across, 1], own.at[across, 1], down).wait_recv()
    stage = [ritz(5, own.at[across], own.at[across], next_y), ritz(9, own.at[across], own.at[across], next_core)]
    for copy in stage:
        copy.start()
    sent += stage
    for load in later:
        load.wait()
    x_transforms(1, pot_ref, ax_ref, bx_ref, re_ref, im_ref)
    y_transform_back(bx_ref, re_ref, im_ref, grid_ref)
    loads[6].wait()
    loads[7].wait()

    backs = [Exchange("tg", n_tg, tg, cols_ref.at[half], returned_ref.at[half], send_t.at[half], recv_t.at[half],
                      own_sem.at[2 + half]) for half in range(2)]
    for half in range(2):
        def gather(peer):
            for block in range(4):
                first = peer * 64 + block // 2 * 32 + half * 16 + block % 2 * 8
                cols_ref[half, peer, block * 8:block * 8 + 8, :] = jnp.concatenate(
                    [grid_ref[pl.ds(pos_ref[first + k], 1), :] for k in range(8)], axis=0)

        backs[half].start(gather)
    coef = Exchange("pool", n_pool, pool, pack_hbm, coef_ref, send_c, recv_c, own_sem.at[0])
    coef.start()
    for k, block in enumerate((z, before, after, across)):
        ritz(2 + k, other.at[block], other.at[block], next_y).wait_recv()
    on_core = ritz(10, other, other, next_core)
    on_core.start()
    sent.append(on_core)
    image = Exchange("pool", n_pool, pool, pack_ref, image_ref, send_p, recv_p, own_sem.at[1])
    for half in range(2):
        backs[half].wait_recv()
        rows = []
        for band in range(4):
            rows.append(jnp.concatenate(
                [returned_ref[half, t, :, part * 64 + band * 16:part * 64 + band * 16 + 16]
                 for part in range(2) for t in range(n_tg)], axis=1))
        res = dot(lanes3(jnp.concatenate(rows, axis=0)), table_ref[...])
        for high in range(2):
            slot = high * 32 + half * 16
            usable = usable_ref[slot:slot + 16, :]
            for band in range(4):
                for part in range(2):
                    at = (part * 4 + band) * 64 + slot
                    row = band * 32 + high * 16
                    applied_ref[at:at + 16, :] = res[row:row + 16, part * 128:(part + 1) * 128] * usable
        owners = [high * 8 + half * 4 + k for high in range(2) for k in range(4)]
        pack_rows(applied_ref, pack_ref, owners)
        for step in range(8):
            turn = lax.rem(pool + step, 8)
            owner = turn // 4 * 8 + half * 4 + lax.rem(turn, 4)

            @pl.when(owner != pool)
            def _():
                image.remote(lax.rem(owner + n_pool - pool, n_pool)).start()

            @pl.when(owner == pool)
            def _():
                image.own().start()

    coef.wait_recv()
    for load in loads[8:]:
        load.wait()
    theirs = ritz_ref.at[y, 1 - core]
    for k, block in enumerate((z, before, after, across)):
        ritz(6 + k, own.at[block], theirs.at[block], next_core).wait_recv()
    ritz(10, other, ritz_ref.at[1 - y, 1 - core], next_core).wait_recv()
    image.wait_recv()
    for exchange in backs + [coef, image]:
        exchange.wait_send()
    for copy in sent:
        copy.wait_send()


def spread(wave, count, ritz, n_tg, n_pool):
    vmem = pl.BlockSpec(memory_space=pltpu.VMEM)
    hbm = pl.BlockSpec(memory_space=pltpu.HBM)
    dma = pltpu.SemaphoreType.DMA
    return pl.pallas_call(
        functools.partial(spread_kernel, n_tg, n_pool),
        out_shape=[jax.ShapeDtypeStruct((n_tg, 64, 128), F32), jax.ShapeDtypeStruct((n_pool, 4, 8, 128), F32),
                   jax.ShapeDtypeStruct((64, 128), F32), jax.ShapeDtypeStruct((4, 128, 128), BF16),
                   jax.ShapeDtypeStruct((4,) + ritz.shape, F32)],
        in_specs=[hbm] * 3,
        out_specs=[vmem] * 4 + [hbm],
        scratch_shapes=[pltpu.VMEM(wave.shape, F32), pltpu.SMEM(count.shape, jnp.int32),
                        pltpu.VMEM((768, 256), BF16), pltpu.VMEM((512, 128), F32),
                        pltpu.VMEM((n_tg, 64, 128), F32), dma((n_tg,)), dma((n_tg,)), dma((1,)), dma((3,)),
                        dma((2,)), dma((2,))],
        compiler_params=pltpu.CompilerParams(collective_id=0, has_side_effects=True, vmem_limit_bytes=LIMIT),
        name="spread",
    )(wave, count, ritz)


def collect(stick_pos, re, im, pot, usable, cs, pack, col, n_tg, n_pool):
    vmem = pl.BlockSpec(memory_space=pltpu.VMEM)
    hbm = pl.BlockSpec(memory_space=pltpu.HBM)
    dma = pltpu.SemaphoreType.DMA
    return pl.pallas_call(
        functools.partial(collect_kernel, n_tg, n_pool),
        out_shape=[jax.ShapeDtypeStruct((512, 128), F32), jax.ShapeDtypeStruct(pack.shape, F32),
                   jax.ShapeDtypeStruct(pack.shape, F32), jax.ShapeDtypeStruct((2, 2) + col.shape, F32)],
        in_specs=[hbm] * 8,
        out_specs=[vmem, hbm, hbm, hbm],
        scratch_shapes=[pltpu.SMEM(stick_pos.shape, jnp.int32), pltpu.VMEM(re.shape, F32), pltpu.VMEM(im.shape, F32),
                        pltpu.VMEM(pot.shape, F32), pltpu.VMEM(usable.shape, F32), pltpu.VMEM(cs.shape, BF16),
                        pltpu.VMEM((256, 768), BF16), pltpu.VMEM((256, 768), BF16), pltpu.VMEM((768, 256), BF16),
                        pltpu.VMEM((16384, 128), F32), pltpu.VMEM((2, n_tg, 32, 128), F32),
                        pltpu.VMEM((2, n_tg, 32, 128), F32), pltpu.VMEM(pack.shape, F32),
                        dma((2, n_tg)), dma((2, n_tg)), dma((n_pool,)), dma((n_pool,)), dma((n_pool,)), dma((n_pool,)),
                        dma((4,)), dma((11,)), dma((11,)), dma((11,))],
        compiler_params=pltpu.CompilerParams(collective_id=1, has_side_effects=True, vmem_limit_bytes=LIMIT),
        name="collect",
    )(stick_pos, re, im, pot, usable, cs, pack, col)


def local(wave_coef, potential, stick_pos, stick_count, ritz_block, slab_base):
    n_tg, n_pool = lax.axis_size("tg"), lax.axis_size("pool")
    slots = wave_coef.shape[2]
    planes, pack, usable, cs, col = spread(wave_coef, stick_count, ritz_block, n_tg, n_pool)
    re, im = lattice(planes.reshape(n_tg * slots, 128), stick_pos, cs)
    applied, image, coef, ritz = collect(stick_pos, re, im, potential, usable, cs, pack, col, n_tg, n_pool)
    ritz = ritz.reshape((2 * n_pool,) + ritz_block.shape[1:])
    rotated, applied = rotate(coef, image, ritz, slab_base, applied)
    return applied.reshape(wave_coef.shape), rotated


def solution(mesh):
    in_specs = (
        P(None, "pool", "tg", None),
        P("tg", None, None),
        P(),
        P(),
        P(None, "pool", None),
        P(None, ("tg", "pool"), None),
    )
    out_specs = (P(None, "pool", "tg", None), P(None, ("tg", "pool"), None))
    return jax.shard_map(local, mesh=mesh, in_specs=in_specs, out_specs=out_specs, check_vma=False)
```
